32 devices in a mesh: ty: 8 (over z, x), tx: 4 (over y, core).
Axes of the slice: x: 2, y: 2, z: 4, core: 2. Of those that a mesh axis runs over, the one named last changes fastest.
Arguments:
- fixed_image: float32 [512, 1024], P('ty', 'tx'), may hold values from -6 to 6
- moving_image: float32 [512, 1024], P('ty', 'tx'), may hold values from -6 to 6
- tissue: int32 [16, 32], P('ty', 'tx'), may hold values from 0 to 1, as said below
Outputs:
- coefficients: float32 [2, 16, 32], P(None, 'ty', 'tx')
- mismatch: float32 [512, 1024], P('ty', 'tx')
The draws below stay inside these ranges and needn't reach their ends.
Inputs may be any that keep to these rules, and one draw needn't show every extreme that they name: 1 marks a block of 32 x 32 fine pixels that holds tissue, 0 background.
All inputs are finite; a program needn't handle non-finite values.
Results may differ from the reference program's by a relative error of at most 0.0003.
Values sent between devices are 32-bit elements; how exact they have to be, the bound alone decides.
A program may use at most 64 MiB of HBM per device.

```python
import jax
import jax.numpy as jnp
from jax import lax

SPACE = 32
HALO = 6
MB = 32
ITERS = 2
H = 512
W = 1024
CR = 16
CC = 32
NBY = 16
NBX = 32


def draw_tissue(key, part):
    subkeys = jax.random.split(key, 5)
    row_index = lax.broadcasted_iota(jnp.int32, (NBY, NBX), 0)
    col_index = lax.broadcasted_iota(jnp.int32, (NBY, NBX), 1)
    centre_y = jax.random.randint(subkeys[0], (4,), 0, NBY)
    centre_x = jax.random.randint(subkeys[1], (4,), 0, NBX)
    radius_y = jax.random.randint(subkeys[2], (4,), max(NBY // 8, 1), max(NBY // 3, 2) + 1)
    radius_x = jax.random.randint(subkeys[3], (4,), max(NBX // 8, 1), max(NBX // 3, 2) + 1)
    inside = row_index < 0
    for centre_index in range(4):
        gap_y = row_index - centre_y[centre_index]
        gap_x = col_index - centre_x[centre_index]
        reach_y = radius_y[centre_index] * radius_y[centre_index]
        reach_x = radius_x[centre_index] * radius_x[centre_index]
        inside = inside | (gap_y * gap_y * reach_x + gap_x * gap_x * reach_y <= reach_y * reach_x)
    hole_mask = jax.random.randint(subkeys[4], (NBY, NBX), 0, 12) == 0
    return jnp.where(inside & jnp.logical_not(hole_mask), 1, 0).astype(jnp.int32)


def steps_of(own_key, shape, shards, smallest, largest):
    factor_of = 1.0
    for dim, shards_of in shards:
        heights = jax.random.uniform(jax.random.fold_in(jax.random.fold_in(own_key, 6), dim), (shards_of,), jnp.float32, smallest / len(shards), largest / len(shards))
        factor_of = factor_of * jnp.repeat(jnp.exp(heights), shape[dim] // shards_of).reshape((-1,) + (1,) * (len(shape) - 1 - dim))
    return factor_of


def scatter_about(stream_key, dims, width, reach, cuts=(), held_as=jnp.bfloat16):
    gain = steps_of(stream_key, dims, cuts, -0.22, 0.18) if cuts else 1.0
    array = jax.random.normal(stream_key, dims, jnp.float32) * width * gain
    return jnp.minimum(jnp.maximum(array, -reach), reach).astype(held_as)


def setup_inputs(seed: int = 0) -> dict:
    arg_keys = jax.random.split(jax.random.key(seed), 4)
    return {
        "fixed_image": scatter_about(arg_keys[0], (H, W), 1.0, 6.0, ((0, 8), (1, 4)), jnp.float32),
        "moving_image": scatter_about(arg_keys[1], (H, W), 1.0, 6.0, ((0, 8), (1, 4)), jnp.float32),
        "tissue": draw_tissue(jax.random.fold_in(arg_keys[3], 71), 0),
    }


offset_pairs = ((0, 2), (0, -2), (2, 0), (-2, 0), (2, 2), (2, -2), (-2, 2), (-2, -2), (0, 4), (0, -4), (4, 0), (-4, 0))
highest = lax.Precision.HIGHEST


def bspline(values):
    magnitude = jnp.abs(values)
    near_part = 2.0 / 3.0 - magnitude * magnitude + 0.5 * magnitude ** 3
    far_part = (2.0 - magnitude) ** 3 / 6.0
    return jnp.where(magnitude < 1.0, near_part, jnp.where(magnitude < 2.0, far_part, 0.0 * magnitude))


def box_mean(values):
    height, breadth = values.shape
    total = values[0:height - 2, 0:breadth - 2]
    for shift_y in range(3):
        for shift_x in range(3):
            if shift_y + shift_x > 0:
                total = total + values[shift_y:height - 2 + shift_y, shift_x:breadth - 2 + shift_x]
    return total / 9.0


def descriptors(padded):
    height, breadth = padded.shape
    centre = padded[4:height - 4, 4:breadth - 4]
    distances = []
    for offset_y, offset_x in offset_pairs:
        shifted = padded[4 + offset_y:height - 4 + offset_y, 4 + offset_x:breadth - 4 + offset_x]
        distances.append(box_mean((centre - shifted) ** 2))
    variance = sum(distances) / 12.0 + 0.1
    return [jnp.exp(-member / variance) for member in distances]


def level_terms(fixed_padded, moving_padded, factor):
    fixed_mind = descriptors(fixed_padded)
    moving_mind = descriptors(moving_padded)
    summed = None
    for fixed_part, moving_part in zip(fixed_mind, moving_mind):
        differ = moving_part[1:-1, 1:-1] - fixed_part[1:-1, 1:-1]
        slope_y = (moving_part[2:, 1:-1] - moving_part[:-2, 1:-1]) / (2.0 * factor)
        slope_x = (moving_part[1:-1, 2:] - moving_part[1:-1, :-2]) / (2.0 * factor)
        parts = (differ * slope_y, differ * slope_x, slope_y * slope_y, slope_y * slope_x, slope_x * slope_x, differ * differ)
        summed = parts if summed is None else tuple(left + right for left, right in zip(summed, parts))
    return summed


def spline_matrix(length, factor, cell_count):
    position = factor * jnp.arange(length, dtype=jnp.float32) + (factor - 1) / 2.0
    knots = jnp.arange(cell_count, dtype=jnp.float32)
    return bspline(position[:, None] / SPACE - knots[None, :])


def expand_mask(tissue, factor):
    side = MB // factor
    block_rows, block_cols = tissue.shape
    spread = jnp.broadcast_to(tissue.astype(jnp.float32)[:, None, :, None], (block_rows, side, block_cols, side))
    return spread.reshape(block_rows * side, block_cols * side)


def displace(left, control, right):
    return jnp.stack([jnp.dot(jnp.dot(left, control[member], precision=highest), right.T, precision=highest) for member in range(2)])


def pool_image(image):
    height, breadth = image.shape
    return image.reshape(height // 2, 2, breadth // 2, 2).mean(axis=(1, 3))


def gradient_terms(summed, weight, field):
    return jnp.stack([weight * (summed[0] + summed[2] * field[0] + summed[3] * field[1]),
                      weight * (summed[1] + summed[3] * field[0] + summed[4] * field[1])])


def curvature_density(summed, weight, motion):
    return weight * (motion[0] * (summed[2] * motion[0] + summed[3] * motion[1])
                     + motion[1] * (summed[3] * motion[0] + summed[4] * motion[1]))


def mismatch_of(summed, field):
    return (summed[5] + 2.0 * (summed[0] * field[0] + summed[1] * field[1])
            + field[0] * (summed[2] * field[0] + summed[3] * field[1])
            + field[1] * (summed[3] * field[0] + summed[4] * field[1]))


def reference(fixed_image, moving_image, tissue):
    coefficients = jnp.zeros((2, CR, CC), jnp.float32)
    summed = None
    field = None
    for factor in (2, 1):
        if factor == 2:
            fixed_level = pool_image(fixed_image)
            moving_level = pool_image(moving_image)
        else:
            fixed_level = fixed_image
            moving_level = moving_image
        summed = level_terms(jnp.pad(fixed_level, HALO), jnp.pad(moving_level, HALO), factor)
        rows_matrix = spline_matrix(fixed_level.shape[0], factor, CR)
        cols_matrix = spline_matrix(fixed_level.shape[1], factor, CC)
        weight = expand_mask(tissue, factor)
        field = displace(rows_matrix, coefficients, cols_matrix)
        for iteration in range(ITERS):
            pixel_grad = gradient_terms(summed, weight, field)
            direction = jnp.stack([jnp.dot(jnp.dot(rows_matrix.T, pixel_grad[member], precision=highest), cols_matrix, precision=highest) for member in range(2)])
            motion = displace(rows_matrix, direction, cols_matrix)
            norm_sum = jnp.sum(direction * direction)
            curvature = jnp.sum(curvature_density(summed, weight, motion))
            step_size = norm_sum / curvature
            coefficients = coefficients - step_size * direction
            field = field - step_size * motion
    return coefficients, mismatch_of(summed, field)
```

```python
import functools

import jax
import jax.numpy as jnp
from jax import lax
from jax.experimental import pallas as pl
from jax.experimental.pallas import tpu as pltpu
from jax.sharding import PartitionSpec as P

SPACE = 32
REACH_Y = 5
REACH_X = 11
RIM = 16
SEGMENT = 16
SET = 32
OWN_SLOT = 7
MESH = pl.DeviceIdType.MESH
F32 = jnp.float32

half_offsets = ((0, 2), (2, 0), (2, 2), (2, -2), (0, 4), (4, 0))
travels = ((-1, 0), (1, 0), (0, -1), (0, 1), (-1, -1), (-1, 1), (1, -1), (1, 1))


def bspline(values):
    magnitude = jnp.abs(values)
    near_part = 2.0 / 3.0 - magnitude * magnitude + 0.5 * magnitude * magnitude * magnitude
    rest = 2.0 - magnitude
    far_part = rest * rest * rest / 6.0
    return jnp.where(magnitude < 1.0, near_part, jnp.where(magnitude < 2.0, far_part, 0.0))


def moved(values, by_y, by_x):
    rows, lanes = values.shape
    if by_x:
        values = pltpu.roll(values, (-by_x) % lanes, 1)
    if by_y:
        values = pltpu.roll(values, (-by_y) % rows, 0)
    return values


def minds_into(image, lane_step, out_ref):
    total = None
    for index, (offset_y, offset_x) in enumerate(half_offsets):
        gap = image - moved(image, offset_y, lane_step * offset_x)
        square = gap * gap
        rows = square + moved(square, 1, 0) + moved(square, -1, 0)
        box = rows + moved(rows, 0, lane_step) + moved(rows, 0, -lane_step)
        other = moved(box, -offset_y, -lane_step * offset_x)
        out_ref[2 * index, : image.shape[0]] = box
        out_ref[2 * index + 1, : image.shape[0]] = other
        both = box + other
        total = both if total is None else total + both
    return -1.0 / (total / 12.0 + 0.9)


def terms_into(fixed, moving, lane_step, factor, fixed_ref, moving_ref, terms_ref, wide):
    rows = fixed.shape[0]
    height = rows - 16
    fixed_scale = minds_into(fixed, lane_step, fixed_ref)[8 : 8 + height, :wide]
    moving_scale = minds_into(moving, lane_step, moving_ref)
    sums = None
    for index in range(12):
        fixed_mind = jnp.exp(fixed_ref[index, 8 : 8 + height, :wide] * fixed_scale)
        mind = jnp.exp(moving_ref[index, :rows] * moving_scale)
        differ = mind[8 : 8 + height, :wide] - fixed_mind
        slope_y = moved(mind[:, :wide], 1, 0) - moved(mind[:, :wide], -1, 0)
        slope_y = slope_y[8 : 8 + height]
        own = mind[8 : 8 + height]
        slope_x = (moved(own, 0, lane_step) - moved(own, 0, -lane_step))[:, :wide]
        parts = (
            differ * slope_y,
            differ * slope_x,
            slope_y * slope_y,
            slope_y * slope_x,
            slope_x * slope_x,
            differ * differ,
        )
        sums = parts if sums is None else tuple(a + b for a, b in zip(sums, parts))
    once = 1.0 / (2.0 * factor)
    scales = (once, once, once * once, once * once, once * once, 1.0)
    for index in range(6):
        terms_ref[index] = sums[index] * scales[index]


def kernel(
    count_y,
    count_x,
    tissue_hbm,
    fixed_hbm,
    moving_hbm,
    coef_ref,
    mismatch_ref,
    mid,
    left_side,
    right_side,
    full,
    fixed_minds,
    moving_minds,
    fine_terms,
    coarse_terms,
    fine_weight,
    coarse_weight,
    fine_rows,
    coarse_rows,
    fine_cols,
    coarse_cols,
    tissue_ref,
    tiles_box,
    scalar_box,
    load_sem,
    rim_send,
    rim_recv,
    tile_send,
    tile_recv,
    scalar_send,
    scalar_recv,
):
    ty = lax.axis_index("ty")
    tx = lax.axis_index("tx")
    count = count_y * count_x
    me = ty * count_x + tx
    height, breadth = fixed_hbm.shape
    knots = count_x * (breadth // SPACE)
    cells_y, cells_x = height // SPACE, breadth // SPACE

    def peer(step):
        other = lax.rem(me + step, count)
        return (other // count_x, lax.rem(other, count_x))

    def for_peers(act):
        if count <= 64:
            for step in range(1, count):
                act(peer(step))
        else:

            def body(step, carry):
                act(peer(step))
                return carry

            lax.fori_loop(1, count, body, 0)

    tissue_load = pltpu.make_async_copy(tissue_hbm, tissue_ref, load_sem.at[2])
    tissue_load.start()
    loads = []
    for image, ref in enumerate((fixed_hbm, moving_hbm)):
        loads.append(
            pltpu.make_async_copy(ref, mid.at[image, RIM : RIM + height], load_sem.at[image])
        )
        loads[image].start()

    low, high = slice(0, RIM), slice(RIM + height, 2 * RIM + height)

    @pl.when(ty == 0)
    def _():
        for ref in (mid, left_side, right_side):
            ref[:, low] = jnp.zeros((2, RIM, ref.shape[2]), F32)

    @pl.when(ty == count_y - 1)
    def _():
        for ref in (mid, left_side, right_side):
            ref[:, high] = jnp.zeros((2, RIM, ref.shape[2]), F32)

    @pl.when(tx == 0)
    def _():
        left_side[...] = jnp.zeros(left_side.shape, F32)

    @pl.when(tx == count_x - 1)
    def _():
        right_side[...] = jnp.zeros(right_side.shape, F32)

    tiles_box[...] = jnp.zeros(tiles_box.shape, F32)

    barrier = pltpu.get_barrier_semaphore()
    near = 2 <= count_y <= 8 and 2 <= count_x <= 4
    greeted = [(y, x) for y in range(-1, 2) for x in range(-1, 2) if (y, x) != (0, 0)]
    if count_y == 8:
        greeted += [(1 - count_y, 0), (count_y - 1, 0)]

    def here(by_y, by_x):
        to_y, to_x = ty + by_y, tx + by_x
        return (to_y >= 0) & (to_y < count_y) & (to_x >= 0) & (to_x < count_x)

    def greet(device):
        pl.semaphore_signal(barrier, 1, device_id=device, device_id_type=MESH)

    if near:
        for by_y, by_x in greeted:

            @pl.when(here(by_y, by_x))
            def _():
                greet((ty + by_y, tx + by_x))

    else:
        for_peers(greet)

    lane = lax.broadcasted_iota(jnp.int32, (8, breadth), 1)
    for k in range(REACH_X):
        fine_cols[k] = bspline(lane.astype(F32) / SPACE - (k - 1.0))
        coarse_cols[k] = bspline((lane.astype(F32) + 0.5) / SPACE - (k - 1.0))
    row = lax.broadcasted_iota(jnp.int32, (height, 128), 0).astype(F32)
    coarse_row = lax.broadcasted_iota(jnp.int32, (height // 2, 128), 0).astype(F32)
    for r in range(REACH_Y):
        fine_rows[r] = bspline(row / SPACE - (r - 1.0))
        coarse_rows[r] = bspline((2.0 * coarse_row + 0.5) / SPACE - (r - 1.0))
    even = lax.rem(lane, 2) == 0
    tissue_load.wait()
    for i in range(cells_y):
        line = jnp.zeros((8, breadth), F32)
        for j in range(cells_x):
            value = tissue_ref[i, j].astype(F32)
            inside = (lane >= j * SPACE) & (lane < (j + 1) * SPACE)
            line = jnp.where(inside, value, line)
        half = jnp.where(even, line, 0.0)
        for part in range(SPACE // 8):
            start = i * SPACE + part * 8
            fine_weight[start : start + 8] = line
        for part in range(SPACE // 16):
            start = i * (SPACE // 2) + part * 8
            coarse_weight[start : start + 8] = half

    if near:
        edge_y = jnp.where((ty == 0) | (ty == count_y - 1), 1, 0)
        edge_x = jnp.where((tx == 0) | (tx == count_x - 1), 1, 0)
        greeters = (3 - edge_y) * (3 - edge_x) - 1
        if count_y == 8:
            greeters = greeters + edge_y
        pl.semaphore_wait(barrier, greeters)
    else:
        pl.semaphore_wait(barrier, count - 1)

    def rows_of(travel):
        if travel == 0:
            return slice(0, height), slice(RIM, RIM + height)
        if travel > 0:
            return slice(height - RIM, height), low
        return slice(0, RIM), high

    def landing(travel_y, travel_x):
        ref = mid if travel_x == 0 else (left_side if travel_x > 0 else right_side)
        return ref.at[:, rows_of(travel_y)[1]]

    def exists(travel_y, travel_x):
        to_y, to_x = ty + travel_y, tx + travel_x
        return (to_y >= 0) & (to_y < count_y) & (to_x >= 0) & (to_x < count_x)

    for index, (travel_y, travel_x) in enumerate(travels):

        @pl.when(exists(travel_y, travel_x))
        def _():
            source_rows = rows_of(travel_y)[0]
            if travel_x == 0:
                lanes = slice(0, breadth)
            elif travel_x > 0:
                lanes = slice(breadth - 128, breadth)
            else:
                lanes = slice(0, 128)
            for image, ref in enumerate((fixed_hbm, moving_hbm)):
                pltpu.make_async_remote_copy(
                    src_ref=ref.at[source_rows, lanes],
                    dst_ref=landing(travel_y, travel_x).at[image],
                    send_sem=rim_send.at[index],
                    recv_sem=rim_recv.at[index],
                    device_id=(ty + travel_y, tx + travel_x),
                    device_id_type=MESH,
                ).start()

    for load in loads:
        load.wait()

    for index, (travel_y, travel_x) in enumerate(travels):

        @pl.when(exists(-travel_y, -travel_x))
        def _():
            place = landing(travel_y, travel_x)
            pltpu.make_async_copy(place, place, rim_recv.at[index]).wait()

    tiles = breadth // 128
    side_lane = lax.broadcasted_iota(jnp.int32, (height + 2 * RIM, 128), 1)
    for image in range(2):
        for tile in range(tiles):
            full[image * (tiles + 1) + tile] = mid[image, :, tile * 128 : (tile + 1) * 128]
        full[image * (tiles + 1) + tiles] = jnp.where(
            side_lane < 64, right_side[image], left_side[image]
        )

    def fine_image(image):
        base = image * (tiles + 1)
        return jnp.concatenate(
            [full[base + tile, 8 : height + 24] for tile in range(tiles + 1)], axis=1
        )

    def coarse_image(image):
        base = image * (tiles + 1)
        span = height // 2 + RIM
        summed = jnp.concatenate(
            [
                full[base + tile, pl.ds(0, span, stride=2), :]
                + full[base + tile, pl.ds(1, span, stride=2), :]
                for tile in range(tiles + 1)
            ],
            axis=1,
        )
        return 0.25 * (summed + moved(summed, 0, 1))

    terms_into(
        coarse_image(0), coarse_image(1), 2, 2, fixed_minds, moving_minds, coarse_terms, breadth
    )

    small_lane = lax.broadcasted_iota(jnp.int32, (8, 128), 1)
    small_row = lax.broadcasted_iota(jnp.int32, (8, 128), 0)
    knot = lax.rem(small_lane, SEGMENT)
    knot_x = tx * cells_x - 1 + knot
    knot_y = ty * cells_y - 1 + small_row
    valid = (knot < REACH_X) & (small_row < REACH_Y) & (knot_x >= 0) & (knot_x < knots)
    valid = valid & (knot_y >= 0) & (knot_y < count_y * cells_y)
    own = (small_lane < SET) & (knot >= 1) & (knot <= cells_x)
    own = own & (small_row >= 1) & (small_row <= cells_y)

    def displace(window, rows_ref, cols_ref, number=0):
        fields = []
        for member in range(2):
            line = None
            for k in range(REACH_X):
                at = number * SET + member * SEGMENT + k
                part = window[:, at : at + 1] * cols_ref[k]
                line = part if line is None else line + part
            field = None
            for r in range(REACH_Y):
                weights = jnp.concatenate([rows_ref[r]] * tiles, axis=1)
                part = weights * line[r : r + 1, :]
                field = part if field is None else field + part
            fields.append(field)
        return fields

    def gather_up(pixels, rows_ref, cols_ref, number=0):
        out = jnp.zeros((8, 128), F32)
        for member in range(2):
            lines = []
            for r in range(REACH_Y):
                weights = jnp.concatenate([rows_ref[r]] * tiles, axis=1)
                lines.append(jnp.sum(weights * pixels[member], axis=0, keepdims=True))
            lines.append(jnp.zeros((8 - REACH_Y, breadth), F32))
            line = jnp.concatenate(lines, axis=0)
            for k in range(REACH_X):
                column = jnp.sum(line * cols_ref[k], axis=1, keepdims=True)
                at = number * SET + member * SEGMENT + k
                out = jnp.where(small_lane == at, column, out)
        return out

    def slot_of(by_y, by_x):
        return (by_y + 2) * 3 + by_x + 1

    around = [(y, x) for y in range(-2, 3) for x in range(-1, 2) if (y, x) != (0, 0)]

    def send_tile(turn, tile):
        tiles_box[turn, OWN_SLOT] = tile
        for by_y, by_x in around:

            @pl.when(exists(by_y, by_x))
            def _():
                slot = slot_of(-by_y, -by_x)
                pltpu.make_async_remote_copy(
                    src_ref=tiles_box.at[turn, OWN_SLOT],
                    dst_ref=tiles_box.at[turn, slot],
                    send_sem=tile_send.at[slot],
                    recv_sem=tile_recv.at[turn, slot],
                    device_id=(ty + by_y, tx + by_x),
                    device_id_type=MESH,
                ).start()

    def collect_tiles(turn):
        for by_y, by_x in around:

            @pl.when(exists(by_y, by_x))
            def _():
                slot = slot_of(by_y, by_x)
                place = tiles_box.at[turn, slot]
                pltpu.make_async_copy(place, place, tile_recv.at[turn, slot]).wait()

        window = None
        for by_x in range(-1, 2):
            total = None
            for by_y in range(-2, 3):
                part = tiles_box[turn, slot_of(by_y, by_x)]
                if by_y:
                    part = pltpu.roll(part, (2 * by_y) % 8, 0)
                if by_y == 2:
                    part = jnp.where(small_row >= 4, part, 0.0)
                if by_y == -2:
                    part = jnp.where(small_row < 1, part, 0.0)
                total = part if total is None else total + part
            if by_x:
                total = pltpu.roll(total, (8 * by_x) % 128, 1)
                reached = (knot >= 8) if by_x > 0 else (knot < REACH_X - 8)
                total = jnp.where(reached, total, 0.0)
            window = total if window is None else window + total
        return jnp.where(valid, window, 0.0)

    def send_scalars(turn, row):
        scalar_box[turn, me] = row

        def act(device):
            pltpu.make_async_remote_copy(
                src_ref=scalar_box.at[turn, me],
                dst_ref=scalar_box.at[turn, me],
                send_sem=scalar_send.at[turn],
                recv_sem=scalar_recv.at[turn],
                device_id=device,
                device_id_type=MESH,
            ).start()

        for_peers(act)

    def collect_scalars(turn):
        part = scalar_box.at[turn, 0 : count - 1]
        pltpu.make_async_copy(part, part, scalar_recv.at[turn]).wait()
        row = jnp.sum(scalar_box[turn], axis=0)
        lanes = lax.broadcasted_iota(jnp.int32, (1, 128), 1)
        return [
            jnp.sum(
                jnp.where((lanes >= SET * i) & (lanes < SET * (i + 1)), row, 0.0), keepdims=True
            )
            for i in range(4)
        ]

    def scalars(first, second, dense):
        third = jnp.where(own, second * second, 0.0)
        middle = jnp.where(own, first * second, 0.0)
        lead = jnp.where(own, first * first, 0.0)
        packed = lead + pltpu.roll(middle, SET, 1) + pltpu.roll(third, 2 * SET, 1)
        row = jnp.sum(packed, axis=0, keepdims=True)
        dense = dense + pltpu.roll(dense, 64, 1)
        dense = dense + pltpu.roll(dense, 32, 1)
        lanes = lax.broadcasted_iota(jnp.int32, (1, 128), 1)
        return jnp.where(lanes >= 3 * SET, dense, row)

    def pulled(terms_ref, motion):
        return (
            terms_ref[2] * motion[0] + terms_ref[3] * motion[1],
            terms_ref[3] * motion[0] + terms_ref[4] * motion[1],
        )

    def weighted(weight_ref, pair):
        return [weight_ref[...] * pair[0], weight_ref[...] * pair[1]]

    def density_row(weight_ref, motion, pull):
        dense = weight_ref[...] * (motion[0] * pull[0] + motion[1] * pull[1])
        line = jnp.sum(dense, axis=0, keepdims=True)
        total = line[:, :128]
        for tile in range(1, tiles):
            total = total + line[:, tile * 128 : (tile + 1) * 128]
        return total

    def steps_of(first, middle, third, fourth):
        step = first / middle
        norm = first - 2.0 * step * middle + step * step * third
        curvature = middle - 2.0 * step * third + step * step * fourth
        return step, norm / curvature

    send_tile(
        0,
        gather_up(
            weighted(coarse_weight, (coarse_terms[0], coarse_terms[1])), coarse_rows, coarse_cols
        ),
    )
    terms_into(fine_image(0), fine_image(1), 1, 1, fixed_minds, moving_minds, fine_terms, breadth)
    fine_start = gather_up(
        weighted(fine_weight, (fine_terms[0], fine_terms[1])), fine_rows, fine_cols, 1
    )
    gradient0 = collect_tiles(0)

    motion = displace(gradient0, coarse_rows, coarse_cols)
    part = gather_up(
        weighted(coarse_weight, pulled(coarse_terms, motion)), coarse_rows, coarse_cols
    )
    send_tile(1, part + fine_start)
    fine_motion0 = displace(gradient0, fine_rows, fine_cols)
    fine_part0 = gather_up(
        weighted(fine_weight, pulled(fine_terms, fine_motion0)), fine_rows, fine_cols
    )
    gradient1 = collect_tiles(1)

    motion = displace(gradient1, coarse_rows, coarse_cols)
    dense = density_row(coarse_weight, motion, pulled(coarse_terms, motion))
    send_scalars(0, scalars(gradient0, gradient1, dense))
    fine_motion1 = displace(gradient1, fine_rows, fine_cols)
    fine_part1 = gather_up(
        weighted(fine_weight, pulled(fine_terms, fine_motion1)), fine_rows, fine_cols, 1
    )
    send_tile(2, fine_part0 + fine_part1)
    fine_gradient = pltpu.roll(gradient1, 128 - SET, 1)
    images = collect_tiles(2)
    step0, step1 = steps_of(*collect_scalars(0))
    near, far = -(step0 + step1), step0 * step1
    control = near * gradient0 + far * gradient1
    direction = fine_gradient + near * images + far * pltpu.roll(images, 128 - SET, 1)

    motion2 = displace(direction, fine_rows, fine_cols)
    send_tile(
        3,
        gather_up(weighted(fine_weight, pulled(fine_terms, motion2)), fine_rows, fine_cols),
    )
    field_y = near * fine_motion0[0] + far * fine_motion1[0]
    field_x = near * fine_motion0[1] + far * fine_motion1[1]
    image = collect_tiles(3)

    motion3 = displace(image, fine_rows, fine_cols)
    dense = density_row(fine_weight, motion3, pulled(fine_terms, motion3))
    send_scalars(1, scalars(direction, image, dense))
    step0, step1 = steps_of(*collect_scalars(1))
    near, far = -(step0 + step1), step0 * step1
    control = control + near * direction + far * image
    field_y = field_y + near * motion2[0] + far * motion3[0]
    field_x = field_x + near * motion2[1] + far * motion3[1]
    pull_y, pull_x = pulled(fine_terms, (field_y, field_x))
    mismatch_ref[...] = (
        fine_terms[5]
        + 2.0 * (fine_terms[0] * field_y + fine_terms[1] * field_x)
        + field_y * pull_y
        + field_x * pull_x
    )
    for member in range(2):
        start = member * SEGMENT + 1
        coef_ref[member] = control[1 : 1 + cells_y, start : start + cells_x]

    for index, (travel_y, travel_x) in enumerate(travels):

        @pl.when(exists(travel_y, travel_x))
        def _():
            place = landing(travel_y, travel_x)
            pltpu.make_async_copy(place, place, rim_send.at[index]).wait()

    for by_y, by_x in around:

        @pl.when(exists(by_y, by_x))
        def _():
            slot = slot_of(-by_y, -by_x)
            place = tiles_box.at[:, slot]
            pltpu.make_async_copy(place, place, tile_send.at[slot]).wait()

    for turn in range(2):
        part = scalar_box.at[turn, 0 : count - 1]
        pltpu.make_async_copy(part, part, scalar_send.at[turn]).wait()


def registered(count_y, count_x, tissue, fixed_image, moving_image):
    height, breadth = fixed_image.shape
    cells_y, cells_x = height // SPACE, breadth // SPACE
    count = count_y * count_x
    tall, full_lanes = height + 2 * RIM, breadth + 128
    vmem = pltpu.VMEM
    scratch = [
        vmem((2, tall, breadth), F32),
        vmem((2, tall, 128), F32),
        vmem((2, tall, 128), F32),
        vmem((2 * (breadth // 128 + 1), tall, 128), F32),
        vmem((12, height + 16, full_lanes), F32),
        vmem((12, height + 16, full_lanes), F32),
        vmem((6, height, breadth), F32),
        vmem((6, height // 2, breadth), F32),
        vmem((height, breadth), F32),
        vmem((height // 2, breadth), F32),
        vmem((REACH_Y, height, 128), F32),
        vmem((REACH_Y, height // 2, 128), F32),
        vmem((REACH_X, 8, breadth), F32),
        vmem((REACH_X, 8, breadth), F32),
        pltpu.SMEM((cells_y, cells_x), jnp.int32),
        vmem((4, 15, 8, 128), F32),
        vmem((2, count, 1, 128), F32),
        pltpu.SemaphoreType.DMA((3,)),
        pltpu.SemaphoreType.DMA((8,)),
        pltpu.SemaphoreType.DMA((8,)),
        pltpu.SemaphoreType.DMA((15,)),
        pltpu.SemaphoreType.DMA((4, 15)),
        pltpu.SemaphoreType.DMA((2,)),
        pltpu.SemaphoreType.DMA((2,)),
    ]
    return pl.pallas_call(
        functools.partial(kernel, count_y, count_x),
        out_shape=(
            jax.ShapeDtypeStruct((2, cells_y, cells_x), F32),
            jax.ShapeDtypeStruct((height, breadth), F32),
        ),
        in_specs=[
            pl.BlockSpec(memory_space=pltpu.HBM),
            pl.BlockSpec(memory_space=pltpu.HBM),
            pl.BlockSpec(memory_space=pltpu.HBM),
        ],
        out_specs=(
            pl.BlockSpec(memory_space=pltpu.VMEM),
            pl.BlockSpec(memory_space=pltpu.VMEM),
        ),
        scratch_shapes=scratch,
        compiler_params=pltpu.CompilerParams(
            collective_id=0, has_side_effects=True, vmem_limit_bytes=16 * 1024 * 1024
        ),
    )(tissue, fixed_image, moving_image)


def closing(coef_in, mismatch_in, coef_out, mismatch_out, sem):
    loads = [
        pltpu.make_async_copy(mismatch_in, mismatch_out, sem.at[0]),
        pltpu.make_async_copy(coef_in, coef_out, sem.at[1]),
    ]
    for load in loads:
        load.start()
    for load in loads:
        load.wait()


def shards(count_y, count_x, fixed_image, moving_image, tissue):
    held = [pltpu.with_memory_space_constraint(x, pltpu.HBM) for x in (tissue, fixed_image, moving_image)]
    coef, mismatch = registered(count_y, count_x, *held)
    return pl.pallas_call(
        closing,
        out_shape=(
            jax.ShapeDtypeStruct(coef.shape, F32),
            jax.ShapeDtypeStruct(mismatch.shape, F32),
        ),
        in_specs=[pl.BlockSpec(memory_space=pl.ANY)] * 2,
        out_specs=(pl.BlockSpec(memory_space=pltpu.HBM),) * 2,
        scratch_shapes=[pltpu.SemaphoreType.DMA((2,))],
        compiler_params=pltpu.CompilerParams(vmem_limit_bytes=4 * 1024 * 1024),
    )(coef, mismatch)


def solution(mesh):
    placed = (P("ty", "tx"), P("ty", "tx"), P("ty", "tx"))
    return jax.shard_map(
        functools.partial(shards, mesh.shape["ty"], mesh.shape["tx"]),
        mesh=mesh,
        in_specs=placed,
        out_specs=(P(None, "ty", "tx"), P("ty", "tx")),
        check_vma=False,
    )
```

```python
import functools

import jax
import jax.numpy as jnp
import numpy as np
from jax import lax
from jax.experimental import pallas as pl
from jax.experimental.pallas import tpu as pltpu
from jax.sharding import PartitionSpec as P

SPACE = 32
REACH_Y = 5
REACH_X = 11
RIM = 16
SEGMENT = 16
SET = 32
OWN_SLOT = 7
MESH = pl.DeviceIdType.MESH
F32 = jnp.float32
B16 = jnp.bfloat16
BLOCK = 16
LARGEST = 64

half_offsets = ((0, 2), (2, 0), (2, 2), (2, -2), (0, 4), (4, 0))
travels = ((-1, 0), (1, 0), (0, -1), (0, 1), (-1, -1), (-1, 1), (1, -1), (1, 1))


def bspline(values):
    magnitude = jnp.abs(values)
    near_part = 2.0 / 3.0 - magnitude * magnitude + 0.5 * magnitude * magnitude * magnitude
    rest = 2.0 - magnitude
    far_part = rest * rest * rest / 6.0
    return jnp.where(magnitude < 1.0, near_part, jnp.where(magnitude < 2.0, far_part, 0.0))


def moved(values, by_y, by_x):
    rows, lanes = values.shape
    if by_x:
        values = pltpu.roll(values, (-by_x) % lanes, 1)
    if by_y:
        values = pltpu.roll(values, (-by_y) % rows, 0)
    return values


def minds_into(image, lane_step, out_ref):
    total = None
    for index, (offset_y, offset_x) in enumerate(half_offsets):
        gap = image - moved(image, offset_y, lane_step * offset_x)
        square = gap * gap
        rows = square + moved(square, 1, 0) + moved(square, -1, 0)
        box = rows + moved(rows, 0, lane_step) + moved(rows, 0, -lane_step)
        other = moved(box, -offset_y, -lane_step * offset_x)
        out_ref[2 * index, : image.shape[0]] = box
        out_ref[2 * index + 1, : image.shape[0]] = other
        both = box + other
        total = both if total is None else total + both
    return -1.0 / (total / 12.0 + 0.9)


def terms_into(fixed, moving, lane_step, factor, fixed_ref, moving_ref, terms_ref, wide):
    rows = fixed.shape[0]
    height = rows - 16
    fixed_scale = minds_into(fixed, lane_step, fixed_ref)[8 : 8 + height, :wide]
    moving_scale = minds_into(moving, lane_step, moving_ref)
    sums = None
    for index in range(12):
        fixed_mind = jnp.exp(fixed_ref[index, 8 : 8 + height, :wide] * fixed_scale)
        mind = jnp.exp(moving_ref[index, :rows] * moving_scale)
        differ = mind[8 : 8 + height, :wide] - fixed_mind
        slope_y = moved(mind[:, :wide], 1, 0) - moved(mind[:, :wide], -1, 0)
        slope_y = slope_y[8 : 8 + height]
        own = mind[8 : 8 + height]
        slope_x = (moved(own, 0, lane_step) - moved(own, 0, -lane_step))[:, :wide]
        parts = (
            differ * slope_y,
            differ * slope_x,
            slope_y * slope_y,
            slope_y * slope_x,
            slope_x * slope_x,
            differ * differ,
        )
        sums = parts if sums is None else tuple(a + b for a, b in zip(sums, parts))
    once = 1.0 / (2.0 * factor)
    scales = (once, once, once * once, once * once, once * once, 1.0)
    for index in range(6):
        terms_ref[index] = sums[index] * scales[index]


def spread_kernel(
    count_y,
    count_x,
    tissue_hbm,
    fixed_hbm,
    moving_hbm,
    coef_ref,
    mismatch_ref,
    mid,
    left_side,
    right_side,
    full,
    fixed_minds,
    moving_minds,
    fine_terms,
    coarse_terms,
    fine_weight,
    coarse_weight,
    fine_rows,
    coarse_rows,
    fine_cols,
    coarse_cols,
    tissue_ref,
    tiles_box,
    scalar_box,
    load_sem,
    rim_send,
    rim_recv,
    tile_send,
    tile_recv,
    scalar_send,
    scalar_recv,
):
    ty = lax.axis_index("ty")
    tx = lax.axis_index("tx")
    count = count_y * count_x
    me = ty * count_x + tx
    height, breadth = fixed_hbm.shape
    knots = count_x * (breadth // SPACE)
    cells_y, cells_x = height // SPACE, breadth // SPACE

    def peer(step):
        other = lax.rem(me + step, count)
        return (other // count_x, lax.rem(other, count_x))

    def for_peers(act):
        if count <= 64:
            for step in range(1, count):
                act(peer(step))
        else:

            def body(step, carry):
                act(peer(step))
                return carry

            lax.fori_loop(1, count, body, 0)

    tissue_load = pltpu.make_async_copy(tissue_hbm, tissue_ref, load_sem.at[2])
    tissue_load.start()
    loads = []
    for image, ref in enumerate((fixed_hbm, moving_hbm)):
        loads.append(
            pltpu.make_async_copy(ref, mid.at[image, RIM : RIM + height], load_sem.at[image])
        )
        loads[image].start()

    low, high = slice(0, RIM), slice(RIM + height, 2 * RIM + height)

    @pl.when(ty == 0)
    def _():
        for ref in (mid, left_side, right_side):
            ref[:, low] = jnp.zeros((2, RIM, ref.shape[2]), F32)

    @pl.when(ty == count_y - 1)
    def _():
        for ref in (mid, left_side, right_side):
            ref[:, high] = jnp.zeros((2, RIM, ref.shape[2]), F32)

    @pl.when(tx == 0)
    def _():
        left_side[...] = jnp.zeros(left_side.shape, F32)

    @pl.when(tx == count_x - 1)
    def _():
        right_side[...] = jnp.zeros(right_side.shape, F32)

    tiles_box[...] = jnp.zeros(tiles_box.shape, F32)

    barrier = pltpu.get_barrier_semaphore()
    near = 2 <= count_y <= 8 and 2 <= count_x <= 4
    greeted = [(y, x) for y in range(-1, 2) for x in range(-1, 2) if (y, x) != (0, 0)]
    if count_y == 8:
        greeted += [(1 - count_y, 0), (count_y - 1, 0)]

    def here(by_y, by_x):
        to_y, to_x = ty + by_y, tx + by_x
        return (to_y >= 0) & (to_y < count_y) & (to_x >= 0) & (to_x < count_x)

    def greet(device):
        pl.semaphore_signal(barrier, 1, device_id=device, device_id_type=MESH)

    if near:
        for by_y, by_x in greeted:

            @pl.when(here(by_y, by_x))
            def _():
                greet((ty + by_y, tx + by_x))

    else:
        for_peers(greet)

    lane = lax.broadcasted_iota(jnp.int32, (8, breadth), 1)
    for k in range(REACH_X):
        fine_cols[k] = bspline(lane.astype(F32) / SPACE - (k - 1.0))
        coarse_cols[k] = bspline((lane.astype(F32) + 0.5) / SPACE - (k - 1.0))
    row = lax.broadcasted_iota(jnp.int32, (height, 128), 0).astype(F32)
    coarse_row = lax.broadcasted_iota(jnp.int32, (height // 2, 128), 0).astype(F32)
    for r in range(REACH_Y):
        fine_rows[r] = bspline(row / SPACE - (r - 1.0))
        coarse_rows[r] = bspline((2.0 * coarse_row + 0.5) / SPACE - (r - 1.0))
    even = lax.rem(lane, 2) == 0
    tissue_load.wait()
    for i in range(cells_y):
        line = jnp.zeros((8, breadth), F32)
        for j in range(cells_x):
            value = tissue_ref[i, j].astype(F32)
            inside = (lane >= j * SPACE) & (lane < (j + 1) * SPACE)
            line = jnp.where(inside, value, line)
        half = jnp.where(even, line, 0.0)
        for part in range(SPACE // 8):
            start = i * SPACE + part * 8
            fine_weight[start : start + 8] = line
        for part in range(SPACE // 16):
            start = i * (SPACE // 2) + part * 8
            coarse_weight[start : start + 8] = half

    if near:
        edge_y = jnp.where((ty == 0) | (ty == count_y - 1), 1, 0)
        edge_x = jnp.where((tx == 0) | (tx == count_x - 1), 1, 0)
        greeters = (3 - edge_y) * (3 - edge_x) - 1
        if count_y == 8:
            greeters = greeters + edge_y
        pl.semaphore_wait(barrier, greeters)
    else:
        pl.semaphore_wait(barrier, count - 1)

    def rows_of(travel):
        if travel == 0:
            return slice(0, height), slice(RIM, RIM + height)
        if travel > 0:
            return slice(height - RIM, height), low
        return slice(0, RIM), high

    def landing(travel_y, travel_x):
        ref = mid if travel_x == 0 else (left_side if travel_x > 0 else right_side)
        return ref.at[:, rows_of(travel_y)[1]]

    def exists(travel_y, travel_x):
        to_y, to_x = ty + travel_y, tx + travel_x
        return (to_y >= 0) & (to_y < count_y) & (to_x >= 0) & (to_x < count_x)

    for index, (travel_y, travel_x) in enumerate(travels):

        @pl.when(exists(travel_y, travel_x))
        def _():
            source_rows = rows_of(travel_y)[0]
            if travel_x == 0:
                lanes = slice(0, breadth)
            elif travel_x > 0:
                lanes = slice(breadth - 128, breadth)
            else:
                lanes = slice(0, 128)
            for image, ref in enumerate((fixed_hbm, moving_hbm)):
                pltpu.make_async_remote_copy(
                    src_ref=ref.at[source_rows, lanes],
                    dst_ref=landing(travel_y, travel_x).at[image],
                    send_sem=rim_send.at[index],
                    recv_sem=rim_recv.at[index],
                    device_id=(ty + travel_y, tx + travel_x),
                    device_id_type=MESH,
                ).start()

    for load in loads:
        load.wait()

    for index, (travel_y, travel_x) in enumerate(travels):

        @pl.when(exists(-travel_y, -travel_x))
        def _():
            place = landing(travel_y, travel_x)
            pltpu.make_async_copy(place, place, rim_recv.at[index]).wait()

    tiles = breadth // 128
    side_lane = lax.broadcasted_iota(jnp.int32, (height + 2 * RIM, 128), 1)
    for image in range(2):
        for tile in range(tiles):
            full[image * (tiles + 1) + tile] = mid[image, :, tile * 128 : (tile + 1) * 128]
        full[image * (tiles + 1) + tiles] = jnp.where(
            side_lane < 64, right_side[image], left_side[image]
        )

    def fine_image(image):
        base = image * (tiles + 1)
        return jnp.concatenate(
            [full[base + tile, 8 : height + 24] for tile in range(tiles + 1)], axis=1
        )

    def coarse_image(image):
        base = image * (tiles + 1)
        span = height // 2 + RIM
        summed = jnp.concatenate(
            [
                full[base + tile, pl.ds(0, span, stride=2), :]
                + full[base + tile, pl.ds(1, span, stride=2), :]
                for tile in range(tiles + 1)
            ],
            axis=1,
        )
        return 0.25 * (summed + moved(summed, 0, 1))

    terms_into(
        coarse_image(0), coarse_image(1), 2, 2, fixed_minds, moving_minds, coarse_terms, breadth
    )

    small_lane = lax.broadcasted_iota(jnp.int32, (8, 128), 1)
    small_row = lax.broadcasted_iota(jnp.int32, (8, 128), 0)
    knot = lax.rem(small_lane, SEGMENT)
    knot_x = tx * cells_x - 1 + knot
    knot_y = ty * cells_y - 1 + small_row
    valid = (knot < REACH_X) & (small_row < REACH_Y) & (knot_x >= 0) & (knot_x < knots)
    valid = valid & (knot_y >= 0) & (knot_y < count_y * cells_y)
    own = (small_lane < SET) & (knot >= 1) & (knot <= cells_x)
    own = own & (small_row >= 1) & (small_row <= cells_y)

    def displace(window, rows_ref, cols_ref, number=0):
        fields = []
        for member in range(2):
            line = None
            for k in range(REACH_X):
                at = number * SET + member * SEGMENT + k
                part = window[:, at : at + 1] * cols_ref[k]
                line = part if line is None else line + part
            field = None
            for r in range(REACH_Y):
                weights = jnp.concatenate([rows_ref[r]] * tiles, axis=1)
                part = weights * line[r : r + 1, :]
                field = part if field is None else field + part
            fields.append(field)
        return fields

    def gather_up(pixels, rows_ref, cols_ref, number=0):
        out = jnp.zeros((8, 128), F32)
        for member in range(2):
            lines = []
            for r in range(REACH_Y):
                weights = jnp.concatenate([rows_ref[r]] * tiles, axis=1)
                lines.append(jnp.sum(weights * pixels[member], axis=0, keepdims=True))
            lines.append(jnp.zeros((8 - REACH_Y, breadth), F32))
            line = jnp.concatenate(lines, axis=0)
            for k in range(REACH_X):
                column = jnp.sum(line * cols_ref[k], axis=1, keepdims=True)
                at = number * SET + member * SEGMENT + k
                out = jnp.where(small_lane == at, column, out)
        return out

    def slot_of(by_y, by_x):
        return (by_y + 2) * 3 + by_x + 1

    around = [(y, x) for y in range(-2, 3) for x in range(-1, 2) if (y, x) != (0, 0)]

    def send_tile(turn, tile):
        tiles_box[turn, OWN_SLOT] = tile
        for by_y, by_x in around:

            @pl.when(exists(by_y, by_x))
            def _():
                slot = slot_of(-by_y, -by_x)
                pltpu.make_async_remote_copy(
                    src_ref=tiles_box.at[turn, OWN_SLOT],
                    dst_ref=tiles_box.at[turn, slot],
                    send_sem=tile_send.at[slot],
                    recv_sem=tile_recv.at[turn, slot],
                    device_id=(ty + by_y, tx + by_x),
                    device_id_type=MESH,
                ).start()

    def collect_tiles(turn):
        for by_y, by_x in around:

            @pl.when(exists(by_y, by_x))
            def _():
                slot = slot_of(by_y, by_x)
                place = tiles_box.at[turn, slot]
                pltpu.make_async_copy(place, place, tile_recv.at[turn, slot]).wait()

        window = None
        for by_x in range(-1, 2):
            total = None
            for by_y in range(-2, 3):
                part = tiles_box[turn, slot_of(by_y, by_x)]
                if by_y:
                    part = pltpu.roll(part, (2 * by_y) % 8, 0)
                if by_y == 2:
                    part = jnp.where(small_row >= 4, part, 0.0)
                if by_y == -2:
                    part = jnp.where(small_row < 1, part, 0.0)
                total = part if total is None else total + part
            if by_x:
                total = pltpu.roll(total, (8 * by_x) % 128, 1)
                reached = (knot >= 8) if by_x > 0 else (knot < REACH_X - 8)
                total = jnp.where(reached, total, 0.0)
            window = total if window is None else window + total
        return jnp.where(valid, window, 0.0)

    def send_scalars(turn, row):
        scalar_box[turn, me] = row

        def act(device):
            pltpu.make_async_remote_copy(
                src_ref=scalar_box.at[turn, me],
                dst_ref=scalar_box.at[turn, me],
                send_sem=scalar_send.at[turn],
                recv_sem=scalar_recv.at[turn],
                device_id=device,
                device_id_type=MESH,
            ).start()

        for_peers(act)

    def collect_scalars(turn):
        part = scalar_box.at[turn, 0 : count - 1]
        pltpu.make_async_copy(part, part, scalar_recv.at[turn]).wait()
        row = jnp.sum(scalar_box[turn], axis=0)
        lanes = lax.broadcasted_iota(jnp.int32, (1, 128), 1)
        return [
            jnp.sum(
                jnp.where((lanes >= SET * i) & (lanes < SET * (i + 1)), row, 0.0), keepdims=True
            )
            for i in range(4)
        ]

    def scalars(first, second, dense):
        third = jnp.where(own, second * second, 0.0)
        middle = jnp.where(own, first * second, 0.0)
        lead = jnp.where(own, first * first, 0.0)
        packed = lead + pltpu.roll(middle, SET, 1) + pltpu.roll(third, 2 * SET, 1)
        row = jnp.sum(packed, axis=0, keepdims=True)
        dense = dense + pltpu.roll(dense, 64, 1)
        dense = dense + pltpu.roll(dense, 32, 1)
        lanes = lax.broadcasted_iota(jnp.int32, (1, 128), 1)
        return jnp.where(lanes >= 3 * SET, dense, row)

    def pulled(terms_ref, motion):
        return (
            terms_ref[2] * motion[0] + terms_ref[3] * motion[1],
            terms_ref[3] * motion[0] + terms_ref[4] * motion[1],
        )

    def weighted(weight_ref, pair):
        return [weight_ref[...] * pair[0], weight_ref[...] * pair[1]]

    def density_row(weight_ref, motion, pull):
        dense = weight_ref[...] * (motion[0] * pull[0] + motion[1] * pull[1])
        line = jnp.sum(dense, axis=0, keepdims=True)
        total = line[:, :128]
        for tile in range(1, tiles):
            total = total + line[:, tile * 128 : (tile + 1) * 128]
        return total

    def steps_of(first, middle, third, fourth):
        step = first / middle
        norm = first - 2.0 * step * middle + step * step * third
        curvature = middle - 2.0 * step * third + step * step * fourth
        return step, norm / curvature

    send_tile(
        0,
        gather_up(
            weighted(coarse_weight, (coarse_terms[0], coarse_terms[1])), coarse_rows, coarse_cols
        ),
    )
    terms_into(fine_image(0), fine_image(1), 1, 1, fixed_minds, moving_minds, fine_terms, breadth)
    fine_start = gather_up(
        weighted(fine_weight, (fine_terms[0], fine_terms[1])), fine_rows, fine_cols, 1
    )
    gradient0 = collect_tiles(0)

    motion = displace(gradient0, coarse_rows, coarse_cols)
    part = gather_up(
        weighted(coarse_weight, pulled(coarse_terms, motion)), coarse_rows, coarse_cols
    )
    send_tile(1, part + fine_start)
    fine_motion0 = displace(gradient0, fine_rows, fine_cols)
    fine_part0 = gather_up(
        weighted(fine_weight, pulled(fine_terms, fine_motion0)), fine_rows, fine_cols
    )
    gradient1 = collect_tiles(1)

    motion = displace(gradient1, coarse_rows, coarse_cols)
    dense = density_row(coarse_weight, motion, pulled(coarse_terms, motion))
    send_scalars(0, scalars(gradient0, gradient1, dense))
    fine_motion1 = displace(gradient1, fine_rows, fine_cols)
    fine_part1 = gather_up(
        weighted(fine_weight, pulled(fine_terms, fine_motion1)), fine_rows, fine_cols, 1
    )
    send_tile(2, fine_part0 + fine_part1)
    fine_gradient = pltpu.roll(gradient1, 128 - SET, 1)
    images = collect_tiles(2)
    step0, step1 = steps_of(*collect_scalars(0))
    near, far = -(step0 + step1), step0 * step1
    control = near * gradient0 + far * gradient1
    direction = fine_gradient + near * images + far * pltpu.roll(images, 128 - SET, 1)

    motion2 = displace(direction, fine_rows, fine_cols)
    send_tile(
        3,
        gather_up(weighted(fine_weight, pulled(fine_terms, motion2)), fine_rows, fine_cols),
    )
    field_y = near * fine_motion0[0] + far * fine_motion1[0]
    field_x = near * fine_motion0[1] + far * fine_motion1[1]
    image = collect_tiles(3)

    motion3 = displace(image, fine_rows, fine_cols)
    dense = density_row(fine_weight, motion3, pulled(fine_terms, motion3))
    send_scalars(1, scalars(direction, image, dense))
    step0, step1 = steps_of(*collect_scalars(1))
    near, far = -(step0 + step1), step0 * step1
    control = control + near * direction + far * image
    field_y = field_y + near * motion2[0] + far * motion3[0]
    field_x = field_x + near * motion2[1] + far * motion3[1]
    pull_y, pull_x = pulled(fine_terms, (field_y, field_x))
    mismatch_ref[...] = (
        fine_terms[5]
        + 2.0 * (fine_terms[0] * field_y + fine_terms[1] * field_x)
        + field_y * pull_y
        + field_x * pull_x
    )
    for member in range(2):
        start = member * SEGMENT + 1
        coef_ref[member] = control[1 : 1 + cells_y, start : start + cells_x]

    for index, (travel_y, travel_x) in enumerate(travels):

        @pl.when(exists(travel_y, travel_x))
        def _():
            place = landing(travel_y, travel_x)
            pltpu.make_async_copy(place, place, rim_send.at[index]).wait()

    for by_y, by_x in around:

        @pl.when(exists(by_y, by_x))
        def _():
            slot = slot_of(-by_y, -by_x)
            place = tiles_box.at[:, slot]
            pltpu.make_async_copy(place, place, tile_send.at[slot]).wait()

    for turn in range(2):
        part = scalar_box.at[turn, 0 : count - 1]
        pltpu.make_async_copy(part, part, scalar_send.at[turn]).wait()


def window_pairs(span):
    return [(k, k + d) for d in range(4) for k in range(span - d)]


def split(values):
    high = values.astype(B16)
    return high, (values - high.astype(F32)).astype(B16)


def spline_array(values):
    magnitude = np.abs(values)
    rest = 2.0 - magnitude
    near_part = 2.0 / 3.0 - magnitude**2 + 0.5 * magnitude**3
    far_part = rest**3 / 6.0
    return np.where(magnitude < 1.0, near_part, np.where(magnitude < 2.0, far_part, 0.0))


def split_array(values):
    values = values.astype(np.float32)
    high = values.astype(B16)
    return high, (values - high.astype(np.float32)).astype(B16)


def level_tables(height, breadth, factor):
    row_at = factor * np.arange(height // factor) + (factor - 1) / 2.0
    col_at = np.arange(breadth) + (factor - 1) / 2.0
    rows = spline_array(row_at[None, :] / SPACE - (np.arange(REACH_Y)[:, None] - 1.0))
    cols = spline_array(col_at[:, None] / SPACE - (np.arange(REACH_X)[None, :] - 1.0))
    row_pairs = np.zeros((BLOCK, row_at.size))
    for at, (r, other) in enumerate(window_pairs(REACH_Y)):
        row_pairs[at] = rows[r] * rows[other]
    lines = np.zeros((2, BLOCK, row_at.size))
    for member in range(2):
        lines[member, member * REACH_Y : (member + 1) * REACH_Y] = rows
    pairs = window_pairs(REACH_X)
    col_table = np.zeros((4, breadth, 128))
    for comp in range(3):
        for at, (k, other) in enumerate(pairs):
            col_table[comp, :, comp * len(pairs) + at] = cols[:, k] * cols[:, other]
    col_table[3, :, 3 * len(pairs) : 3 * len(pairs) + REACH_X] = cols

    def left(table):
        high, low = split_array(table)
        return np.concatenate([high, high, low], axis=1)

    high, low = split_array(col_table.reshape(4 * breadth, 128))
    return (
        left(row_pairs),
        np.concatenate([left(lines[0]), left(lines[1])], axis=1),
        np.concatenate([high, low], axis=1),
    )


def assembly_tables(count_y, count_x, cells_y, cells_x):
    knots_y, knots_x = count_y * cells_y, count_x * cells_x
    pairs = window_pairs(REACH_X)
    width = 8 * knots_x
    cols = np.zeros((count_x * 128, 3 * width + 128), np.float32)
    for tx in range(count_x):
        for comp in range(3):
            for at, (k, other) in enumerate(pairs):
                first, second = tx * cells_x - 1 + k, tx * cells_x - 1 + other
                if first < 0 or second >= knots_x:
                    continue
                source, gap = tx * 128 + comp * len(pairs) + at, other - k
                cols[source, comp * width + (3 + gap) * knots_x + first] = 1.0
                cols[source, comp * width + (3 - gap) * knots_x + second] = 1.0
        for k in range(REACH_X):
            knot = tx * cells_x - 1 + k
            if 0 <= knot < knots_x:
                for group in range(128 // knots_x):
                    cols[tx * 128 + 3 * len(pairs) + k, 3 * width + group * knots_x + knot] = 1.0
    rows = np.zeros((9 * knots_y, count_y * BLOCK), np.float32)
    for ty in range(count_y):
        for at, (r, other) in enumerate(window_pairs(REACH_Y)):
            first, second = ty * cells_y - 1 + r, ty * cells_y - 1 + other
            if first < 0 or second >= knots_y:
                continue
            rows[(3 + other - r) * knots_y + first, ty * BLOCK + at] = 1.0
            rows[(3 - other + r) * knots_y + second, ty * BLOCK + at] = 1.0
        for member in range(2):
            for r in range(REACH_Y):
                knot = ty * cells_y - 1 + r
                if 0 <= knot < knots_y:
                    rows[(7 + member) * knots_y + knot, ty * BLOCK + member * REACH_Y + r] = 1.0
    return cols.astype(B16), np.concatenate([rows, rows], axis=1).astype(B16)


def dot(left, right):
    return jnp.dot(left, right, preferred_element_type=F32)


def gathered_kernel(
    count_y,
    count_x,
    tissue_hbm,
    fixed_hbm,
    moving_hbm,
    *rest,
):
    tables_hbm, rest = rest[:8], rest[8:]
    coef_ref, mismatch_ref = rest[:2]
    tables, rest = rest[2:10], rest[10:]
    (
        mid,
        left_side,
        right_side,
        full,
        fixed_minds,
        moving_minds,
        fine_terms,
        coarse_terms,
        fine_weight,
        coarse_weight,
        tissue_ref,
        boxes,
        stencils,
        last_rows,
        last_cols,
        load_sem,
        table_sem,
        rim_send,
        rim_recv,
        block_send,
        block_recv,
        relay_send,
        relay_recv,
    ) = rest
    fine_tables, coarse_tables, (gather_cols, gather_rows) = tables[:3], tables[3:6], tables[6:]
    ty = lax.axis_index("ty")
    tx = lax.axis_index("tx")
    count = count_y * count_x
    half = count // 2
    me = ty * count_x + tx
    parity = lax.rem(tx, 2)
    place = ty * (count_x // 2) + tx // 2
    sibling = (ty, tx + 1 - 2 * parity)
    height, breadth = fixed_hbm.shape
    cells_y, cells_x = height // SPACE, breadth // SPACE
    knots_y, knots_x = count_y * cells_y, count_x * cells_x
    width = 8 * knots_x

    def exists(by_y, by_x):
        to_y, to_x = ty + by_y, tx + by_x
        return (to_y >= 0) & (to_y < count_y) & (to_x >= 0) & (to_x < count_x)

    barrier = pltpu.get_barrier_semaphore()
    for step in range(1, count):
        other = lax.rem(me + step, count)
        pl.semaphore_signal(
            barrier,
            1,
            device_id=(other // count_x, lax.rem(other, count_x)),
            device_id_type=MESH,
        )

    tissue_load = pltpu.make_async_copy(tissue_hbm, tissue_ref, load_sem.at[2])
    tissue_load.start()
    loads = []
    for image, ref in enumerate((fixed_hbm, moving_hbm)):
        loads.append(
            pltpu.make_async_copy(ref, mid.at[image, RIM : RIM + height], load_sem.at[image])
        )
        loads[image].start()
    table_loads = []
    for index, (source, target) in enumerate(zip(tables_hbm, tables)):
        table_loads.append(pltpu.make_async_copy(source, target, table_sem.at[index]))
        table_loads[index].start()

    low, high = slice(0, RIM), slice(RIM + height, 2 * RIM + height)

    @pl.when(ty == 0)
    def _():
        for ref in (mid, left_side, right_side):
            ref[:, low] = jnp.zeros((2, RIM, ref.shape[2]), F32)

    @pl.when(ty == count_y - 1)
    def _():
        for ref in (mid, left_side, right_side):
            ref[:, high] = jnp.zeros((2, RIM, ref.shape[2]), F32)

    @pl.when(tx == 0)
    def _():
        left_side[...] = jnp.zeros(left_side.shape, F32)

    @pl.when(tx == count_x - 1)
    def _():
        right_side[...] = jnp.zeros(right_side.shape, F32)

    lane = lax.broadcasted_iota(jnp.int32, (8, breadth), 1)
    even = lax.rem(lane, 2) == 0
    tissue_load.wait()
    for i in range(cells_y):
        line = jnp.zeros((8, breadth), F32)
        for j in range(cells_x):
            value = tissue_ref[i, j].astype(F32)
            inside = (lane >= j * SPACE) & (lane < (j + 1) * SPACE)
            line = jnp.where(inside, value, line)
        halved = jnp.where(even, line, 0.0)
        for part in range(SPACE // 8):
            start = i * SPACE + part * 8
            fine_weight[start : start + 8] = line
        for part in range(SPACE // 16):
            start = i * (SPACE // 2) + part * 8
            coarse_weight[start : start + 8] = halved

    def rows_of(travel):
        if travel == 0:
            return slice(0, height), slice(RIM, RIM + height)
        if travel > 0:
            return slice(height - RIM, height), low
        return slice(0, RIM), high

    def landing(travel_y, travel_x):
        ref = mid if travel_x == 0 else (left_side if travel_x > 0 else right_side)
        return ref.at[:, rows_of(travel_y)[1]]

    pl.semaphore_wait(barrier, count - 1)

    for index, (travel_y, travel_x) in enumerate(travels):

        @pl.when(exists(travel_y, travel_x))
        def _():
            source_rows = rows_of(travel_y)[0]
            if travel_x == 0:
                lanes = slice(0, breadth)
            elif travel_x > 0:
                lanes = slice(breadth - 128, breadth)
            else:
                lanes = slice(0, 128)
            for image, ref in enumerate((fixed_hbm, moving_hbm)):
                pltpu.make_async_remote_copy(
                    src_ref=ref.at[source_rows, lanes],
                    dst_ref=landing(travel_y, travel_x).at[image],
                    send_sem=rim_send.at[index],
                    recv_sem=rim_recv.at[index],
                    device_id=(ty + travel_y, tx + travel_x),
                    device_id_type=MESH,
                ).start()

    knot = lax.broadcasted_iota(jnp.int32, (128, breadth), 0)
    at_x = lax.broadcasted_iota(jnp.int32, (128, breadth), 1).astype(F32) / SPACE
    last = bspline(at_x - (knot - tx * cells_x).astype(F32))
    last_high, last_low = split(jnp.where(knot < knots_x, last, 0.0))
    last_cols[:, :breadth] = last_high
    last_cols[:, breadth:] = last_low
    knot = lax.broadcasted_iota(jnp.int32, (height, 128), 1)
    at_y = lax.broadcasted_iota(jnp.int32, (height, 128), 0).astype(F32) / SPACE
    third = knot // knots_y
    last_high, last_low = split(
        bspline(at_y - (lax.rem(knot, knots_y) - ty * cells_y).astype(F32))
    )
    kept = jnp.where(third < 2, last_high.astype(F32), last_low.astype(F32))
    last_rows[...] = jnp.where(third < 3, kept, 0.0).astype(B16)

    for load in loads:
        load.wait()

    for index, (travel_y, travel_x) in enumerate(travels):

        @pl.when(exists(-travel_y, -travel_x))
        def _():
            spot = landing(travel_y, travel_x)
            pltpu.make_async_copy(spot, spot, rim_recv.at[index]).wait()

    tiles = breadth // 128
    side_lane = lax.broadcasted_iota(jnp.int32, (height + 2 * RIM, 128), 1)
    for image in range(2):
        for tile in range(tiles):
            full[image * (tiles + 1) + tile] = mid[image, :, tile * 128 : (tile + 1) * 128]
        full[image * (tiles + 1) + tiles] = jnp.where(
            side_lane < 64, right_side[image], left_side[image]
        )

    def fine_image(image):
        base = image * (tiles + 1)
        return jnp.concatenate(
            [full[base + tile, 8 : height + 24] for tile in range(tiles + 1)], axis=1
        )

    def coarse_image(image):
        base = image * (tiles + 1)
        span = height // 2 + RIM
        summed = jnp.concatenate(
            [
                full[base + tile, pl.ds(0, span, stride=2), :]
                + full[base + tile, pl.ds(1, span, stride=2), :]
                for tile in range(tiles + 1)
            ],
            axis=1,
        )
        return 0.25 * (summed + moved(summed, 0, 1))

    def block_of(terms_ref, weight_ref, level):
        row_pairs, row_lines, col_table = level
        weight = weight_ref[...]
        upper, lower = split(
            jnp.concatenate([weight * terms_ref[index] for index in (2, 3, 4)], axis=1)
        )
        pairs = dot(row_pairs[...], jnp.concatenate([upper, lower, upper], axis=0))
        stack = []
        for member in range(2):
            upper, lower = split(weight * terms_ref[member])
            stack += [upper, lower, upper]
        lines = dot(row_lines[...], jnp.concatenate(stack, axis=0))
        upper, lower = split(jnp.concatenate([pairs, lines], axis=1))
        out = dot(jnp.concatenate([upper, lower], axis=0), col_table[...])
        return out[:BLOCK, :128] + out[BLOCK:, :128] + out[:BLOCK, 128:]

    def send_block(level, block):
        boxes[level, parity, place] = block
        for step_y in range(count_y):
            for step_x in range(count_x // 2):
                if step_y + step_x == 0:
                    continue
                to_y = lax.rem(ty + step_y, count_y)
                to_x = 2 * lax.rem(tx // 2 + step_x, count_x // 2) + parity
                pltpu.make_async_remote_copy(
                    src_ref=boxes.at[level, parity, place],
                    dst_ref=boxes.at[level, parity, place],
                    send_sem=block_send.at[level],
                    recv_sem=block_recv.at[level],
                    device_id=(to_y, to_x),
                    device_id_type=MESH,
                ).start()

    def relay_of(level):
        return pltpu.make_async_remote_copy(
            src_ref=boxes.at[level, parity],
            dst_ref=boxes.at[level, parity],
            send_sem=relay_send.at[level],
            recv_sem=relay_recv.at[level],
            device_id=sibling,
            device_id_type=MESH,
        )

    def relay(level):
        part = boxes.at[level, 0, 0 : half - 1]
        pltpu.make_async_copy(part, part, block_recv.at[level]).wait()
        relay_of(level).start()
        spot = boxes.at[level, 1 - parity]
        pltpu.make_async_copy(spot, spot, relay_recv.at[level]).wait()

    def assemble(level):
        columns = []
        for to_x in range(count_x):
            columns.append(
                jnp.concatenate(
                    [
                        boxes[level, to_x % 2, to_y * (count_x // 2) + to_x // 2]
                        for to_y in range(count_y)
                    ],
                    axis=0,
                )
            )
        upper, lower = split(jnp.concatenate(columns, axis=1))
        out = dot(jnp.concatenate([upper, lower], axis=0), gather_cols[...])
        rows = count_y * BLOCK
        upper, lower = split(out[:rows] + out[rows:])
        stencils[level] = dot(gather_rows[...], jnp.concatenate([upper, lower], axis=0))

    group = lax.broadcasted_iota(jnp.int32, (knots_y, 128), 1) // knots_x

    def spread(values):
        halves = []
        for start in (-3, 1):
            out = None
            for index in range(4):
                gap = start + index
                rolled = pltpu.roll(values, (-gap) % 128, 1) if gap else values
                out = rolled if out is None else jnp.where(group >= index, rolled, out)
            halves.append(out)
        return halves

    def start_of(level):
        return [
            stencils[level, (7 + member) * knots_y : (8 + member) * knots_y, 3 * width :]
            for member in range(2)
        ]

    def pull(level, pair):
        spreads = [spread(values) for values in pair]
        sums = [None, None]
        for gap in range(-3, 4):
            at = (gap + 3) * knots_y
            for source in range(2):
                for part in range(2):
                    shifted = spreads[source][part]
                    if gap:
                        shifted = pltpu.roll(shifted, (-gap) % knots_y, 0)
                    for member in range(2):
                        lanes = (member + source) * width + part * 128
                        term = stencils[level, at : at + knots_y, lanes : lanes + 128] * shifted
                        old = sums[member]
                        sums[member] = term if old is None else old + term
        out = []
        for total in sums:
            total = total + pltpu.roll(total, 64, 1)
            out.append(total + pltpu.roll(total, 32, 1))
        return out

    def inner(first, second):
        return jnp.sum(first[0] * second[0] + first[1] * second[1], keepdims=True)

    def descend(level, control, gradient):
        image = pull(level, gradient)
        step = inner(gradient, gradient) / inner(gradient, image)
        control = [c - step * g for c, g in zip(control, gradient)]
        gradient = [g - step * i for g, i in zip(gradient, image)]
        image = pull(level, gradient)
        step = inner(gradient, gradient) / inner(gradient, image)
        return [c - step * g for c, g in zip(control, gradient)]

    for load in table_loads:
        load.wait()
    terms_into(
        coarse_image(0), coarse_image(1), 2, 2, fixed_minds, moving_minds, coarse_terms, breadth
    )
    send_block(0, block_of(coarse_terms, coarse_weight, coarse_tables))
    terms_into(fine_image(0), fine_image(1), 1, 1, fixed_minds, moving_minds, fine_terms, breadth)
    send_block(1, block_of(fine_terms, fine_weight, fine_tables))

    relay(0)
    assemble(0)
    control = [jnp.zeros((knots_y, 128), F32)] * 2
    control = descend(0, control, start_of(0))
    relay(1)
    assemble(1)
    gradient = [b + i for b, i in zip(start_of(1), pull(1, control))]
    control = descend(1, control, gradient)

    upper, lower = split(jnp.concatenate(control, axis=0))
    rows = 2 * knots_y
    out = dot(jnp.concatenate([upper, lower], axis=0), last_cols[...])
    lines = out[:rows, :breadth] + out[rows:, :breadth] + out[:rows, breadth:]
    upper, lower = split(jnp.concatenate([lines[:knots_y], lines[knots_y:]], axis=1))
    blank = jnp.zeros((128 - 3 * knots_y, 2 * breadth), B16)
    field = dot(last_rows[...], jnp.concatenate([upper, lower, upper, blank], axis=0))
    field_y, field_x = field[:, :breadth], field[:, breadth:]
    pull_y = fine_terms[2] * field_y + fine_terms[3] * field_x
    pull_x = fine_terms[3] * field_y + fine_terms[4] * field_x
    mismatch_ref[...] = (
        fine_terms[5]
        + 2.0 * (fine_terms[0] * field_y + fine_terms[1] * field_x)
        + field_y * pull_y
        + field_x * pull_x
    )
    for member in range(2):
        own = pltpu.roll(control[member], lax.rem(128 - cells_x * tx, 128), 1)
        own = pltpu.roll(own, lax.rem(knots_y - cells_y * ty, knots_y), 0)
        coef_ref[member] = own[:cells_y, :cells_x]

    for index, (travel_y, travel_x) in enumerate(travels):

        @pl.when(exists(travel_y, travel_x))
        def _():
            spot = landing(travel_y, travel_x)
            pltpu.make_async_copy(spot, spot, rim_send.at[index]).wait()

    for level in range(2):
        part = boxes.at[level, 0, 0 : half - 1]
        pltpu.make_async_copy(part, part, block_send.at[level]).wait()
        relay_of(level).wait_send()


def spread_call(count_y, count_x, tissue, fixed_image, moving_image):
    height, breadth = fixed_image.shape
    cells_y, cells_x = height // SPACE, breadth // SPACE
    count = count_y * count_x
    tall, full_lanes = height + 2 * RIM, breadth + 128
    vmem = pltpu.VMEM
    scratch = [
        vmem((2, tall, breadth), F32),
        vmem((2, tall, 128), F32),
        vmem((2, tall, 128), F32),
        vmem((2 * (breadth // 128 + 1), tall, 128), F32),
        vmem((12, height + 16, full_lanes), F32),
        vmem((12, height + 16, full_lanes), F32),
        vmem((6, height, breadth), F32),
        vmem((6, height // 2, breadth), F32),
        vmem((height, breadth), F32),
        vmem((height // 2, breadth), F32),
        vmem((REACH_Y, height, 128), F32),
        vmem((REACH_Y, height // 2, 128), F32),
        vmem((REACH_X, 8, breadth), F32),
        vmem((REACH_X, 8, breadth), F32),
        pltpu.SMEM((cells_y, cells_x), jnp.int32),
        vmem((4, 15, 8, 128), F32),
        vmem((2, count, 1, 128), F32),
        pltpu.SemaphoreType.DMA((3,)),
        pltpu.SemaphoreType.DMA((8,)),
        pltpu.SemaphoreType.DMA((8,)),
        pltpu.SemaphoreType.DMA((15,)),
        pltpu.SemaphoreType.DMA((4, 15)),
        pltpu.SemaphoreType.DMA((2,)),
        pltpu.SemaphoreType.DMA((2,)),
    ]
    return pl.pallas_call(
        functools.partial(spread_kernel, count_y, count_x),
        out_shape=(
            jax.ShapeDtypeStruct((2, cells_y, cells_x), F32),
            jax.ShapeDtypeStruct((height, breadth), F32),
        ),
        in_specs=[
            pl.BlockSpec(memory_space=pltpu.HBM),
            pl.BlockSpec(memory_space=pltpu.HBM),
            pl.BlockSpec(memory_space=pltpu.HBM),
        ],
        out_specs=(
            pl.BlockSpec(memory_space=pltpu.VMEM),
            pl.BlockSpec(memory_space=pltpu.VMEM),
        ),
        scratch_shapes=scratch,
        compiler_params=pltpu.CompilerParams(
            collective_id=0, has_side_effects=True, vmem_limit_bytes=16 * 1024 * 1024
        ),
    )(tissue, fixed_image, moving_image)


def closing(coef_in, mismatch_in, coef_out, mismatch_out, sem):
    loads = [
        pltpu.make_async_copy(mismatch_in, mismatch_out, sem.at[0]),
        pltpu.make_async_copy(coef_in, coef_out, sem.at[1]),
    ]
    for load in loads:
        load.start()
    for load in loads:
        load.wait()


def gathered_call(count_y, count_x, tissue, fixed_image, moving_image):
    height, breadth = fixed_image.shape
    cells_y, cells_x = height // SPACE, breadth // SPACE
    count = count_y * count_x
    tall, full_lanes = height + 2 * RIM, breadth + 128
    vmem, dma = pltpu.VMEM, pltpu.SemaphoreType.DMA
    tables = (
        level_tables(height, breadth, 1)
        + level_tables(height, breadth, 2)
        + assembly_tables(count_y, count_x, cells_y, cells_x)
    )
    scratch = [vmem(table.shape, B16) for table in tables] + [
        vmem((2, tall, breadth), F32),
        vmem((2, tall, 128), F32),
        vmem((2, tall, 128), F32),
        vmem((2 * (breadth // 128 + 1), tall, 128), F32),
        vmem((12, height + 16, full_lanes), F32),
        vmem((12, height + 16, full_lanes), F32),
        vmem((6, height, breadth), F32),
        vmem((6, height // 2, breadth), F32),
        vmem((height, breadth), F32),
        vmem((height // 2, breadth), F32),
        pltpu.SMEM((cells_y, cells_x), jnp.int32),
        vmem((2, 2, count // 2, BLOCK, 128), F32),
        vmem((2, tables[7].shape[0], tables[6].shape[1]), F32),
        vmem((height, 128), B16),
        vmem((128, 2 * breadth), B16),
        dma((3,)),
        dma((8,)),
        dma((8,)),
        dma((8,)),
        dma((2,)),
        dma((2,)),
        dma((2,)),
        dma((2,)),
    ]
    held = [
        pltpu.with_memory_space_constraint(jnp.asarray(table), pltpu.HBM) for table in tables
    ]
    return pl.pallas_call(
        functools.partial(gathered_kernel, count_y, count_x),
        out_shape=(
            jax.ShapeDtypeStruct((2, cells_y, cells_x), F32),
            jax.ShapeDtypeStruct((height, breadth), F32),
        ),
        in_specs=[pl.BlockSpec(memory_space=pltpu.HBM)] * 11,
        out_specs=(
            pl.BlockSpec(memory_space=pltpu.VMEM),
            pl.BlockSpec(memory_space=pltpu.VMEM),
        ),
        scratch_shapes=scratch,
        compiler_params=pltpu.CompilerParams(
            collective_id=1, has_side_effects=True, vmem_limit_bytes=32 * 1024 * 1024
        ),
    )(tissue, fixed_image, moving_image, *held)


def shards(count_y, count_x, fixed_image, moving_image, tissue):
    held = [pltpu.with_memory_space_constraint(x, pltpu.HBM) for x in (tissue, fixed_image, moving_image)]
    height, breadth = fixed_image.shape
    fits = height == 2 * SPACE and breadth == 8 * SPACE and count_x % 2 == 0
    fits = fits and count_x * (breadth // SPACE) == 32 and count_y * count_x <= LARGEST
    call = gathered_call if fits else spread_call
    coef, mismatch = call(count_y, count_x, *held)
    return pl.pallas_call(
        closing,
        out_shape=(
            jax.ShapeDtypeStruct(coef.shape, F32),
            jax.ShapeDtypeStruct(mismatch.shape, F32),
        ),
        in_specs=[pl.BlockSpec(memory_space=pl.ANY)] * 2,
        out_specs=(pl.BlockSpec(memory_space=pltpu.HBM),) * 2,
        scratch_shapes=[pltpu.SemaphoreType.DMA((2,))],
        compiler_params=pltpu.CompilerParams(vmem_limit_bytes=4 * 1024 * 1024),
    )(coef, mismatch)


def solution(mesh):
    placed = (P("ty", "tx"), P("ty", "tx"), P("ty", "tx"))
    return jax.shard_map(
        functools.partial(shards, mesh.shape["ty"], mesh.shape["tx"]),
        mesh=mesh,
        in_specs=placed,
        out_specs=(P(None, "ty", "tx"), P("ty", "tx")),
        check_vma=False,
    )
```

```python
import functools

import jax
import jax.numpy as jnp
import numpy as np
from jax import lax
from jax.experimental import pallas as pl
from jax.experimental.pallas import tpu as pltpu
from jax.sharding import PartitionSpec as P

SPACE = 32
REACH_Y = 5
REACH_X = 11
RIM = 16
SEGMENT = 16
SET = 32
OWN_SLOT = 7
MESH = pl.DeviceIdType.MESH
F32 = jnp.float32
B16 = jnp.bfloat16
BLOCK = 16
LARGEST = 64

half_offsets = ((0, 2), (2, 0), (2, 2), (2, -2), (0, 4), (4, 0))
far_greets = (2, -2, 4)
travels = ((-1, 0), (1, 0), (0, -1), (0, 1), (-1, -1), (-1, 1), (1, -1), (1, 1))


def bspline(values):
    magnitude = jnp.abs(values)
    near_part = 2.0 / 3.0 - magnitude * magnitude + 0.5 * magnitude * magnitude * magnitude
    rest = 2.0 - magnitude
    far_part = rest * rest * rest / 6.0
    return jnp.where(magnitude < 1.0, near_part, jnp.where(magnitude < 2.0, far_part, 0.0))


def moved(values, by_y, by_x):
    rows, lanes = values.shape
    if by_x:
        values = pltpu.roll(values, (-by_x) % lanes, 1)
    if by_y:
        values = pltpu.roll(values, (-by_y) % rows, 0)
    return values


def minds_into(image, lane_step, out_ref):
    total = None
    for index, (offset_y, offset_x) in enumerate(half_offsets):
        gap = image - moved(image, offset_y, lane_step * offset_x)
        square = gap * gap
        rows = square + moved(square, 1, 0) + moved(square, -1, 0)
        box = rows + moved(rows, 0, lane_step) + moved(rows, 0, -lane_step)
        other = moved(box, -offset_y, -lane_step * offset_x)
        out_ref[2 * index, : image.shape[0]] = box
        out_ref[2 * index + 1, : image.shape[0]] = other
        both = box + other
        total = both if total is None else total + both
    return -1.0 / (total / 12.0 + 0.9)


def terms_into(fixed, moving, lane_step, factor, fixed_ref, moving_ref, terms_ref, wide):
    rows = fixed.shape[0]
    height = rows - 16
    fixed_scale = minds_into(fixed, lane_step, fixed_ref)[8 : 8 + height, :wide]
    moving_scale = minds_into(moving, lane_step, moving_ref)
    sums = None
    for index in range(12):
        fixed_mind = jnp.exp(fixed_ref[index, 8 : 8 + height, :wide] * fixed_scale)
        mind = jnp.exp(moving_ref[index, :rows] * moving_scale)
        differ = mind[8 : 8 + height, :wide] - fixed_mind
        slope_y = moved(mind[:, :wide], 1, 0) - moved(mind[:, :wide], -1, 0)
        slope_y = slope_y[8 : 8 + height]
        own = mind[8 : 8 + height]
        slope_x = (moved(own, 0, lane_step) - moved(own, 0, -lane_step))[:, :wide]
        parts = (
            differ * slope_y,
            differ * slope_x,
            slope_y * slope_y,
            slope_y * slope_x,
            slope_x * slope_x,
            differ * differ,
        )
        sums = parts if sums is None else tuple(a + b for a, b in zip(sums, parts))
    once = 1.0 / (2.0 * factor)
    scales = (once, once, once * once, once * once, once * once, 1.0)
    for index in range(6):
        terms_ref[index] = sums[index] * scales[index]


def spread_kernel(
    count_y,
    count_x,
    tissue_hbm,
    fixed_hbm,
    moving_hbm,
    coef_ref,
    mismatch_ref,
    mid,
    left_side,
    right_side,
    full,
    fixed_minds,
    moving_minds,
    fine_terms,
    coarse_terms,
    fine_weight,
    coarse_weight,
    fine_rows,
    coarse_rows,
    fine_cols,
    coarse_cols,
    tissue_ref,
    tiles_box,
    scalar_box,
    load_sem,
    rim_send,
    rim_recv,
    tile_send,
    tile_recv,
    scalar_send,
    scalar_recv,
):
    ty = lax.axis_index("ty")
    tx = lax.axis_index("tx")
    count = count_y * count_x
    me = ty * count_x + tx
    height, breadth = fixed_hbm.shape
    knots = count_x * (breadth // SPACE)
    cells_y, cells_x = height // SPACE, breadth // SPACE

    def peer(step):
        other = lax.rem(me + step, count)
        return (other // count_x, lax.rem(other, count_x))

    def for_peers(act):
        if count <= 64:
            for step in range(1, count):
                act(peer(step))
        else:

            def body(step, carry):
                act(peer(step))
                return carry

            lax.fori_loop(1, count, body, 0)

    tissue_load = pltpu.make_async_copy(tissue_hbm, tissue_ref, load_sem.at[2])
    tissue_load.start()
    loads = []
    for image, ref in enumerate((fixed_hbm, moving_hbm)):
        loads.append(
            pltpu.make_async_copy(ref, mid.at[image, RIM : RIM + height], load_sem.at[image])
        )
        loads[image].start()

    low, high = slice(0, RIM), slice(RIM + height, 2 * RIM + height)

    @pl.when(ty == 0)
    def _():
        for ref in (mid, left_side, right_side):
            ref[:, low] = jnp.zeros((2, RIM, ref.shape[2]), F32)

    @pl.when(ty == count_y - 1)
    def _():
        for ref in (mid, left_side, right_side):
            ref[:, high] = jnp.zeros((2, RIM, ref.shape[2]), F32)

    @pl.when(tx == 0)
    def _():
        left_side[...] = jnp.zeros(left_side.shape, F32)

    @pl.when(tx == count_x - 1)
    def _():
        right_side[...] = jnp.zeros(right_side.shape, F32)

    tiles_box[...] = jnp.zeros(tiles_box.shape, F32)

    barrier = pltpu.get_barrier_semaphore()
    near = 2 <= count_y <= 8 and 2 <= count_x <= 4
    greeted = [(y, x) for y in range(-1, 2) for x in range(-1, 2) if (y, x) != (0, 0)]
    if count_y == 8:
        greeted += [(1 - count_y, 0), (count_y - 1, 0)]

    def here(by_y, by_x):
        to_y, to_x = ty + by_y, tx + by_x
        return (to_y >= 0) & (to_y < count_y) & (to_x >= 0) & (to_x < count_x)

    def greet(device):
        pl.semaphore_signal(barrier, 1, device_id=device, device_id_type=MESH)

    if near:
        for by_y, by_x in greeted:

            @pl.when(here(by_y, by_x))
            def _():
                greet((ty + by_y, tx + by_x))

    else:
        for_peers(greet)

    lane = lax.broadcasted_iota(jnp.int32, (8, breadth), 1)
    for k in range(REACH_X):
        fine_cols[k] = bspline(lane.astype(F32) / SPACE - (k - 1.0))
        coarse_cols[k] = bspline((lane.astype(F32) + 0.5) / SPACE - (k - 1.0))
    row = lax.broadcasted_iota(jnp.int32, (height, 128), 0).astype(F32)
    coarse_row = lax.broadcasted_iota(jnp.int32, (height // 2, 128), 0).astype(F32)
    for r in range(REACH_Y):
        fine_rows[r] = bspline(row / SPACE - (r - 1.0))
        coarse_rows[r] = bspline((2.0 * coarse_row + 0.5) / SPACE - (r - 1.0))
    even = lax.rem(lane, 2) == 0
    tissue_load.wait()
    for i in range(cells_y):
        line = jnp.zeros((8, breadth), F32)
        for j in range(cells_x):
            value = tissue_ref[i, j].astype(F32)
            inside = (lane >= j * SPACE) & (lane < (j + 1) * SPACE)
            line = jnp.where(inside, value, line)
        half = jnp.where(even, line, 0.0)
        for part in range(SPACE // 8):
            start = i * SPACE + part * 8
            fine_weight[start : start + 8] = line
        for part in range(SPACE // 16):
            start = i * (SPACE // 2) + part * 8
            coarse_weight[start : start + 8] = half

    if near:
        edge_y = jnp.where((ty == 0) | (ty == count_y - 1), 1, 0)
        edge_x = jnp.where((tx == 0) | (tx == count_x - 1), 1, 0)
        greeters = (3 - edge_y) * (3 - edge_x) - 1
        if count_y == 8:
            greeters = greeters + edge_y
        pl.semaphore_wait(barrier, greeters)
    else:
        pl.semaphore_wait(barrier, count - 1)

    def rows_of(travel):
        if travel == 0:
            return slice(0, height), slice(RIM, RIM + height)
        if travel > 0:
            return slice(height - RIM, height), low
        return slice(0, RIM), high

    def landing(travel_y, travel_x):
        ref = mid if travel_x == 0 else (left_side if travel_x > 0 else right_side)
        return ref.at[:, rows_of(travel_y)[1]]

    def exists(travel_y, travel_x):
        to_y, to_x = ty + travel_y, tx + travel_x
        return (to_y >= 0) & (to_y < count_y) & (to_x >= 0) & (to_x < count_x)

    for index, (travel_y, travel_x) in enumerate(travels):

        @pl.when(exists(travel_y, travel_x))
        def _():
            source_rows = rows_of(travel_y)[0]
            if travel_x == 0:
                lanes = slice(0, breadth)
            elif travel_x > 0:
                lanes = slice(breadth - 128, breadth)
            else:
                lanes = slice(0, 128)
            for image, ref in enumerate((fixed_hbm, moving_hbm)):
                pltpu.make_async_remote_copy(
                    src_ref=ref.at[source_rows, lanes],
                    dst_ref=landing(travel_y, travel_x).at[image],
                    send_sem=rim_send.at[index],
                    recv_sem=rim_recv.at[index],
                    device_id=(ty + travel_y, tx + travel_x),
                    device_id_type=MESH,
                ).start()

    for load in loads:
        load.wait()

    for index, (travel_y, travel_x) in enumerate(travels):

        @pl.when(exists(-travel_y, -travel_x))
        def _():
            place = landing(travel_y, travel_x)
            pltpu.make_async_copy(place, place, rim_recv.at[index]).wait()

    tiles = breadth // 128
    side_lane = lax.broadcasted_iota(jnp.int32, (height + 2 * RIM, 128), 1)
    for image in range(2):
        for tile in range(tiles):
            full[image * (tiles + 1) + tile] = mid[image, :, tile * 128 : (tile + 1) * 128]
        full[image * (tiles + 1) + tiles] = jnp.where(
            side_lane < 64, right_side[image], left_side[image]
        )

    def fine_image(image):
        base = image * (tiles + 1)
        return jnp.concatenate(
            [full[base + tile, 8 : height + 24] for tile in range(tiles + 1)], axis=1
        )

    def coarse_image(image):
        base = image * (tiles + 1)
        span = height // 2 + RIM
        summed = jnp.concatenate(
            [
                full[base + tile, pl.ds(0, span, stride=2), :]
                + full[base + tile, pl.ds(1, span, stride=2), :]
                for tile in range(tiles + 1)
            ],
            axis=1,
        )
        return 0.25 * (summed + moved(summed, 0, 1))

    terms_into(
        coarse_image(0), coarse_image(1), 2, 2, fixed_minds, moving_minds, coarse_terms, breadth
    )

    small_lane = lax.broadcasted_iota(jnp.int32, (8, 128), 1)
    small_row = lax.broadcasted_iota(jnp.int32, (8, 128), 0)
    knot = lax.rem(small_lane, SEGMENT)
    knot_x = tx * cells_x - 1 + knot
    knot_y = ty * cells_y - 1 + small_row
    valid = (knot < REACH_X) & (small_row < REACH_Y) & (knot_x >= 0) & (knot_x < knots)
    valid = valid & (knot_y >= 0) & (knot_y < count_y * cells_y)
    own = (small_lane < SET) & (knot >= 1) & (knot <= cells_x)
    own = own & (small_row >= 1) & (small_row <= cells_y)

    def displace(window, rows_ref, cols_ref, number=0):
        fields = []
        for member in range(2):
            line = None
            for k in range(REACH_X):
                at = number * SET + member * SEGMENT + k
                part = window[:, at : at + 1] * cols_ref[k]
                line = part if line is None else line + part
            field = None
            for r in range(REACH_Y):
                weights = jnp.concatenate([rows_ref[r]] * tiles, axis=1)
                part = weights * line[r : r + 1, :]
                field = part if field is None else field + part
            fields.append(field)
        return fields

    def gather_up(pixels, rows_ref, cols_ref, number=0):
        out = jnp.zeros((8, 128), F32)
        for member in range(2):
            lines = []
            for r in range(REACH_Y):
                weights = jnp.concatenate([rows_ref[r]] * tiles, axis=1)
                lines.append(jnp.sum(weights * pixels[member], axis=0, keepdims=True))
            lines.append(jnp.zeros((8 - REACH_Y, breadth), F32))
            line = jnp.concatenate(lines, axis=0)
            for k in range(REACH_X):
                column = jnp.sum(line * cols_ref[k], axis=1, keepdims=True)
                at = number * SET + member * SEGMENT + k
                out = jnp.where(small_lane == at, column, out)
        return out

    def slot_of(by_y, by_x):
        return (by_y + 2) * 3 + by_x + 1

    around = [(y, x) for y in range(-2, 3) for x in range(-1, 2) if (y, x) != (0, 0)]

    def send_tile(turn, tile):
        tiles_box[turn, OWN_SLOT] = tile
        for by_y, by_x in around:

            @pl.when(exists(by_y, by_x))
            def _():
                slot = slot_of(-by_y, -by_x)
                pltpu.make_async_remote_copy(
                    src_ref=tiles_box.at[turn, OWN_SLOT],
                    dst_ref=tiles_box.at[turn, slot],
                    send_sem=tile_send.at[slot],
                    recv_sem=tile_recv.at[turn, slot],
                    device_id=(ty + by_y, tx + by_x),
                    device_id_type=MESH,
                ).start()

    def collect_tiles(turn):
        for by_y, by_x in around:

            @pl.when(exists(by_y, by_x))
            def _():
                slot = slot_of(by_y, by_x)
                place = tiles_box.at[turn, slot]
                pltpu.make_async_copy(place, place, tile_recv.at[turn, slot]).wait()

        window = None
        for by_x in range(-1, 2):
            total = None
            for by_y in range(-2, 3):
                part = tiles_box[turn, slot_of(by_y, by_x)]
                if by_y:
                    part = pltpu.roll(part, (2 * by_y) % 8, 0)
                if by_y == 2:
                    part = jnp.where(small_row >= 4, part, 0.0)
                if by_y == -2:
                    part = jnp.where(small_row < 1, part, 0.0)
                total = part if total is None else total + part
            if by_x:
                total = pltpu.roll(total, (8 * by_x) % 128, 1)
                reached = (knot >= 8) if by_x > 0 else (knot < REACH_X - 8)
                total = jnp.where(reached, total, 0.0)
            window = total if window is None else window + total
        return jnp.where(valid, window, 0.0)

    def send_scalars(turn, row):
        scalar_box[turn, me] = row

        def act(device):
            pltpu.make_async_remote_copy(
                src_ref=scalar_box.at[turn, me],
                dst_ref=scalar_box.at[turn, me],
                send_sem=scalar_send.at[turn],
                recv_sem=scalar_recv.at[turn],
                device_id=device,
                device_id_type=MESH,
            ).start()

        for_peers(act)

    def collect_scalars(turn):
        part = scalar_box.at[turn, 0 : count - 1]
        pltpu.make_async_copy(part, part, scalar_recv.at[turn]).wait()
        row = jnp.sum(scalar_box[turn], axis=0)
        lanes = lax.broadcasted_iota(jnp.int32, (1, 128), 1)
        return [
            jnp.sum(
                jnp.where((lanes >= SET * i) & (lanes < SET * (i + 1)), row, 0.0), keepdims=True
            )
            for i in range(4)
        ]

    def scalars(first, second, dense):
        third = jnp.where(own, second * second, 0.0)
        middle = jnp.where(own, first * second, 0.0)
        lead = jnp.where(own, first * first, 0.0)
        packed = lead + pltpu.roll(middle, SET, 1) + pltpu.roll(third, 2 * SET, 1)
        row = jnp.sum(packed, axis=0, keepdims=True)
        dense = dense + pltpu.roll(dense, 64, 1)
        dense = dense + pltpu.roll(dense, 32, 1)
        lanes = lax.broadcasted_iota(jnp.int32, (1, 128), 1)
        return jnp.where(lanes >= 3 * SET, dense, row)

    def pulled(terms_ref, motion):
        return (
            terms_ref[2] * motion[0] + terms_ref[3] * motion[1],
            terms_ref[3] * motion[0] + terms_ref[4] * motion[1],
        )

    def weighted(weight_ref, pair):
        return [weight_ref[...] * pair[0], weight_ref[...] * pair[1]]

    def density_row(weight_ref, motion, pull):
        dense = weight_ref[...] * (motion[0] * pull[0] + motion[1] * pull[1])
        line = jnp.sum(dense, axis=0, keepdims=True)
        total = line[:, :128]
        for tile in range(1, tiles):
            total = total + line[:, tile * 128 : (tile + 1) * 128]
        return total

    def steps_of(first, middle, third, fourth):
        step = first / middle
        norm = first - 2.0 * step * middle + step * step * third
        curvature = middle - 2.0 * step * third + step * step * fourth
        return step, norm / curvature

    send_tile(
        0,
        gather_up(
            weighted(coarse_weight, (coarse_terms[0], coarse_terms[1])), coarse_rows, coarse_cols
        ),
    )
    terms_into(fine_image(0), fine_image(1), 1, 1, fixed_minds, moving_minds, fine_terms, breadth)
    fine_start = gather_up(
        weighted(fine_weight, (fine_terms[0], fine_terms[1])), fine_rows, fine_cols, 1
    )
    gradient0 = collect_tiles(0)

    motion = displace(gradient0, coarse_rows, coarse_cols)
    part = gather_up(
        weighted(coarse_weight, pulled(coarse_terms, motion)), coarse_rows, coarse_cols
    )
    send_tile(1, part + fine_start)
    fine_motion0 = displace(gradient0, fine_rows, fine_cols)
    fine_part0 = gather_up(
        weighted(fine_weight, pulled(fine_terms, fine_motion0)), fine_rows, fine_cols
    )
    gradient1 = collect_tiles(1)

    motion = displace(gradient1, coarse_rows, coarse_cols)
    dense = density_row(coarse_weight, motion, pulled(coarse_terms, motion))
    send_scalars(0, scalars(gradient0, gradient1, dense))
    fine_motion1 = displace(gradient1, fine_rows, fine_cols)
    fine_part1 = gather_up(
        weighted(fine_weight, pulled(fine_terms, fine_motion1)), fine_rows, fine_cols, 1
    )
    send_tile(2, fine_part0 + fine_part1)
    fine_gradient = pltpu.roll(gradient1, 128 - SET, 1)
    images = collect_tiles(2)
    step0, step1 = steps_of(*collect_scalars(0))
    near, far = -(step0 + step1), step0 * step1
    control = near * gradient0 + far * gradient1
    direction = fine_gradient + near * images + far * pltpu.roll(images, 128 - SET, 1)

    motion2 = displace(direction, fine_rows, fine_cols)
    send_tile(
        3,
        gather_up(weighted(fine_weight, pulled(fine_terms, motion2)), fine_rows, fine_cols),
    )
    field_y = near * fine_motion0[0] + far * fine_motion1[0]
    field_x = near * fine_motion0[1] + far * fine_motion1[1]
    image = collect_tiles(3)

    motion3 = displace(image, fine_rows, fine_cols)
    dense = density_row(fine_weight, motion3, pulled(fine_terms, motion3))
    send_scalars(1, scalars(direction, image, dense))
    step0, step1 = steps_of(*collect_scalars(1))
    near, far = -(step0 + step1), step0 * step1
    control = control + near * direction + far * image
    field_y = field_y + near * motion2[0] + far * motion3[0]
    field_x = field_x + near * motion2[1] + far * motion3[1]
    pull_y, pull_x = pulled(fine_terms, (field_y, field_x))
    mismatch_ref[...] = (
        fine_terms[5]
        + 2.0 * (fine_terms[0] * field_y + fine_terms[1] * field_x)
        + field_y * pull_y
        + field_x * pull_x
    )
    for member in range(2):
        start = member * SEGMENT + 1
        coef_ref[member] = control[1 : 1 + cells_y, start : start + cells_x]

    for index, (travel_y, travel_x) in enumerate(travels):

        @pl.when(exists(travel_y, travel_x))
        def _():
            place = landing(travel_y, travel_x)
            pltpu.make_async_copy(place, place, rim_send.at[index]).wait()

    for by_y, by_x in around:

        @pl.when(exists(by_y, by_x))
        def _():
            slot = slot_of(-by_y, -by_x)
            place = tiles_box.at[:, slot]
            pltpu.make_async_copy(place, place, tile_send.at[slot]).wait()

    for turn in range(2):
        part = scalar_box.at[turn, 0 : count - 1]
        pltpu.make_async_copy(part, part, scalar_send.at[turn]).wait()


def window_pairs(span):
    return [(k, k + d) for d in range(4) for k in range(span - d)]


def split(values):
    high = values.astype(B16)
    return high, (values - high.astype(F32)).astype(B16)


def spline_array(values):
    magnitude = np.abs(values)
    rest = 2.0 - magnitude
    near_part = 2.0 / 3.0 - magnitude**2 + 0.5 * magnitude**3
    far_part = rest**3 / 6.0
    return np.where(magnitude < 1.0, near_part, np.where(magnitude < 2.0, far_part, 0.0))


def split_array(values):
    values = values.astype(np.float32)
    high = values.astype(B16)
    return high, (values - high.astype(np.float32)).astype(B16)


def level_tables(height, breadth, factor):
    row_at = factor * np.arange(height // factor) + (factor - 1) / 2.0
    col_at = np.arange(breadth) - (factor - 1) / 2.0
    rows = spline_array(row_at[None, :] / SPACE - (np.arange(REACH_Y)[:, None] - 1.0))
    cols = spline_array(col_at[:, None] / SPACE - (np.arange(REACH_X)[None, :] - 1.0))
    row_pairs = np.zeros((BLOCK, row_at.size))
    for at, (r, other) in enumerate(window_pairs(REACH_Y)):
        row_pairs[at] = rows[r] * rows[other]
    lines = np.zeros((2, BLOCK, row_at.size))
    for member in range(2):
        lines[member, member * REACH_Y : (member + 1) * REACH_Y] = rows
    pairs = window_pairs(REACH_X)
    col_table = np.zeros((4, breadth, 128))
    for comp in range(3):
        for at, (k, other) in enumerate(pairs):
            col_table[comp, :, comp * len(pairs) + at] = cols[:, k] * cols[:, other]
    col_table[3, :, 3 * len(pairs) : 3 * len(pairs) + REACH_X] = cols

    def left(table):
        high, low = split_array(table)
        return np.concatenate([high, high, low], axis=1)

    high, low = split_array(col_table.reshape(4 * breadth, 128))
    return (
        left(row_pairs),
        np.concatenate([left(lines[0]), left(lines[1])], axis=1),
        np.concatenate([high, low], axis=1),
    )


def assembly_tables(count_y, count_x, cells_y, cells_x):
    knots_y, knots_x = count_y * cells_y, count_x * cells_x
    pairs = window_pairs(REACH_X)
    width = 8 * knots_x
    cols = np.zeros((count_x * 128, 3 * width + 128), np.float32)
    for tx in range(count_x):
        for comp in range(3):
            for at, (k, other) in enumerate(pairs):
                first, second = tx * cells_x - 1 + k, tx * cells_x - 1 + other
                if first < 0 or second >= knots_x:
                    continue
                source, gap = tx * 128 + comp * len(pairs) + at, other - k
                cols[source, comp * width + (3 + gap) * knots_x + first] = 1.0
                cols[source, comp * width + (3 - gap) * knots_x + second] = 1.0
        for k in range(REACH_X):
            knot = tx * cells_x - 1 + k
            if 0 <= knot < knots_x:
                for group in range(128 // knots_x):
                    cols[tx * 128 + 3 * len(pairs) + k, 3 * width + group * knots_x + knot] = 1.0
    rows = np.zeros((9 * knots_y, count_y * BLOCK), np.float32)
    for ty in range(count_y):
        for at, (r, other) in enumerate(window_pairs(REACH_Y)):
            first, second = ty * cells_y - 1 + r, ty * cells_y - 1 + other
            if first < 0 or second >= knots_y:
                continue
            rows[(3 + other - r) * knots_y + first, ty * BLOCK + at] = 1.0
            rows[(3 - other + r) * knots_y + second, ty * BLOCK + at] = 1.0
        for member in range(2):
            for r in range(REACH_Y):
                knot = ty * cells_y - 1 + r
                if 0 <= knot < knots_y:
                    rows[(7 + member) * knots_y + knot, ty * BLOCK + member * REACH_Y + r] = 1.0
    return cols.astype(B16), np.concatenate([rows, rows], axis=1).astype(B16)


def dot(left, right):
    return jnp.dot(left, right, preferred_element_type=F32)


def shifted_tiles(parts, step, wanted):
    lane = lax.broadcasted_iota(jnp.int32, parts[0].shape, 1)
    rolled = [pltpu.roll(part, (-step) % 128, 1) for part in parts]
    count = len(parts)
    out = []
    for at in range(wanted):
        if step > 0:
            out.append(jnp.where(lane < 128 - step, rolled[at], rolled[(at + 1) % count]))
        else:
            out.append(jnp.where(lane >= -step, rolled[at], rolled[(at - 1) % count]))
    return out


def minds_tiled(scale, boxes_ref, minds_ref, rows):
    count = scale.shape[1] // 128
    for index in range(12):
        mind = jnp.exp(boxes_ref[index, :rows] * scale)
        for tile in range(count):
            minds_ref[index, tile, :rows] = mind[:, tile * 128 : (tile + 1) * 128]


def sums_into(minds_ref, fixed_of, lane_step, factor, terms_ref):
    height, breadth = terms_ref.shape[1:]
    tiles = breadth // 128
    once = 1.0 / (2.0 * factor)
    scales = (once, once, once * once, once * once, once * once, 1.0)
    for start in range(0, height, 8):
        base = 8 + start
        sums = None
        for index in range(12):
            own = [minds_ref[index, tile, base : base + 8] for tile in range(tiles + 1)]
            fixed = fixed_of(index, base, own)
            ahead = shifted_tiles(own, lane_step, tiles)
            behind = shifted_tiles(own, -lane_step, tiles)
            parts = []
            for tile in range(tiles):
                differ = own[tile] - fixed[tile]
                slope_y = (
                    minds_ref[index, tile, base + 1 : base + 9]
                    - minds_ref[index, tile, base - 1 : base + 7]
                )
                slope_x = ahead[tile] - behind[tile]
                parts += [
                    differ * slope_y,
                    differ * slope_x,
                    slope_y * slope_y,
                    slope_y * slope_x,
                    slope_x * slope_x,
                    differ * differ,
                ]
            sums = parts if sums is None else [a + b for a, b in zip(sums, parts)]
        for tile in range(tiles):
            for term in range(6):
                terms_ref[term, start : start + 8, tile * 128 : (tile + 1) * 128] = (
                    sums[6 * tile + term] * scales[term]
                )


def greeted_by(count_y, count_x, y, x):
    near = {(y + by_y, x + by_x) for by_y, by_x in travels}
    near = {(a, b) for a, b in near if 0 <= a < count_y and 0 <= b < count_x}
    return near | {((y + step) % count_y, x ^ 1) for step in far_greets}


def two_steps_reach(count_y, count_x):
    if count_y < 8 or count_x % 2:
        return False
    every = [(y, x) for y in range(count_y) for x in range(count_x)]
    greeted = {at: greeted_by(count_y, count_x, *at) for at in every}
    for y, x in every:
        known = greeted[y, x].union(*(greeted[at] for at in greeted[y, x]))
        if not {at for at in every if (at[1] - x) % 2 == 0 and at != (y, x)} <= known:
            return False
    return True


def gathered_kernel(
    count_y,
    count_x,
    tissue_hbm,
    fixed_hbm,
    moving_hbm,
    *rest,
):
    tables_hbm, rest = rest[:8], rest[8:]
    coef_ref, mismatch_ref = rest[:2]
    tables, rest = rest[2:10], rest[10:]
    (
        mid,
        left_side,
        right_side,
        full,
        fixed_boxes,
        boxes_ref,
        minds_ref,
        fixed_minds,
        fine_terms,
        coarse_terms,
        fine_weight,
        coarse_weight,
        tissue_ref,
        boxes,
        stencils,
        last_rows,
        last_cols,
        load_sem,
        table_sem,
        rim_send,
        rim_recv,
        block_send,
        block_recv,
        relay_send,
        relay_recv,
        ready,
    ) = rest
    fine_tables, coarse_tables, (gather_cols, gather_rows) = tables[:3], tables[3:6], tables[6:]
    ty = lax.axis_index("ty")
    tx = lax.axis_index("tx")
    count = count_y * count_x
    half = count // 2
    me = ty * count_x + tx
    parity = lax.rem(tx, 2)
    place = ty * (count_x // 2) + tx // 2
    sibling = (ty, tx + 1 - 2 * parity)
    height, breadth = fixed_hbm.shape
    cells_y, cells_x = height // SPACE, breadth // SPACE
    knots_y, knots_x = count_y * cells_y, count_x * cells_x
    width = 8 * knots_x

    def exists(by_y, by_x):
        to_y, to_x = ty + by_y, tx + by_x
        return (to_y >= 0) & (to_y < count_y) & (to_x >= 0) & (to_x < count_x)

    few = two_steps_reach(count_y, count_x)

    def greet_far(semaphore):
        for step in far_greets:
            other = (lax.rem(ty + step + count_y, count_y), sibling[1])
            pl.semaphore_signal(semaphore, 1, device_id=other, device_id_type=MESH)

    barrier = pltpu.get_barrier_semaphore()
    if few:
        for by_y, by_x in travels:

            @pl.when(exists(by_y, by_x))
            def _():
                pl.semaphore_signal(
                    barrier, 1, device_id=(ty + by_y, tx + by_x), device_id_type=MESH
                )

        greet_far(barrier)
        edge_y = jnp.where((ty == 0) | (ty == count_y - 1), 1, 0)
        edge_x = jnp.where((tx == 0) | (tx == count_x - 1), 1, 0)
        greeters = (3 - edge_y) * (3 - edge_x) - 1 + len(far_greets)
    else:
        for step in range(1, count):
            other = lax.rem(me + step, count)
            other = (other // count_x, lax.rem(other, count_x))
            pl.semaphore_signal(barrier, 1, device_id=other, device_id_type=MESH)
        greeters = count - 1

    tissue_load = pltpu.make_async_copy(tissue_hbm, tissue_ref, load_sem.at[2])
    tissue_load.start()
    loads = []
    for image, ref in enumerate((fixed_hbm, moving_hbm)):
        loads.append(
            pltpu.make_async_copy(ref, mid.at[image, RIM : RIM + height], load_sem.at[image])
        )
        loads[image].start()
    table_loads = []
    for index, (source, target) in enumerate(zip(tables_hbm, tables)):
        table_loads.append(pltpu.make_async_copy(source, target, table_sem.at[index]))
        table_loads[index].start()

    low, high = slice(0, RIM), slice(RIM + height, 2 * RIM + height)

    @pl.when(ty == 0)
    def _():
        for ref in (mid, left_side, right_side):
            ref[:, low] = jnp.zeros((2, RIM, ref.shape[2]), F32)

    @pl.when(ty == count_y - 1)
    def _():
        for ref in (mid, left_side, right_side):
            ref[:, high] = jnp.zeros((2, RIM, ref.shape[2]), F32)

    @pl.when(tx == 0)
    def _():
        left_side[...] = jnp.zeros(left_side.shape, F32)

    @pl.when(tx == count_x - 1)
    def _():
        right_side[...] = jnp.zeros(right_side.shape, F32)

    lane = lax.broadcasted_iota(jnp.int32, (8, breadth), 1)
    even = lax.rem(lane, 2) == 0
    tissue_load.wait()
    for i in range(cells_y):
        line = jnp.zeros((8, breadth), F32)
        for j in range(cells_x):
            value = tissue_ref[i, j].astype(F32)
            inside = (lane >= j * SPACE) & (lane < (j + 1) * SPACE)
            line = jnp.where(inside, value, line)
        halved = jnp.where(even, 0.0, line)
        for part in range(SPACE // 8):
            start = i * SPACE + part * 8
            fine_weight[start : start + 8] = line
        for part in range(SPACE // 16):
            start = i * (SPACE // 2) + part * 8
            coarse_weight[start : start + 8] = halved

    def rows_of(travel):
        if travel == 0:
            return slice(0, height), slice(RIM, RIM + height)
        if travel > 0:
            return slice(height - RIM, height), low
        return slice(0, RIM), high

    def landing(travel_y, travel_x):
        ref = mid if travel_x == 0 else (left_side if travel_x > 0 else right_side)
        return ref.at[:, rows_of(travel_y)[1]]

    pl.semaphore_wait(barrier, greeters)

    for index, (travel_y, travel_x) in enumerate(travels):

        @pl.when(exists(travel_y, travel_x))
        def _():
            source_rows = rows_of(travel_y)[0]
            if travel_x == 0:
                lanes = slice(0, breadth)
            elif travel_x > 0:
                lanes = slice(breadth - 128, breadth)
            else:
                lanes = slice(0, 128)
            for image, ref in enumerate((fixed_hbm, moving_hbm)):
                pltpu.make_async_remote_copy(
                    src_ref=ref.at[source_rows, lanes],
                    dst_ref=landing(travel_y, travel_x).at[image],
                    send_sem=rim_send.at[index],
                    recv_sem=rim_recv.at[index],
                    device_id=(ty + travel_y, tx + travel_x),
                    device_id_type=MESH,
                ).start()

    if few:
        greet_far(ready)

    knot = lax.broadcasted_iota(jnp.int32, (128, breadth), 0)
    at_x = lax.broadcasted_iota(jnp.int32, (128, breadth), 1).astype(F32) / SPACE
    last = bspline(at_x - (knot - tx * cells_x).astype(F32))
    last_high, last_low = split(jnp.where(knot < knots_x, last, 0.0))
    last_cols[:, :breadth] = last_high
    last_cols[:, breadth:] = last_low
    knot = lax.broadcasted_iota(jnp.int32, (height, 128), 1)
    at_y = lax.broadcasted_iota(jnp.int32, (height, 128), 0).astype(F32) / SPACE
    third = knot // knots_y
    last_high, last_low = split(
        bspline(at_y - (lax.rem(knot, knots_y) - ty * cells_y).astype(F32))
    )
    kept = jnp.where(third < 2, last_high.astype(F32), last_low.astype(F32))
    last_rows[...] = jnp.where(third < 3, kept, 0.0).astype(B16)

    for load in loads:
        load.wait()

    for index, (travel_y, travel_x) in enumerate(travels):

        @pl.when(exists(-travel_y, -travel_x))
        def _():
            spot = landing(travel_y, travel_x)
            pltpu.make_async_copy(spot, spot, rim_recv.at[index]).wait()

    tiles = breadth // 128
    side_lane = lax.broadcasted_iota(jnp.int32, (height + 2 * RIM, 128), 1)
    for image in range(2):
        for tile in range(tiles):
            full[image * (tiles + 1) + tile] = mid[image, :, tile * 128 : (tile + 1) * 128]
        full[image * (tiles + 1) + tiles] = jnp.where(
            side_lane < 64, right_side[image], left_side[image]
        )

    def fine_image(image):
        base = image * (tiles + 1)
        return jnp.concatenate(
            [full[base + tile, 8 : height + 24] for tile in range(tiles + 1)], axis=1
        )

    def coarse_pair():
        span = height // 2 + RIM
        summed = []
        for image in range(2):
            base = image * (tiles + 1)
            summed.append(
                jnp.concatenate(
                    [
                        full[base + tile, pl.ds(0, span, stride=2), :]
                        + full[base + tile, pl.ds(1, span, stride=2), :]
                        for tile in range(tiles + 1)
                    ],
                    axis=1,
                )
            )
        fixed, moving = summed
        at = lax.broadcasted_iota(jnp.int32, fixed.shape, 1)
        pair = jnp.where(
            lax.rem(at, 2) == 0, fixed + moved(fixed, 0, 1), moving + moved(moving, 0, -1)
        )
        return 0.25 * pair

    def coarse_terms_into():
        pair = coarse_pair()
        minds_tiled(minds_into(pair, 2, boxes_ref), boxes_ref, minds_ref, pair.shape[0])

        def fixed_of(index, base, own):
            return shifted_tiles(own, -1, tiles)

        sums_into(minds_ref, fixed_of, 2, 2, coarse_terms)

    def fine_terms_into():
        fixed_minds[...] = minds_into(fine_image(0), 1, fixed_boxes)[8 : 8 + height, :breadth]
        image = fine_image(1)
        minds_tiled(minds_into(image, 1, boxes_ref), boxes_ref, minds_ref, image.shape[0])

        def fixed_of(index, base, own):
            return [
                jnp.exp(
                    fixed_boxes[index, base : base + 8, tile * 128 : (tile + 1) * 128]
                    * fixed_minds[base - 8 : base, tile * 128 : (tile + 1) * 128]
                )
                for tile in range(tiles)
            ]

        sums_into(minds_ref, fixed_of, 1, 1, fine_terms)

    def block_of(terms_ref, weight_ref, level):
        row_pairs, row_lines, col_table = level
        weight = weight_ref[...]
        upper, lower = split(
            jnp.concatenate([weight * terms_ref[index] for index in (2, 3, 4)], axis=1)
        )
        pairs = dot(row_pairs[...], jnp.concatenate([upper, lower, upper], axis=0))
        stack = []
        for member in range(2):
            upper, lower = split(weight * terms_ref[member])
            stack += [upper, lower, upper]
        lines = dot(row_lines[...], jnp.concatenate(stack, axis=0))
        upper, lower = split(jnp.concatenate([pairs, lines], axis=1))
        out = dot(jnp.concatenate([upper, lower], axis=0), col_table[...])
        return out[:BLOCK, :128] + out[BLOCK:, :128] + out[:BLOCK, 128:]

    def send_block(level, block):
        boxes[level, parity, place] = block
        order = [(a, b) for a in range(count_y) for b in range(count_x // 2) if a + b]
        for step_y, step_x in sorted(order, key=lambda p: abs(p[0] - count_y // 2) - p[1]):
            if True:
                to_y = lax.rem(ty + step_y, count_y)
                to_x = 2 * lax.rem(tx // 2 + step_x, count_x // 2) + parity
                pltpu.make_async_remote_copy(
                    src_ref=boxes.at[level, parity, place],
                    dst_ref=boxes.at[level, parity, place],
                    send_sem=block_send.at[level],
                    recv_sem=block_recv.at[level],
                    device_id=(to_y, to_x),
                    device_id_type=MESH,
                ).start()

    def relay_of(level):
        return pltpu.make_async_remote_copy(
            src_ref=boxes.at[level, parity],
            dst_ref=boxes.at[level, parity],
            send_sem=relay_send.at[level],
            recv_sem=relay_recv.at[level],
            device_id=sibling,
            device_id_type=MESH,
        )

    def relay(level):
        part = boxes.at[level, 0, 0 : half - 1]
        pltpu.make_async_copy(part, part, block_recv.at[level]).wait()
        relay_of(level).start()
        spot = boxes.at[level, 1 - parity]
        pltpu.make_async_copy(spot, spot, relay_recv.at[level]).wait()

    def assemble(level):
        columns = []
        for to_x in range(count_x):
            columns.append(
                jnp.concatenate(
                    [
                        boxes[level, to_x % 2, to_y * (count_x // 2) + to_x // 2]
                        for to_y in range(count_y)
                    ],
                    axis=0,
                )
            )
        upper, lower = split(jnp.concatenate(columns, axis=1))
        out = dot(jnp.concatenate([upper, lower], axis=0), gather_cols[...])
        rows = count_y * BLOCK
        upper, lower = split(out[:rows] + out[rows:])
        stencils[level] = dot(gather_rows[...], jnp.concatenate([upper, lower], axis=0))

    group = lax.broadcasted_iota(jnp.int32, (knots_y, 128), 1) // knots_x

    def spread(values):
        halves = []
        for start in (-3, 1):
            out = None
            for index in range(4):
                gap = start + index
                rolled = pltpu.roll(values, (-gap) % 128, 1) if gap else values
                out = rolled if out is None else jnp.where(group >= index, rolled, out)
            halves.append(out)
        return halves

    def start_of(level):
        return [
            stencils[level, (7 + member) * knots_y : (8 + member) * knots_y, 3 * width :]
            for member in range(2)
        ]

    def pull(level, pair):
        spreads = [spread(values) for values in pair]
        sums = [None, None]
        for gap in range(-3, 4):
            at = (gap + 3) * knots_y
            for source in range(2):
                for part in range(2):
                    shifted = spreads[source][part]
                    if gap:
                        shifted = pltpu.roll(shifted, (-gap) % knots_y, 0)
                    for member in range(2):
                        lanes = (member + source) * width + part * 128
                        term = stencils[level, at : at + knots_y, lanes : lanes + 128] * shifted
                        old = sums[member]
                        sums[member] = term if old is None else old + term
        out = []
        for total in sums:
            total = total + pltpu.roll(total, 64, 1)
            out.append(total + pltpu.roll(total, 32, 1))
        return out

    def inner(first, second):
        return jnp.sum(first[0] * second[0] + first[1] * second[1], keepdims=True)

    def descend(level, control, gradient):
        image = pull(level, gradient)
        step = inner(gradient, gradient) / inner(gradient, image)
        control = [c - step * g for c, g in zip(control, gradient)]
        gradient = [g - step * i for g, i in zip(gradient, image)]
        image = pull(level, gradient)
        step = inner(gradient, gradient) / inner(gradient, image)
        return [c - step * g for c, g in zip(control, gradient)]

    for load in table_loads:
        load.wait()
    coarse_terms_into()
    coarse_block = block_of(coarse_terms, coarse_weight, coarse_tables)
    if few:
        pl.semaphore_wait(ready, len(far_greets))
    send_block(0, coarse_block)
    fine_terms_into()
    send_block(1, block_of(fine_terms, fine_weight, fine_tables))

    relay(0)
    assemble(0)
    control = [jnp.zeros((knots_y, 128), F32)] * 2
    control = descend(0, control, start_of(0))
    relay(1)
    assemble(1)
    gradient = [b + i for b, i in zip(start_of(1), pull(1, control))]
    control = descend(1, control, gradient)

    upper, lower = split(jnp.concatenate(control, axis=0))
    rows = 2 * knots_y
    out = dot(jnp.concatenate([upper, lower], axis=0), last_cols[...])
    lines = out[:rows, :breadth] + out[rows:, :breadth] + out[:rows, breadth:]
    upper, lower = split(jnp.concatenate([lines[:knots_y], lines[knots_y:]], axis=1))
    blank = jnp.zeros((128 - 3 * knots_y, 2 * breadth), B16)
    field = dot(last_rows[...], jnp.concatenate([upper, lower, upper, blank], axis=0))
    field_y, field_x = field[:, :breadth], field[:, breadth:]
    pull_y = fine_terms[2] * field_y + fine_terms[3] * field_x
    pull_x = fine_terms[3] * field_y + fine_terms[4] * field_x
    mismatch_ref[...] = (
        fine_terms[5]
        + 2.0 * (fine_terms[0] * field_y + fine_terms[1] * field_x)
        + field_y * pull_y
        + field_x * pull_x
    )
    for member in range(2):
        own = pltpu.roll(control[member], lax.rem(128 - cells_x * tx, 128), 1)
        own = pltpu.roll(own, lax.rem(knots_y - cells_y * ty, knots_y), 0)
        coef_ref[member] = own[:cells_y, :cells_x]

    for index, (travel_y, travel_x) in enumerate(travels):

        @pl.when(exists(travel_y, travel_x))
        def _():
            spot = landing(travel_y, travel_x)
            pltpu.make_async_copy(spot, spot, rim_send.at[index]).wait()

    for level in range(2):
        part = boxes.at[level, 0, 0 : half - 1]
        pltpu.make_async_copy(part, part, block_send.at[level]).wait()
        relay_of(level).wait_send()


def spread_call(count_y, count_x, tissue, fixed_image, moving_image):
    height, breadth = fixed_image.shape
    cells_y, cells_x = height // SPACE, breadth // SPACE
    count = count_y * count_x
    tall, full_lanes = height + 2 * RIM, breadth + 128
    vmem = pltpu.VMEM
    scratch = [
        vmem((2, tall, breadth), F32),
        vmem((2, tall, 128), F32),
        vmem((2, tall, 128), F32),
        vmem((2 * (breadth // 128 + 1), tall, 128), F32),
        vmem((12, height + 16, full_lanes), F32),
        vmem((12, height + 16, full_lanes), F32),
        vmem((6, height, breadth), F32),
        vmem((6, height // 2, breadth), F32),
        vmem((height, breadth), F32),
        vmem((height // 2, breadth), F32),
        vmem((REACH_Y, height, 128), F32),
        vmem((REACH_Y, height // 2, 128), F32),
        vmem((REACH_X, 8, breadth), F32),
        vmem((REACH_X, 8, breadth), F32),
        pltpu.SMEM((cells_y, cells_x), jnp.int32),
        vmem((4, 15, 8, 128), F32),
        vmem((2, count, 1, 128), F32),
        pltpu.SemaphoreType.DMA((3,)),
        pltpu.SemaphoreType.DMA((8,)),
        pltpu.SemaphoreType.DMA((8,)),
        pltpu.SemaphoreType.DMA((15,)),
        pltpu.SemaphoreType.DMA((4, 15)),
        pltpu.SemaphoreType.DMA((2,)),
        pltpu.SemaphoreType.DMA((2,)),
    ]
    return pl.pallas_call(
        functools.partial(spread_kernel, count_y, count_x),
        out_shape=(
            jax.ShapeDtypeStruct((2, cells_y, cells_x), F32),
            jax.ShapeDtypeStruct((height, breadth), F32),
        ),
        in_specs=[
            pl.BlockSpec(memory_space=pltpu.HBM),
            pl.BlockSpec(memory_space=pltpu.HBM),
            pl.BlockSpec(memory_space=pltpu.HBM),
        ],
        out_specs=(
            pl.BlockSpec(memory_space=pltpu.VMEM),
            pl.BlockSpec(memory_space=pltpu.VMEM),
        ),
        scratch_shapes=scratch,
        compiler_params=pltpu.CompilerParams(
            collective_id=0, has_side_effects=True, vmem_limit_bytes=16 * 1024 * 1024
        ),
    )(tissue, fixed_image, moving_image)


def closing(coef_in, mismatch_in, coef_out, mismatch_out, sem):
    loads = [
        pltpu.make_async_copy(mismatch_in, mismatch_out, sem.at[0]),
        pltpu.make_async_copy(coef_in, coef_out, sem.at[1]),
    ]
    for load in loads:
        load.start()
    for load in loads:
        load.wait()


def gathered_call(count_y, count_x, tissue, fixed_image, moving_image):
    height, breadth = fixed_image.shape
    cells_y, cells_x = height // SPACE, breadth // SPACE
    count = count_y * count_x
    tall, full_lanes = height + 2 * RIM, breadth + 128
    vmem, dma = pltpu.VMEM, pltpu.SemaphoreType.DMA
    tables = (
        level_tables(height, breadth, 1)
        + level_tables(height, breadth, 2)
        + assembly_tables(count_y, count_x, cells_y, cells_x)
    )
    scratch = [vmem(table.shape, B16) for table in tables] + [
        vmem((2, tall, breadth), F32),
        vmem((2, tall, 128), F32),
        vmem((2, tall, 128), F32),
        vmem((2 * (breadth // 128 + 1), tall, 128), F32),
        vmem((12, height + 16, full_lanes), F32),
        vmem((12, height + 16, full_lanes), F32),
        vmem((12, breadth // 128 + 1, height + 16, 128), F32),
        vmem((height, breadth), F32),
        vmem((6, height, breadth), F32),
        vmem((6, height // 2, breadth), F32),
        vmem((height, breadth), F32),
        vmem((height // 2, breadth), F32),
        pltpu.SMEM((cells_y, cells_x), jnp.int32),
        vmem((2, 2, count // 2, BLOCK, 128), F32),
        vmem((2, tables[7].shape[0], tables[6].shape[1]), F32),
        vmem((height, 128), B16),
        vmem((128, 2 * breadth), B16),
        dma((3,)),
        dma((8,)),
        dma((8,)),
        dma((8,)),
        dma((2,)),
        dma((2,)),
        dma((2,)),
        dma((2,)),
        pltpu.SemaphoreType.REGULAR,
    ]
    held = [
        pltpu.with_memory_space_constraint(jnp.asarray(table), pltpu.HBM) for table in tables
    ]
    return pl.pallas_call(
        functools.partial(gathered_kernel, count_y, count_x),
        out_shape=(
            jax.ShapeDtypeStruct((2, cells_y, cells_x), F32),
            jax.ShapeDtypeStruct((height, breadth), F32),
        ),
        in_specs=[pl.BlockSpec(memory_space=pltpu.HBM)] * 11,
        out_specs=(
            pl.BlockSpec(memory_space=pltpu.VMEM),
            pl.BlockSpec(memory_space=pltpu.VMEM),
        ),
        scratch_shapes=scratch,
        compiler_params=pltpu.CompilerParams(
            collective_id=1, has_side_effects=True, vmem_limit_bytes=32 * 1024 * 1024
        ),
    )(tissue, fixed_image, moving_image, *held)


def shards(count_y, count_x, fixed_image, moving_image, tissue):
    held = [pltpu.with_memory_space_constraint(x, pltpu.HBM) for x in (tissue, fixed_image, moving_image)]
    height, breadth = fixed_image.shape
    fits = height == 2 * SPACE and breadth == 8 * SPACE and count_x % 2 == 0
    fits = fits and count_x * (breadth // SPACE) == 32 and count_y * count_x <= LARGEST
    call = gathered_call if fits else spread_call
    coef, mismatch = call(count_y, count_x, *held)
    return pl.pallas_call(
        closing,
        out_shape=(
            jax.ShapeDtypeStruct(coef.shape, F32),
            jax.ShapeDtypeStruct(mismatch.shape, F32),
        ),
        in_specs=[pl.BlockSpec(memory_space=pl.ANY)] * 2,
        out_specs=(pl.BlockSpec(memory_space=pltpu.HBM),) * 2,
        scratch_shapes=[pltpu.SemaphoreType.DMA((2,))],
        compiler_params=pltpu.CompilerParams(vmem_limit_bytes=4 * 1024 * 1024),
    )(coef, mismatch)


def solution(mesh):
    placed = (P("ty", "tx"), P("ty", "tx"), P("ty", "tx"))
    return jax.shard_map(
        functools.partial(shards, mesh.shape["ty"], mesh.shape["tx"]),
        mesh=mesh,
        in_specs=placed,
        out_specs=(P(None, "ty", "tx"), P("ty", "tx")),
        check_vma=False,
    )
```

```python
import functools

import jax
import jax.numpy as jnp
import numpy as np
from jax import lax
from jax.experimental import pallas as pl
from jax.experimental.pallas import tpu as pltpu
from jax.sharding import PartitionSpec as P

SPACE = 32
REACH_Y = 5
REACH_X = 11
RIM = 16
SEGMENT = 16
SET = 32
OWN_SLOT = 7
MESH = pl.DeviceIdType.MESH
F32 = jnp.float32
B16 = jnp.bfloat16
BLOCK = 16
PARTS = 3
LOG2E = 1.4426950408889634
LARGEST = 64

half_offsets = ((0, 2), (2, 0), (2, 2), (2, -2), (0, 4), (4, 0))
far_greets = (2, -2, 4)
travels = ((-1, 0), (1, 0), (0, -1), (0, 1), (-1, -1), (-1, 1), (1, -1), (1, 1))


def bspline(values):
    magnitude = jnp.abs(values)
    near_part = 2.0 / 3.0 - magnitude * magnitude + 0.5 * magnitude * magnitude * magnitude
    rest = 2.0 - magnitude
    far_part = rest * rest * rest / 6.0
    return jnp.where(magnitude < 1.0, near_part, jnp.where(magnitude < 2.0, far_part, 0.0))


def moved(values, by_y, by_x):
    rows, lanes = values.shape
    if by_x:
        values = pltpu.roll(values, (-by_x) % lanes, 1)
    if by_y:
        values = pltpu.roll(values, (-by_y) % rows, 0)
    return values


def minds_into(image, lane_step, out_ref):
    total = None
    for index, (offset_y, offset_x) in enumerate(half_offsets):
        gap = image - moved(image, offset_y, lane_step * offset_x)
        square = gap * gap
        rows = square + moved(square, 1, 0) + moved(square, -1, 0)
        box = rows + moved(rows, 0, lane_step) + moved(rows, 0, -lane_step)
        other = moved(box, -offset_y, -lane_step * offset_x)
        out_ref[2 * index, : image.shape[0]] = box
        out_ref[2 * index + 1, : image.shape[0]] = other
        both = box + other
        total = both if total is None else total + both
    return -1.0 / (total / 12.0 + 0.9)


def terms_into(fixed, moving, lane_step, factor, fixed_ref, moving_ref, terms_ref, wide):
    rows = fixed.shape[0]
    height = rows - 16
    fixed_scale = minds_into(fixed, lane_step, fixed_ref)[8 : 8 + height, :wide]
    moving_scale = minds_into(moving, lane_step, moving_ref)
    sums = None
    for index in range(12):
        fixed_mind = jnp.exp(fixed_ref[index, 8 : 8 + height, :wide] * fixed_scale)
        mind = jnp.exp(moving_ref[index, :rows] * moving_scale)
        differ = mind[8 : 8 + height, :wide] - fixed_mind
        slope_y = moved(mind[:, :wide], 1, 0) - moved(mind[:, :wide], -1, 0)
        slope_y = slope_y[8 : 8 + height]
        own = mind[8 : 8 + height]
        slope_x = (moved(own, 0, lane_step) - moved(own, 0, -lane_step))[:, :wide]
        parts = (
            differ * slope_y,
            differ * slope_x,
            slope_y * slope_y,
            slope_y * slope_x,
            slope_x * slope_x,
            differ * differ,
        )
        sums = parts if sums is None else tuple(a + b for a, b in zip(sums, parts))
    once = 1.0 / (2.0 * factor)
    scales = (once, once, once * once, once * once, once * once, 1.0)
    for index in range(6):
        terms_ref[index] = sums[index] * scales[index]


def spread_kernel(
    count_y,
    count_x,
    tissue_hbm,
    fixed_hbm,
    moving_hbm,
    coef_ref,
    mismatch_ref,
    mid,
    left_side,
    right_side,
    full,
    fixed_minds,
    moving_minds,
    fine_terms,
    coarse_terms,
    fine_weight,
    coarse_weight,
    fine_rows,
    coarse_rows,
    fine_cols,
    coarse_cols,
    tissue_ref,
    tiles_box,
    scalar_box,
    load_sem,
    rim_send,
    rim_recv,
    tile_send,
    tile_recv,
    scalar_send,
    scalar_recv,
):
    ty = lax.axis_index("ty")
    tx = lax.axis_index("tx")
    count = count_y * count_x
    me = ty * count_x + tx
    height, breadth = fixed_hbm.shape
    knots = count_x * (breadth // SPACE)
    cells_y, cells_x = height // SPACE, breadth // SPACE

    def peer(step):
        other = lax.rem(me + step, count)
        return (other // count_x, lax.rem(other, count_x))

    def for_peers(act):
        if count <= 64:
            for step in range(1, count):
                act(peer(step))
        else:

            def body(step, carry):
                act(peer(step))
                return carry

            lax.fori_loop(1, count, body, 0)

    tissue_load = pltpu.make_async_copy(tissue_hbm, tissue_ref, load_sem.at[2])
    tissue_load.start()
    loads = []
    for image, ref in enumerate((fixed_hbm, moving_hbm)):
        loads.append(
            pltpu.make_async_copy(ref, mid.at[image, RIM : RIM + height], load_sem.at[image])
        )
        loads[image].start()

    low, high = slice(0, RIM), slice(RIM + height, 2 * RIM + height)

    @pl.when(ty == 0)
    def _():
        for ref in (mid, left_side, right_side):
            ref[:, low] = jnp.zeros((2, RIM, ref.shape[2]), F32)

    @pl.when(ty == count_y - 1)
    def _():
        for ref in (mid, left_side, right_side):
            ref[:, high] = jnp.zeros((2, RIM, ref.shape[2]), F32)

    @pl.when(tx == 0)
    def _():
        left_side[...] = jnp.zeros(left_side.shape, F32)

    @pl.when(tx == count_x - 1)
    def _():
        right_side[...] = jnp.zeros(right_side.shape, F32)

    tiles_box[...] = jnp.zeros(tiles_box.shape, F32)

    barrier = pltpu.get_barrier_semaphore()
    near = 2 <= count_y <= 8 and 2 <= count_x <= 4
    greeted = [(y, x) for y in range(-1, 2) for x in range(-1, 2) if (y, x) != (0, 0)]
    if count_y == 8:
        greeted += [(1 - count_y, 0), (count_y - 1, 0)]

    def here(by_y, by_x):
        to_y, to_x = ty + by_y, tx + by_x
        return (to_y >= 0) & (to_y < count_y) & (to_x >= 0) & (to_x < count_x)

    def greet(device):
        pl.semaphore_signal(barrier, 1, device_id=device, device_id_type=MESH)

    if near:
        for by_y, by_x in greeted:

            @pl.when(here(by_y, by_x))
            def _():
                greet((ty + by_y, tx + by_x))

    else:
        for_peers(greet)

    lane = lax.broadcasted_iota(jnp.int32, (8, breadth), 1)
    for k in range(REACH_X):
        fine_cols[k] = bspline(lane.astype(F32) / SPACE - (k - 1.0))
        coarse_cols[k] = bspline((lane.astype(F32) + 0.5) / SPACE - (k - 1.0))
    row = lax.broadcasted_iota(jnp.int32, (height, 128), 0).astype(F32)
    coarse_row = lax.broadcasted_iota(jnp.int32, (height // 2, 128), 0).astype(F32)
    for r in range(REACH_Y):
        fine_rows[r] = bspline(row / SPACE - (r - 1.0))
        coarse_rows[r] = bspline((2.0 * coarse_row + 0.5) / SPACE - (r - 1.0))
    even = lax.rem(lane, 2) == 0
    tissue_load.wait()
    for i in range(cells_y):
        line = jnp.zeros((8, breadth), F32)
        for j in range(cells_x):
            value = tissue_ref[i, j].astype(F32)
            inside = (lane >= j * SPACE) & (lane < (j + 1) * SPACE)
            line = jnp.where(inside, value, line)
        half = jnp.where(even, line, 0.0)
        for part in range(SPACE // 8):
            start = i * SPACE + part * 8
            fine_weight[start : start + 8] = line
        for part in range(SPACE // 16):
            start = i * (SPACE // 2) + part * 8
            coarse_weight[start : start + 8] = half

    if near:
        edge_y = jnp.where((ty == 0) | (ty == count_y - 1), 1, 0)
        edge_x = jnp.where((tx == 0) | (tx == count_x - 1), 1, 0)
        greeters = (3 - edge_y) * (3 - edge_x) - 1
        if count_y == 8:
            greeters = greeters + edge_y
        pl.semaphore_wait(barrier, greeters)
    else:
        pl.semaphore_wait(barrier, count - 1)

    def rows_of(travel):
        if travel == 0:
            return slice(0, height), slice(RIM, RIM + height)
        if travel > 0:
            return slice(height - RIM, height), low
        return slice(0, RIM), high

    def landing(travel_y, travel_x):
        ref = mid if travel_x == 0 else (left_side if travel_x > 0 else right_side)
        return ref.at[:, rows_of(travel_y)[1]]

    def exists(travel_y, travel_x):
        to_y, to_x = ty + travel_y, tx + travel_x
        return (to_y >= 0) & (to_y < count_y) & (to_x >= 0) & (to_x < count_x)

    for index, (travel_y, travel_x) in enumerate(travels):

        @pl.when(exists(travel_y, travel_x))
        def _():
            source_rows = rows_of(travel_y)[0]
            if travel_x == 0:
                lanes = slice(0, breadth)
            elif travel_x > 0:
                lanes = slice(breadth - 128, breadth)
            else:
                lanes = slice(0, 128)
            for image, ref in enumerate((fixed_hbm, moving_hbm)):
                pltpu.make_async_remote_copy(
                    src_ref=ref.at[source_rows, lanes],
                    dst_ref=landing(travel_y, travel_x).at[image],
                    send_sem=rim_send.at[index],
                    recv_sem=rim_recv.at[index],
                    device_id=(ty + travel_y, tx + travel_x),
                    device_id_type=MESH,
                ).start()

    for load in loads:
        load.wait()

    for index, (travel_y, travel_x) in enumerate(travels):

        @pl.when(exists(-travel_y, -travel_x))
        def _():
            place = landing(travel_y, travel_x)
            pltpu.make_async_copy(place, place, rim_recv.at[index]).wait()

    tiles = breadth // 128
    side_lane = lax.broadcasted_iota(jnp.int32, (height + 2 * RIM, 128), 1)
    for image in range(2):
        for tile in range(tiles):
            full[image * (tiles + 1) + tile] = mid[image, :, tile * 128 : (tile + 1) * 128]
        full[image * (tiles + 1) + tiles] = jnp.where(
            side_lane < 64, right_side[image], left_side[image]
        )

    def fine_image(image):
        base = image * (tiles + 1)
        return jnp.concatenate(
            [full[base + tile, 8 : height + 24] for tile in range(tiles + 1)], axis=1
        )

    def coarse_image(image):
        base = image * (tiles + 1)
        span = height // 2 + RIM
        summed = jnp.concatenate(
            [
                full[base + tile, pl.ds(0, span, stride=2), :]
                + full[base + tile, pl.ds(1, span, stride=2), :]
                for tile in range(tiles + 1)
            ],
            axis=1,
        )
        return 0.25 * (summed + moved(summed, 0, 1))

    terms_into(
        coarse_image(0), coarse_image(1), 2, 2, fixed_minds, moving_minds, coarse_terms, breadth
    )

    small_lane = lax.broadcasted_iota(jnp.int32, (8, 128), 1)
    small_row = lax.broadcasted_iota(jnp.int32, (8, 128), 0)
    knot = lax.rem(small_lane, SEGMENT)
    knot_x = tx * cells_x - 1 + knot
    knot_y = ty * cells_y - 1 + small_row
    valid = (knot < REACH_X) & (small_row < REACH_Y) & (knot_x >= 0) & (knot_x < knots)
    valid = valid & (knot_y >= 0) & (knot_y < count_y * cells_y)
    own = (small_lane < SET) & (knot >= 1) & (knot <= cells_x)
    own = own & (small_row >= 1) & (small_row <= cells_y)

    def displace(window, rows_ref, cols_ref, number=0):
        fields = []
        for member in range(2):
            line = None
            for k in range(REACH_X):
                at = number * SET + member * SEGMENT + k
                part = window[:, at : at + 1] * cols_ref[k]
                line = part if line is None else line + part
            field = None
            for r in range(REACH_Y):
                weights = jnp.concatenate([rows_ref[r]] * tiles, axis=1)
                part = weights * line[r : r + 1, :]
                field = part if field is None else field + part
            fields.append(field)
        return fields

    def gather_up(pixels, rows_ref, cols_ref, number=0):
        out = jnp.zeros((8, 128), F32)
        for member in range(2):
            lines = []
            for r in range(REACH_Y):
                weights = jnp.concatenate([rows_ref[r]] * tiles, axis=1)
                lines.append(jnp.sum(weights * pixels[member], axis=0, keepdims=True))
            lines.append(jnp.zeros((8 - REACH_Y, breadth), F32))
            line = jnp.concatenate(lines, axis=0)
            for k in range(REACH_X):
                column = jnp.sum(line * cols_ref[k], axis=1, keepdims=True)
                at = number * SET + member * SEGMENT + k
                out = jnp.where(small_lane == at, column, out)
        return out

    def slot_of(by_y, by_x):
        return (by_y + 2) * 3 + by_x + 1

    around = [(y, x) for y in range(-2, 3) for x in range(-1, 2) if (y, x) != (0, 0)]

    def send_tile(turn, tile):
        tiles_box[turn, OWN_SLOT] = tile
        for by_y, by_x in around:

            @pl.when(exists(by_y, by_x))
            def _():
                slot = slot_of(-by_y, -by_x)
                pltpu.make_async_remote_copy(
                    src_ref=tiles_box.at[turn, OWN_SLOT],
                    dst_ref=tiles_box.at[turn, slot],
                    send_sem=tile_send.at[slot],
                    recv_sem=tile_recv.at[turn, slot],
                    device_id=(ty + by_y, tx + by_x),
                    device_id_type=MESH,
                ).start()

    def collect_tiles(turn):
        for by_y, by_x in around:

            @pl.when(exists(by_y, by_x))
            def _():
                slot = slot_of(by_y, by_x)
                place = tiles_box.at[turn, slot]
                pltpu.make_async_copy(place, place, tile_recv.at[turn, slot]).wait()

        window = None
        for by_x in range(-1, 2):
            total = None
            for by_y in range(-2, 3):
                part = tiles_box[turn, slot_of(by_y, by_x)]
                if by_y:
                    part = pltpu.roll(part, (2 * by_y) % 8, 0)
                if by_y == 2:
                    part = jnp.where(small_row >= 4, part, 0.0)
                if by_y == -2:
                    part = jnp.where(small_row < 1, part, 0.0)
                total = part if total is None else total + part
            if by_x:
                total = pltpu.roll(total, (8 * by_x) % 128, 1)
                reached = (knot >= 8) if by_x > 0 else (knot < REACH_X - 8)
                total = jnp.where(reached, total, 0.0)
            window = total if window is None else window + total
        return jnp.where(valid, window, 0.0)

    def send_scalars(turn, row):
        scalar_box[turn, me] = row

        def act(device):
            pltpu.make_async_remote_copy(
                src_ref=scalar_box.at[turn, me],
                dst_ref=scalar_box.at[turn, me],
                send_sem=scalar_send.at[turn],
                recv_sem=scalar_recv.at[turn],
                device_id=device,
                device_id_type=MESH,
            ).start()

        for_peers(act)

    def collect_scalars(turn):
        part = scalar_box.at[turn, 0 : count - 1]
        pltpu.make_async_copy(part, part, scalar_recv.at[turn]).wait()
        row = jnp.sum(scalar_box[turn], axis=0)
        lanes = lax.broadcasted_iota(jnp.int32, (1, 128), 1)
        return [
            jnp.sum(
                jnp.where((lanes >= SET * i) & (lanes < SET * (i + 1)), row, 0.0), keepdims=True
            )
            for i in range(4)
        ]

    def scalars(first, second, dense):
        third = jnp.where(own, second * second, 0.0)
        middle = jnp.where(own, first * second, 0.0)
        lead = jnp.where(own, first * first, 0.0)
        packed = lead + pltpu.roll(middle, SET, 1) + pltpu.roll(third, 2 * SET, 1)
        row = jnp.sum(packed, axis=0, keepdims=True)
        dense = dense + pltpu.roll(dense, 64, 1)
        dense = dense + pltpu.roll(dense, 32, 1)
        lanes = lax.broadcasted_iota(jnp.int32, (1, 128), 1)
        return jnp.where(lanes >= 3 * SET, dense, row)

    def pulled(terms_ref, motion):
        return (
            terms_ref[2] * motion[0] + terms_ref[3] * motion[1],
            terms_ref[3] * motion[0] + terms_ref[4] * motion[1],
        )

    def weighted(weight_ref, pair):
        return [weight_ref[...] * pair[0], weight_ref[...] * pair[1]]

    def density_row(weight_ref, motion, pull):
        dense = weight_ref[...] * (motion[0] * pull[0] + motion[1] * pull[1])
        line = jnp.sum(dense, axis=0, keepdims=True)
        total = line[:, :128]
        for tile in range(1, tiles):
            total = total + line[:, tile * 128 : (tile + 1) * 128]
        return total

    def steps_of(first, middle, third, fourth):
        step = first / middle
        norm = first - 2.0 * step * middle + step * step * third
        curvature = middle - 2.0 * step * third + step * step * fourth
        return step, norm / curvature

    send_tile(
        0,
        gather_up(
            weighted(coarse_weight, (coarse_terms[0], coarse_terms[1])), coarse_rows, coarse_cols
        ),
    )
    terms_into(fine_image(0), fine_image(1), 1, 1, fixed_minds, moving_minds, fine_terms, breadth)
    fine_start = gather_up(
        weighted(fine_weight, (fine_terms[0], fine_terms[1])), fine_rows, fine_cols, 1
    )
    gradient0 = collect_tiles(0)

    motion = displace(gradient0, coarse_rows, coarse_cols)
    part = gather_up(
        weighted(coarse_weight, pulled(coarse_terms, motion)), coarse_rows, coarse_cols
    )
    send_tile(1, part + fine_start)
    fine_motion0 = displace(gradient0, fine_rows, fine_cols)
    fine_part0 = gather_up(
        weighted(fine_weight, pulled(fine_terms, fine_motion0)), fine_rows, fine_cols
    )
    gradient1 = collect_tiles(1)

    motion = displace(gradient1, coarse_rows, coarse_cols)
    dense = density_row(coarse_weight, motion, pulled(coarse_terms, motion))
    send_scalars(0, scalars(gradient0, gradient1, dense))
    fine_motion1 = displace(gradient1, fine_rows, fine_cols)
    fine_part1 = gather_up(
        weighted(fine_weight, pulled(fine_terms, fine_motion1)), fine_rows, fine_cols, 1
    )
    send_tile(2, fine_part0 + fine_part1)
    fine_gradient = pltpu.roll(gradient1, 128 - SET, 1)
    images = collect_tiles(2)
    step0, step1 = steps_of(*collect_scalars(0))
    near, far = -(step0 + step1), step0 * step1
    control = near * gradient0 + far * gradient1
    direction = fine_gradient + near * images + far * pltpu.roll(images, 128 - SET, 1)

    motion2 = displace(direction, fine_rows, fine_cols)
    send_tile(
        3,
        gather_up(weighted(fine_weight, pulled(fine_terms, motion2)), fine_rows, fine_cols),
    )
    field_y = near * fine_motion0[0] + far * fine_motion1[0]
    field_x = near * fine_motion0[1] + far * fine_motion1[1]
    image = collect_tiles(3)

    motion3 = displace(image, fine_rows, fine_cols)
    dense = density_row(fine_weight, motion3, pulled(fine_terms, motion3))
    send_scalars(1, scalars(direction, image, dense))
    step0, step1 = steps_of(*collect_scalars(1))
    near, far = -(step0 + step1), step0 * step1
    control = control + near * direction + far * image
    field_y = field_y + near * motion2[0] + far * motion3[0]
    field_x = field_x + near * motion2[1] + far * motion3[1]
    pull_y, pull_x = pulled(fine_terms, (field_y, field_x))
    mismatch_ref[...] = (
        fine_terms[5]
        + 2.0 * (fine_terms[0] * field_y + fine_terms[1] * field_x)
        + field_y * pull_y
        + field_x * pull_x
    )
    for member in range(2):
        start = member * SEGMENT + 1
        coef_ref[member] = control[1 : 1 + cells_y, start : start + cells_x]

    for index, (travel_y, travel_x) in enumerate(travels):

        @pl.when(exists(travel_y, travel_x))
        def _():
            place = landing(travel_y, travel_x)
            pltpu.make_async_copy(place, place, rim_send.at[index]).wait()

    for by_y, by_x in around:

        @pl.when(exists(by_y, by_x))
        def _():
            slot = slot_of(-by_y, -by_x)
            place = tiles_box.at[:, slot]
            pltpu.make_async_copy(place, place, tile_send.at[slot]).wait()

    for turn in range(2):
        part = scalar_box.at[turn, 0 : count - 1]
        pltpu.make_async_copy(part, part, scalar_send.at[turn]).wait()


def window_pairs(span):
    return [(k, k + d) for d in range(4) for k in range(span - d)]


def split(values):
    high = values.astype(B16)
    return high, (values - high.astype(F32)).astype(B16)


def spline_array(values):
    magnitude = np.abs(values)
    rest = 2.0 - magnitude
    near_part = 2.0 / 3.0 - magnitude**2 + 0.5 * magnitude**3
    far_part = rest**3 / 6.0
    return np.where(magnitude < 1.0, near_part, np.where(magnitude < 2.0, far_part, 0.0))


def split_array(values):
    values = values.astype(np.float32)
    high = values.astype(B16)
    return high, (values - high.astype(np.float32)).astype(B16)


def strided_columns(breadth, factor):
    lane, part = np.arange(128)[None, :], np.arange(PARTS)[:, None]
    if factor == 1:
        column = PARTS * lane + part - 8
        return column, (column >= 0) & (column < breadth)
    column = PARTS * (lane - 64) + part - 6
    return column, (lane >= 64) & (column >= 0) & (column < breadth // 2)


def natural_lane(column, breadth):
    return column if column >= 0 else breadth + 128 + column


def stride_tables(breadth):
    size = breadth + 128
    fine = np.zeros((size, PARTS * 128))
    for place in range(breadth + 16):
        fine[natural_lane(place - 8, breadth), place % PARTS * 128 + place // PARTS] = 1.0
    coarse = np.zeros((2, size, PARTS * 128))
    for image in range(2):
        for place in range(breadth // 2 + 12):
            at = place % PARTS * 128 + image * 64 + place // PARTS
            for side in range(2):
                coarse[image, natural_lane(2 * (place - 6) + side, breadth), at] = 0.25
    back = fine[:breadth].T
    return tuple(table.astype(B16) for table in (fine, coarse[0], coarse[1], back))


def level_tables(height, breadth, factor):
    row_at = factor * np.arange(height // factor) + (factor - 1) / 2.0
    column, taken = strided_columns(breadth, factor)
    col_at = (factor * column + (factor - 1) / 2.0).reshape(-1)
    rows = spline_array(row_at[None, :] / SPACE - (np.arange(REACH_Y)[:, None] - 1.0))
    cols = spline_array(col_at[:, None] / SPACE - (np.arange(REACH_X)[None, :] - 1.0))
    cols = cols * taken.reshape(-1, 1)
    row_pairs = np.zeros((BLOCK, row_at.size))
    for at, (r, other) in enumerate(window_pairs(REACH_Y)):
        row_pairs[at] = rows[r] * rows[other]
    lines = np.zeros((2, BLOCK, row_at.size))
    for member in range(2):
        lines[member, member * REACH_Y : (member + 1) * REACH_Y] = rows
    pairs = window_pairs(REACH_X)
    col_table = np.zeros((4, col_at.size, 128))
    for comp in range(3):
        for at, (k, other) in enumerate(pairs):
            col_table[comp, :, comp * len(pairs) + at] = cols[:, k] * cols[:, other]
    col_table[3, :, 3 * len(pairs) : 3 * len(pairs) + REACH_X] = cols

    def left(table):
        high, low = split_array(table)
        return np.concatenate([high, high, low], axis=1)

    high, low = split_array(col_table.reshape(4 * col_at.size, 128))
    return (
        left(row_pairs),
        np.concatenate([left(lines[0]), left(lines[1])], axis=1),
        np.concatenate([high, low], axis=1),
    )


def assembly_tables(count_y, count_x, cells_y, cells_x):
    knots_y, knots_x = count_y * cells_y, count_x * cells_x
    pairs = window_pairs(REACH_X)
    width = 8 * knots_x
    cols = np.zeros((count_x * 128, 3 * width + 128), np.float32)
    for tx in range(count_x):
        start = (tx % 2 * (count_x // 2) + tx // 2) * 128
        for comp in range(3):
            for at, (k, other) in enumerate(pairs):
                first, second = tx * cells_x - 1 + k, tx * cells_x - 1 + other
                if first < 0 or second >= knots_x:
                    continue
                source, gap = start + comp * len(pairs) + at, other - k
                cols[source, comp * width + (3 + gap) * knots_x + first] = 1.0
                cols[source, comp * width + (3 - gap) * knots_x + second] = 1.0
        for k in range(REACH_X):
            knot = tx * cells_x - 1 + k
            if 0 <= knot < knots_x:
                for group in range(128 // knots_x):
                    cols[start + 3 * len(pairs) + k, 3 * width + group * knots_x + knot] = 1.0
    rows = np.zeros((9 * knots_y, count_y * BLOCK), np.float32)
    for ty in range(count_y):
        for at, (r, other) in enumerate(window_pairs(REACH_Y)):
            first, second = ty * cells_y - 1 + r, ty * cells_y - 1 + other
            if first < 0 or second >= knots_y:
                continue
            rows[(3 + other - r) * knots_y + first, ty * BLOCK + at] = 1.0
            rows[(3 - other + r) * knots_y + second, ty * BLOCK + at] = 1.0
        for member in range(2):
            for r in range(REACH_Y):
                knot = ty * cells_y - 1 + r
                if 0 <= knot < knots_y:
                    rows[(7 + member) * knots_y + knot, ty * BLOCK + member * REACH_Y + r] = 1.0
    return cols.astype(B16), np.concatenate([rows, rows], axis=1).astype(B16)


def dot(left, right):
    return jnp.dot(left, right, preferred_element_type=F32)


def strided(parts, step):
    out = []
    for at in range(PARTS):
        carry, source = divmod(at + step, PARTS)
        part = parts[source]
        out.append(pltpu.roll(part, (-carry) % 128, 1) if carry else part)
    return out


def lowered(parts, step):
    return [pltpu.roll(part, (-step) % part.shape[0], 0) for part in parts] if step else parts


def split_three(values):
    high = values.astype(B16)
    rest = values - high.astype(F32)
    middle = rest.astype(B16)
    return [high, middle, (rest - middle.astype(F32)).astype(B16)]


def boxes_into(parts, boxes_ref):
    rows = parts[0].shape[0]
    turned = {step: strided(parts, step) for step in (2, -2, 4)}
    turned[0] = parts
    total = None
    for index, (offset_y, offset_x) in enumerate(half_offsets):
        other = lowered(turned[offset_x], offset_y)
        square = [(p - q) * (p - q) for p, q in zip(parts, other)]
        lines = [
            p + q + r for p, q, r in zip(square, lowered(square, 1), lowered(square, -1))
        ]
        box = [p + q + r for p, q, r in zip(lines, strided(lines, 1), strided(lines, -1))]
        back = lowered(strided(box, -offset_x) if offset_x else box, -offset_y)
        for at in range(PARTS):
            boxes_ref[2 * index, at, :rows] = box[at]
            boxes_ref[2 * index + 1, at, :rows] = back[at]
        both = [p + q for p, q in zip(box, back)]
        total = both if total is None else [p + q for p, q in zip(total, both)]
    return [-LOG2E / (part / 12.0 + 0.9) for part in total]


def minds_tiled(scale, boxes_ref, minds_ref):
    rows = scale[0].shape[0]
    for index in range(12):
        for at in range(PARTS):
            minds_ref[index, at, :rows] = jnp.exp2(boxes_ref[index, at, :rows] * scale[at])


def sums_into(minds_ref, fixed_of, factor, terms_ref):
    height = terms_ref.shape[1]
    once = 1.0 / (2.0 * factor)
    scales = (once, once, once * once, once * once, once * once, 1.0)
    for start in range(0, height, 8):
        base = 8 + start
        sums = None
        for index in range(12):
            own = [minds_ref[index, at, base : base + 8] for at in range(PARTS)]
            fixed = fixed_of(index, base, own)
            ahead, behind = strided(own, 1), strided(own, -1)
            parts = []
            for at in range(PARTS):
                differ = own[at] - fixed[at]
                slope_y = (
                    minds_ref[index, at, base + 1 : base + 9]
                    - minds_ref[index, at, base - 1 : base + 7]
                )
                slope_x = ahead[at] - behind[at]
                parts += [
                    differ * slope_y,
                    differ * slope_x,
                    slope_y * slope_y,
                    slope_y * slope_x,
                    slope_x * slope_x,
                    differ * differ,
                ]
            sums = parts if sums is None else [a + b for a, b in zip(sums, parts)]
        for at in range(PARTS):
            for term in range(6):
                terms_ref[term, start : start + 8, at * 128 : (at + 1) * 128] = (
                    sums[6 * at + term] * scales[term]
                )


def greeted_by(count_y, count_x, y, x):
    near = {(y + by_y, x + by_x) for by_y, by_x in travels}
    near = {(a, b) for a, b in near if 0 <= a < count_y and 0 <= b < count_x}
    return near | {((y + step) % count_y, x ^ 1) for step in far_greets}


def two_steps_reach(count_y, count_x):
    if count_y < 8 or count_x % 2:
        return False
    every = [(y, x) for y in range(count_y) for x in range(count_x)]
    greeted = {at: greeted_by(count_y, count_x, *at) for at in every}
    for y, x in every:
        known = greeted[y, x].union(*(greeted[at] for at in greeted[y, x]))
        if not {at for at in every if (at[1] - x) % 2 == 0 and at != (y, x)} <= known:
            return False
    return True


def gathered_kernel(
    count_y,
    count_x,
    tissue_hbm,
    fixed_hbm,
    moving_hbm,
    *rest,
):
    tables_hbm, rest = rest[:12], rest[12:]
    coef_ref, mismatch_ref = rest[:2]
    tables, rest = rest[2:14], rest[14:]
    (
        mid,
        left_side,
        right_side,
        full,
        fixed_boxes,
        boxes_ref,
        minds_ref,
        fixed_minds,
        fine_terms,
        coarse_terms,
        fine_weight,
        coarse_weight,
        tissue_ref,
        boxes,
        stencils,
        last_rows,
        last_cols,
        load_sem,
        table_sem,
        rim_send,
        rim_recv,
        block_send,
        block_recv,
        relay_send,
        relay_recv,
        ready,
    ) = rest
    fine_tables, coarse_tables, (gather_cols, gather_rows) = tables[:3], tables[3:6], tables[6:8]
    fine_stride, fixed_stride, moving_stride, stride_back = tables[8:]
    ty = lax.axis_index("ty")
    tx = lax.axis_index("tx")
    count = count_y * count_x
    half = count // 2
    me = ty * count_x + tx
    parity = lax.rem(tx, 2)
    place = ty * (count_x // 2) + tx // 2
    sibling = (ty, tx + 1 - 2 * parity)
    height, breadth = fixed_hbm.shape
    cells_y, cells_x = height // SPACE, breadth // SPACE
    knots_y, knots_x = count_y * cells_y, count_x * cells_x
    width = 8 * knots_x
    used = len(window_pairs(REACH_Y))
    wide = PARTS * 128

    def exists(by_y, by_x):
        to_y, to_x = ty + by_y, tx + by_x
        return (to_y >= 0) & (to_y < count_y) & (to_x >= 0) & (to_x < count_x)

    few = two_steps_reach(count_y, count_x)

    def greet_far(semaphore):
        for step in far_greets:
            other = (lax.rem(ty + step + count_y, count_y), sibling[1])
            pl.semaphore_signal(semaphore, 1, device_id=other, device_id_type=MESH)

    barrier = pltpu.get_barrier_semaphore()
    if few:
        for by_y, by_x in travels:

            @pl.when(exists(by_y, by_x))
            def _():
                pl.semaphore_signal(
                    barrier, 1, device_id=(ty + by_y, tx + by_x), device_id_type=MESH
                )

        greet_far(barrier)
        edge_y = jnp.where((ty == 0) | (ty == count_y - 1), 1, 0)
        edge_x = jnp.where((tx == 0) | (tx == count_x - 1), 1, 0)
        greeters = (3 - edge_y) * (3 - edge_x) - 1 + len(far_greets)
    else:
        for step in range(1, count):
            other = lax.rem(me + step, count)
            other = (other // count_x, lax.rem(other, count_x))
            pl.semaphore_signal(barrier, 1, device_id=other, device_id_type=MESH)
        greeters = count - 1

    tissue_load = pltpu.make_async_copy(tissue_hbm, tissue_ref, load_sem.at[2])
    tissue_load.start()
    loads = []
    for image, ref in enumerate((fixed_hbm, moving_hbm)):
        loads.append(
            pltpu.make_async_copy(ref, mid.at[image, RIM : RIM + height], load_sem.at[image])
        )
        loads[image].start()

    boxes[:, :, :, used:] = jnp.zeros((2, 2, half, BLOCK - used, 128), F32)
    low, high = slice(0, RIM), slice(RIM + height, 2 * RIM + height)

    @pl.when(ty == 0)
    def _():
        for ref in (mid, left_side, right_side):
            ref[:, low] = jnp.zeros((2, RIM, ref.shape[2]), F32)

    @pl.when(ty == count_y - 1)
    def _():
        for ref in (mid, left_side, right_side):
            ref[:, high] = jnp.zeros((2, RIM, ref.shape[2]), F32)

    @pl.when(tx == 0)
    def _():
        left_side[...] = jnp.zeros(left_side.shape, F32)

    @pl.when(tx == count_x - 1)
    def _():
        right_side[...] = jnp.zeros(right_side.shape, F32)

    lane = lax.broadcasted_iota(jnp.int32, (8, 128), 1)
    tissue_load.wait()
    for i in range(cells_y):
        for at in range(PARTS):
            fine_at = PARTS * lane + at - 8
            coarse_at = jnp.where(lane < 64, -1, 2 * (PARTS * (lane - 64) + at - 6))
            fine_line = jnp.zeros((8, 128), F32)
            coarse_line = jnp.zeros((8, 128), F32)
            for j in range(cells_x):
                value = tissue_ref[i, j].astype(F32)
                low_x, high_x = j * SPACE, (j + 1) * SPACE
                inside = (fine_at >= low_x) & (fine_at < high_x)
                fine_line = jnp.where(inside, value, fine_line)
                inside = (coarse_at >= low_x) & (coarse_at < high_x)
                coarse_line = jnp.where(inside, value, coarse_line)
            lanes = slice(at * 128, (at + 1) * 128)
            for part in range(SPACE // 8):
                start = i * SPACE + part * 8
                fine_weight[start : start + 8, lanes] = fine_line
            for part in range(SPACE // 16):
                start = i * (SPACE // 2) + part * 8
                coarse_weight[start : start + 8, lanes] = coarse_line

    def rows_of(travel):
        if travel == 0:
            return slice(0, height), slice(RIM, RIM + height)
        if travel > 0:
            return slice(height - RIM, height), low
        return slice(0, RIM), high

    def landing(travel_y, travel_x):
        ref = mid if travel_x == 0 else (left_side if travel_x > 0 else right_side)
        return ref.at[:, rows_of(travel_y)[1]]

    for load in loads:
        load.wait()
    pl.semaphore_wait(barrier, greeters)

    for index, (travel_y, travel_x) in sorted(enumerate(travels), key=lambda item: -abs(item[1][1])):

        @pl.when(exists(travel_y, travel_x))
        def _():
            source_rows = rows_of(travel_y)[0]
            if travel_x == 0:
                lanes = slice(0, breadth)
            elif travel_x > 0:
                lanes = slice(breadth - 128, breadth)
            else:
                lanes = slice(0, 128)
            source_rows = slice(source_rows.start + RIM, source_rows.stop + RIM)
            pltpu.make_async_remote_copy(
                src_ref=mid.at[:, source_rows, lanes],
                dst_ref=landing(travel_y, travel_x),
                send_sem=rim_send.at[index],
                recv_sem=rim_recv.at[index],
                device_id=(ty + travel_y, tx + travel_x),
                device_id_type=MESH,
            ).start()

    if few:
        greet_far(ready)
    table_loads = []
    for index, (source, target) in enumerate(zip(tables_hbm, tables)):
        table_loads.append(pltpu.make_async_copy(source, target, table_sem.at[index]))
        table_loads[index].start()

    knot = lax.broadcasted_iota(jnp.int32, (128, 128), 0)
    lane = lax.broadcasted_iota(jnp.int32, (128, 128), 1)
    for at in range(PARTS):
        at_x = (PARTS * lane + at - 8).astype(F32) / SPACE
        last = bspline(at_x - (knot - tx * cells_x).astype(F32))
        last_high, last_low = split(jnp.where(knot < knots_x, last, 0.0))
        last_cols[:, at * 128 : (at + 1) * 128] = last_high
        last_cols[:, wide + at * 128 : wide + (at + 1) * 128] = last_low
    knot = lax.broadcasted_iota(jnp.int32, (height, 128), 1)
    at_y = lax.broadcasted_iota(jnp.int32, (height, 128), 0).astype(F32) / SPACE
    third = knot // knots_y
    last_high, last_low = split(
        bspline(at_y - (lax.rem(knot, knots_y) - ty * cells_y).astype(F32))
    )
    kept = jnp.where(third < 2, last_high.astype(F32), last_low.astype(F32))
    last_rows[...] = jnp.where(third < 3, kept, 0.0).astype(B16)

    for index, (travel_y, travel_x) in enumerate(travels):

        @pl.when(exists(-travel_y, -travel_x))
        def _():
            spot = landing(travel_y, travel_x)
            pltpu.make_async_copy(spot, spot, rim_recv.at[index]).wait()

    tiles = breadth // 128
    side_lane = lax.broadcasted_iota(jnp.int32, (height + 2 * RIM, 128), 1)
    for image in range(2):
        for tile in range(tiles):
            full[image * (tiles + 1) + tile] = mid[image, :, tile * 128 : (tile + 1) * 128]
        full[image * (tiles + 1) + tiles] = jnp.where(
            side_lane < 64, right_side[image], left_side[image]
        )

    def fine_image(image):
        base = image * (tiles + 1)
        return jnp.concatenate(
            [full[base + tile, 8 : height + 24] for tile in range(tiles + 1)], axis=1
        )

    def coarse_image(image):
        base = image * (tiles + 1)
        span = height // 2 + RIM
        return jnp.concatenate(
            [
                full[base + tile, pl.ds(0, span, stride=2), :]
                + full[base + tile, pl.ds(1, span, stride=2), :]
                for tile in range(tiles + 1)
            ],
            axis=1,
        )

    def parts_of(values):
        return [values[:, at * 128 : (at + 1) * 128] for at in range(PARTS)]

    def coarse_terms_into():
        pair = None
        for image, table in enumerate((fixed_stride, moving_stride)):
            pieces = split_three(coarse_image(image))
            out = dot(jnp.concatenate(pieces, axis=0), table[...])
            rows = pieces[0].shape[0]
            out = out[:rows] + out[rows : 2 * rows] + out[2 * rows :]
            pair = out if pair is None else pair + out
        minds_tiled(boxes_into(parts_of(pair), boxes_ref), boxes_ref, minds_ref)

        def fixed_of(index, base, own):
            return [pltpu.roll(part, 64, 1) for part in own]

        sums_into(minds_ref, fixed_of, 2, coarse_terms)

    def fine_terms_into():
        pieces = split_three(jnp.concatenate([fine_image(0), fine_image(1)], axis=0))
        out = dot(jnp.concatenate(pieces, axis=0), fine_stride[...])
        rows = height + 16
        both = out[: 2 * rows] + out[2 * rows : 4 * rows] + out[4 * rows :]
        scale = boxes_into(parts_of(both[:rows]), fixed_boxes)
        for at in range(PARTS):
            fixed_minds[:, at * 128 : (at + 1) * 128] = scale[at][8 : 8 + height]
        minds_tiled(boxes_into(parts_of(both[rows:]), boxes_ref), boxes_ref, minds_ref)

        def fixed_of(index, base, own):
            return [
                jnp.exp2(
                    fixed_boxes[index, at, base : base + 8]
                    * fixed_minds[base - 8 : base, at * 128 : (at + 1) * 128]
                )
                for at in range(PARTS)
            ]

        sums_into(minds_ref, fixed_of, 1, fine_terms)

    def block_of(terms_ref, weight_ref, level):
        row_pairs, row_lines, col_table = level
        weight = weight_ref[...]
        upper, lower = split(
            jnp.concatenate([weight * terms_ref[index] for index in (2, 3, 4)], axis=1)
        )
        pairs = dot(row_pairs[...], jnp.concatenate([upper, lower, upper], axis=0))
        stack = []
        for member in range(2):
            upper, lower = split(weight * terms_ref[member])
            stack += [upper, lower, upper]
        lines = dot(row_lines[...], jnp.concatenate(stack, axis=0))
        upper, lower = split(jnp.concatenate([pairs, lines], axis=1))
        out = dot(jnp.concatenate([upper, lower], axis=0), col_table[...])
        return out[:BLOCK, :128] + out[BLOCK:, :128] + out[:BLOCK, 128:]

    def send_block(level, block):
        boxes[level, parity, place, 0:used] = block[:used]
        order = [(a, b) for a in range(count_y) for b in range(count_x // 2) if a + b]
        for step_y, step_x in sorted(order, key=lambda p: abs(p[0] - count_y // 2) - p[1]):
            if True:
                to_y = lax.rem(ty + step_y, count_y)
                to_x = 2 * lax.rem(tx // 2 + step_x, count_x // 2) + parity
                pltpu.make_async_remote_copy(
                    src_ref=boxes.at[level, parity, place, 0:used],
                    dst_ref=boxes.at[level, parity, place, 0:used],
                    send_sem=block_send.at[level],
                    recv_sem=block_recv.at[level],
                    device_id=(to_y, to_x),
                    device_id_type=MESH,
                ).start()

    def relay_of(level):
        return pltpu.make_async_remote_copy(
            src_ref=boxes.at[level, parity, :, 0:used],
            dst_ref=boxes.at[level, parity, :, 0:used],
            send_sem=relay_send.at[level],
            recv_sem=relay_recv.at[level],
            device_id=sibling,
            device_id_type=MESH,
        )

    def columns_of(level, side):
        across = count_x // 2
        columns = [
            jnp.concatenate(
                [boxes[level, side, to_y * across + to_x] for to_y in range(count_y)], axis=0
            )
            for to_x in range(across)
        ]
        upper, lower = split(jnp.concatenate(columns, axis=1))
        lines = pl.ds(pl.multiple_of(side * (across * 128), 128), across * 128)
        out = dot(jnp.concatenate([upper, lower], axis=0), gather_cols[lines])
        return out[: count_y * BLOCK] + out[count_y * BLOCK :]

    def relay(level):
        part = boxes.at[level, 0, 0 : half - 1, 0:used]
        pltpu.make_async_copy(part, part, block_recv.at[level]).wait()
        relay_of(level).start()

    def assemble(level, own):
        spot = boxes.at[level, 1 - parity, :, 0:used]
        pltpu.make_async_copy(spot, spot, relay_recv.at[level]).wait()
        upper, lower = split(own + columns_of(level, 1 - parity))
        stencils[level] = dot(gather_rows[...], jnp.concatenate([upper, lower], axis=0))

    group = lax.broadcasted_iota(jnp.int32, (knots_y, 128), 1) // knots_x

    def spread(values):
        halves = []
        for start in (-3, 1):
            out = None
            for index in range(4):
                gap = start + index
                rolled = pltpu.roll(values, (-gap) % 128, 1) if gap else values
                out = rolled if out is None else jnp.where(group >= index, rolled, out)
            halves.append(out)
        return halves

    def start_of(level):
        return [
            stencils[level, (7 + member) * knots_y : (8 + member) * knots_y, 3 * width :]
            for member in range(2)
        ]

    def pull(level, pair):
        spreads = [spread(values) for values in pair]
        sums = [None, None]
        for gap in range(-3, 4):
            at = (gap + 3) * knots_y
            for source in range(2):
                for part in range(2):
                    shifted = spreads[source][part]
                    if gap:
                        shifted = pltpu.roll(shifted, (-gap) % knots_y, 0)
                    for member in range(2):
                        lanes = (member + source) * width + part * 128
                        term = stencils[level, at : at + knots_y, lanes : lanes + 128] * shifted
                        old = sums[member]
                        sums[member] = term if old is None else old + term
        out = []
        for total in sums:
            total = total + pltpu.roll(total, 64, 1)
            out.append(total + pltpu.roll(total, 32, 1))
        return out

    def inner(first, second):
        return jnp.sum(first[0] * second[0] + first[1] * second[1], keepdims=True)

    def descend(level, control, gradient):
        image = pull(level, gradient)
        step = inner(gradient, gradient) / inner(gradient, image)
        control = [c - step * g for c, g in zip(control, gradient)]
        return control, [g - step * i for g, i in zip(gradient, image)]

    for load in table_loads:
        load.wait()
    coarse_terms_into()
    coarse_block = block_of(coarse_terms, coarse_weight, coarse_tables)
    if few:
        pl.semaphore_wait(ready, len(far_greets))
    send_block(0, coarse_block)
    fine_terms_into()
    send_block(1, block_of(fine_terms, fine_weight, fine_tables))

    relay(0)
    assemble(0, columns_of(0, parity))
    control = [jnp.zeros((knots_y, 128), F32)] * 2
    control, gradient = descend(0, control, start_of(0))
    relay(1)
    fine_own = columns_of(1, parity)
    control, _ = descend(0, control, gradient)
    assemble(1, fine_own)
    gradient = [b + i for b, i in zip(start_of(1), pull(1, control))]
    control, gradient = descend(1, control, gradient)
    control, _ = descend(1, control, gradient)

    upper, lower = split(jnp.concatenate(control, axis=0))
    rows = 2 * knots_y
    out = dot(jnp.concatenate([upper, lower], axis=0), last_cols[...])
    lines = out[:rows, :wide] + out[rows:, :wide] + out[:rows, wide:]
    upper, lower = split(jnp.concatenate([lines[:knots_y], lines[knots_y:]], axis=1))
    blank = jnp.zeros((128 - 3 * knots_y, 2 * wide), B16)
    field = dot(last_rows[...], jnp.concatenate([upper, lower, upper, blank], axis=0))
    field_y, field_x = field[:, :wide], field[:, wide:]
    pull_y = fine_terms[2] * field_y + fine_terms[3] * field_x
    pull_x = fine_terms[3] * field_y + fine_terms[4] * field_x
    mismatch = (
        fine_terms[5]
        + 2.0 * (fine_terms[0] * field_y + fine_terms[1] * field_x)
        + field_y * pull_y
        + field_x * pull_x
    )
    upper, lower = split(mismatch)
    out = dot(jnp.concatenate([upper, lower], axis=0), stride_back[...])
    mismatch_ref[...] = out[:height] + out[height:]
    for member in range(2):
        own = pltpu.roll(control[member], lax.rem(128 - cells_x * tx, 128), 1)
        own = pltpu.roll(own, lax.rem(knots_y - cells_y * ty, knots_y), 0)
        coef_ref[member] = own[:cells_y, :cells_x]

    for index, (travel_y, travel_x) in enumerate(travels):

        @pl.when(exists(travel_y, travel_x))
        def _():
            spot = landing(travel_y, travel_x)
            pltpu.make_async_copy(spot, spot, rim_send.at[index]).wait()

    for level in range(2):
        part = boxes.at[level, 0, 0 : half - 1, 0:used]
        pltpu.make_async_copy(part, part, block_send.at[level]).wait()
        relay_of(level).wait_send()


def spread_call(count_y, count_x, tissue, fixed_image, moving_image):
    height, breadth = fixed_image.shape
    cells_y, cells_x = height // SPACE, breadth // SPACE
    count = count_y * count_x
    tall, full_lanes = height + 2 * RIM, breadth + 128
    vmem = pltpu.VMEM
    scratch = [
        vmem((2, tall, breadth), F32),
        vmem((2, tall, 128), F32),
        vmem((2, tall, 128), F32),
        vmem((2 * (breadth // 128 + 1), tall, 128), F32),
        vmem((12, height + 16, full_lanes), F32),
        vmem((12, height + 16, full_lanes), F32),
        vmem((6, height, breadth), F32),
        vmem((6, height // 2, breadth), F32),
        vmem((height, breadth), F32),
        vmem((height // 2, breadth), F32),
        vmem((REACH_Y, height, 128), F32),
        vmem((REACH_Y, height // 2, 128), F32),
        vmem((REACH_X, 8, breadth), F32),
        vmem((REACH_X, 8, breadth), F32),
        pltpu.SMEM((cells_y, cells_x), jnp.int32),
        vmem((4, 15, 8, 128), F32),
        vmem((2, count, 1, 128), F32),
        pltpu.SemaphoreType.DMA((3,)),
        pltpu.SemaphoreType.DMA((8,)),
        pltpu.SemaphoreType.DMA((8,)),
        pltpu.SemaphoreType.DMA((15,)),
        pltpu.SemaphoreType.DMA((4, 15)),
        pltpu.SemaphoreType.DMA((2,)),
        pltpu.SemaphoreType.DMA((2,)),
    ]
    return pl.pallas_call(
        functools.partial(spread_kernel, count_y, count_x),
        out_shape=(
            jax.ShapeDtypeStruct((2, cells_y, cells_x), F32),
            jax.ShapeDtypeStruct((height, breadth), F32),
        ),
        in_specs=[
            pl.BlockSpec(memory_space=pltpu.HBM),
            pl.BlockSpec(memory_space=pltpu.HBM),
            pl.BlockSpec(memory_space=pltpu.HBM),
        ],
        out_specs=(
            pl.BlockSpec(memory_space=pltpu.VMEM),
            pl.BlockSpec(memory_space=pltpu.VMEM),
        ),
        scratch_shapes=scratch,
        compiler_params=pltpu.CompilerParams(
            collective_id=0, has_side_effects=True, vmem_limit_bytes=16 * 1024 * 1024
        ),
    )(tissue, fixed_image, moving_image)


def closing(coef_in, mismatch_in, coef_out, mismatch_out, sem):
    loads = [
        pltpu.make_async_copy(mismatch_in, mismatch_out, sem.at[0]),
        pltpu.make_async_copy(coef_in, coef_out, sem.at[1]),
    ]
    for load in loads:
        load.start()
    for load in loads:
        load.wait()


def gathered_call(count_y, count_x, tissue, fixed_image, moving_image):
    height, breadth = fixed_image.shape
    cells_y, cells_x = height // SPACE, breadth // SPACE
    count = count_y * count_x
    tall, wide = height + 2 * RIM, PARTS * 128
    vmem, dma = pltpu.VMEM, pltpu.SemaphoreType.DMA
    tables = (
        level_tables(height, breadth, 1)
        + level_tables(height, breadth, 2)
        + assembly_tables(count_y, count_x, cells_y, cells_x)
        + stride_tables(breadth)
    )
    scratch = [vmem(table.shape, B16) for table in tables] + [
        vmem((2, tall, breadth), F32),
        vmem((2, tall, 128), F32),
        vmem((2, tall, 128), F32),
        vmem((2 * (breadth // 128 + 1), tall, 128), F32),
        vmem((12, PARTS, height + 16, 128), F32),
        vmem((12, PARTS, height + 16, 128), F32),
        vmem((12, PARTS, height + 16, 128), F32),
        vmem((height, wide), F32),
        vmem((6, height, wide), F32),
        vmem((6, height // 2, wide), F32),
        vmem((height, wide), F32),
        vmem((height // 2, wide), F32),
        pltpu.SMEM((cells_y, cells_x), jnp.int32),
        vmem((2, 2, count // 2, BLOCK, 128), F32),
        vmem((2, tables[7].shape[0], tables[6].shape[1]), F32),
        vmem((height, 128), B16),
        vmem((128, 2 * wide), B16),
        dma((3,)),
        dma((12,)),
        dma((8,)),
        dma((8,)),
        dma((2,)),
        dma((2,)),
        dma((2,)),
        dma((2,)),
        pltpu.SemaphoreType.REGULAR,
    ]
    held = [
        pltpu.with_memory_space_constraint(jnp.asarray(table), pltpu.HBM) for table in tables
    ]
    return pl.pallas_call(
        functools.partial(gathered_kernel, count_y, count_x),
        out_shape=(
            jax.ShapeDtypeStruct((2, cells_y, cells_x), F32),
            jax.ShapeDtypeStruct((height, breadth), F32),
        ),
        in_specs=[pl.BlockSpec(memory_space=pltpu.HBM)] * 15,
        out_specs=(
            pl.BlockSpec(memory_space=pltpu.VMEM),
            pl.BlockSpec(memory_space=pltpu.VMEM),
        ),
        scratch_shapes=scratch,
        compiler_params=pltpu.CompilerParams(
            collective_id=1, has_side_effects=True, vmem_limit_bytes=32 * 1024 * 1024
        ),
    )(tissue, fixed_image, moving_image, *held)


def shards(count_y, count_x, fixed_image, moving_image, tissue):
    held = [pltpu.with_memory_space_constraint(x, pltpu.HBM) for x in (tissue, fixed_image, moving_image)]
    height, breadth = fixed_image.shape
    fits = height == 2 * SPACE and breadth == 8 * SPACE and count_x % 2 == 0
    fits = fits and count_x * (breadth // SPACE) == 32 and count_y * count_x <= LARGEST
    call = gathered_call if fits else spread_call
    coef, mismatch = call(count_y, count_x, *held)
    return pl.pallas_call(
        closing,
        out_shape=(
            jax.ShapeDtypeStruct(coef.shape, F32),
            jax.ShapeDtypeStruct(mismatch.shape, F32),
        ),
        in_specs=[pl.BlockSpec(memory_space=pl.ANY)] * 2,
        out_specs=(pl.BlockSpec(memory_space=pltpu.HBM),) * 2,
        scratch_shapes=[pltpu.SemaphoreType.DMA((2,))],
        compiler_params=pltpu.CompilerParams(vmem_limit_bytes=4 * 1024 * 1024),
    )(coef, mismatch)


def solution(mesh):
    placed = (P("ty", "tx"), P("ty", "tx"), P("ty", "tx"))
    return jax.shard_map(
        functools.partial(shards, mesh.shape["ty"], mesh.shape["tx"]),
        mesh=mesh,
        in_specs=placed,
        out_specs=(P(None, "ty", "tx"), P("ty", "tx")),
        check_vma=False,
    )
```

```python
import functools

import jax
import jax.numpy as jnp
import numpy as np
from jax import lax
from jax.experimental import pallas as pl
from jax.experimental.pallas import tpu as pltpu
from jax.sharding import PartitionSpec as P

SPACE = 32
REACH_Y = 5
REACH_X = 11
RIM = 16
SEGMENT = 16
SET = 32
OWN_SLOT = 7
MESH = pl.DeviceIdType.MESH
F32 = jnp.float32
B16 = jnp.bfloat16
BLOCK = 16
PARTS = 3
LOG2E = 1.4426950408889634
LARGEST = 64

half_offsets = ((0, 2), (2, 0), (2, 2), (2, -2), (0, 4), (4, 0))
far_greets = (2, -2, 4)
travels = ((-1, 0), (1, 0), (0, -1), (0, 1), (-1, -1), (-1, 1), (1, -1), (1, 1))


def bspline(values):
    magnitude = jnp.abs(values)
    near_part = 2.0 / 3.0 - magnitude * magnitude + 0.5 * magnitude * magnitude * magnitude
    rest = 2.0 - magnitude
    far_part = rest * rest * rest / 6.0
    return jnp.where(magnitude < 1.0, near_part, jnp.where(magnitude < 2.0, far_part, 0.0))


def moved(values, by_y, by_x):
    rows, lanes = values.shape
    if by_x:
        values = pltpu.roll(values, (-by_x) % lanes, 1)
    if by_y:
        values = pltpu.roll(values, (-by_y) % rows, 0)
    return values


def minds_into(image, lane_step, out_ref):
    total = None
    for index, (offset_y, offset_x) in enumerate(half_offsets):
        gap = image - moved(image, offset_y, lane_step * offset_x)
        square = gap * gap
        rows = square + moved(square, 1, 0) + moved(square, -1, 0)
        box = rows + moved(rows, 0, lane_step) + moved(rows, 0, -lane_step)
        other = moved(box, -offset_y, -lane_step * offset_x)
        out_ref[2 * index, : image.shape[0]] = box
        out_ref[2 * index + 1, : image.shape[0]] = other
        both = box + other
        total = both if total is None else total + both
    return -1.0 / (total / 12.0 + 0.9)


def terms_into(fixed, moving, lane_step, factor, fixed_ref, moving_ref, terms_ref, wide):
    rows = fixed.shape[0]
    height = rows - 16
    fixed_scale = minds_into(fixed, lane_step, fixed_ref)[8 : 8 + height, :wide]
    moving_scale = minds_into(moving, lane_step, moving_ref)
    sums = None
    for index in range(12):
        fixed_mind = jnp.exp(fixed_ref[index, 8 : 8 + height, :wide] * fixed_scale)
        mind = jnp.exp(moving_ref[index, :rows] * moving_scale)
        differ = mind[8 : 8 + height, :wide] - fixed_mind
        slope_y = moved(mind[:, :wide], 1, 0) - moved(mind[:, :wide], -1, 0)
        slope_y = slope_y[8 : 8 + height]
        own = mind[8 : 8 + height]
        slope_x = (moved(own, 0, lane_step) - moved(own, 0, -lane_step))[:, :wide]
        parts = (
            differ * slope_y,
            differ * slope_x,
            slope_y * slope_y,
            slope_y * slope_x,
            slope_x * slope_x,
            differ * differ,
        )
        sums = parts if sums is None else tuple(a + b for a, b in zip(sums, parts))
    once = 1.0 / (2.0 * factor)
    scales = (once, once, once * once, once * once, once * once, 1.0)
    for index in range(6):
        terms_ref[index] = sums[index] * scales[index]


def spread_kernel(
    count_y,
    count_x,
    tissue_hbm,
    fixed_hbm,
    moving_hbm,
    coef_ref,
    mismatch_ref,
    mid,
    left_side,
    right_side,
    full,
    fixed_minds,
    moving_minds,
    fine_terms,
    coarse_terms,
    fine_weight,
    coarse_weight,
    fine_rows,
    coarse_rows,
    fine_cols,
    coarse_cols,
    tissue_ref,
    tiles_box,
    scalar_box,
    load_sem,
    rim_send,
    rim_recv,
    tile_send,
    tile_recv,
    scalar_send,
    scalar_recv,
):
    ty = lax.axis_index("ty")
    tx = lax.axis_index("tx")
    count = count_y * count_x
    me = ty * count_x + tx
    height, breadth = fixed_hbm.shape
    knots = count_x * (breadth // SPACE)
    cells_y, cells_x = height // SPACE, breadth // SPACE

    def peer(step):
        other = lax.rem(me + step, count)
        return (other // count_x, lax.rem(other, count_x))

    def for_peers(act):
        if count <= 64:
            for step in range(1, count):
                act(peer(step))
        else:

            def body(step, carry):
                act(peer(step))
                return carry

            lax.fori_loop(1, count, body, 0)

    tissue_load = pltpu.make_async_copy(tissue_hbm, tissue_ref, load_sem.at[2])
    tissue_load.start()
    loads = []
    for image, ref in enumerate((fixed_hbm, moving_hbm)):
        loads.append(
            pltpu.make_async_copy(ref, mid.at[image, RIM : RIM + height], load_sem.at[image])
        )
        loads[image].start()

    low, high = slice(0, RIM), slice(RIM + height, 2 * RIM + height)

    @pl.when(ty == 0)
    def _():
        for ref in (mid, left_side, right_side):
            ref[:, low] = jnp.zeros((2, RIM, ref.shape[2]), F32)

    @pl.when(ty == count_y - 1)
    def _():
        for ref in (mid, left_side, right_side):
            ref[:, high] = jnp.zeros((2, RIM, ref.shape[2]), F32)

    @pl.when(tx == 0)
    def _():
        left_side[...] = jnp.zeros(left_side.shape, F32)

    @pl.when(tx == count_x - 1)
    def _():
        right_side[...] = jnp.zeros(right_side.shape, F32)

    tiles_box[...] = jnp.zeros(tiles_box.shape, F32)

    barrier = pltpu.get_barrier_semaphore()
    near = 2 <= count_y <= 8 and 2 <= count_x <= 4
    greeted = [(y, x) for y in range(-1, 2) for x in range(-1, 2) if (y, x) != (0, 0)]
    if count_y == 8:
        greeted += [(1 - count_y, 0), (count_y - 1, 0)]

    def here(by_y, by_x):
        to_y, to_x = ty + by_y, tx + by_x
        return (to_y >= 0) & (to_y < count_y) & (to_x >= 0) & (to_x < count_x)

    def greet(device):
        pl.semaphore_signal(barrier, 1, device_id=device, device_id_type=MESH)

    if near:
        for by_y, by_x in greeted:

            @pl.when(here(by_y, by_x))
            def _():
                greet((ty + by_y, tx + by_x))

    else:
        for_peers(greet)

    lane = lax.broadcasted_iota(jnp.int32, (8, breadth), 1)
    for k in range(REACH_X):
        fine_cols[k] = bspline(lane.astype(F32) / SPACE - (k - 1.0))
        coarse_cols[k] = bspline((lane.astype(F32) + 0.5) / SPACE - (k - 1.0))
    row = lax.broadcasted_iota(jnp.int32, (height, 128), 0).astype(F32)
    coarse_row = lax.broadcasted_iota(jnp.int32, (height // 2, 128), 0).astype(F32)
    for r in range(REACH_Y):
        fine_rows[r] = bspline(row / SPACE - (r - 1.0))
        coarse_rows[r] = bspline((2.0 * coarse_row + 0.5) / SPACE - (r - 1.0))
    even = lax.rem(lane, 2) == 0
    tissue_load.wait()
    for i in range(cells_y):
        line = jnp.zeros((8, breadth), F32)
        for j in range(cells_x):
            value = tissue_ref[i, j].astype(F32)
            inside = (lane >= j * SPACE) & (lane < (j + 1) * SPACE)
            line = jnp.where(inside, value, line)
        half = jnp.where(even, line, 0.0)
        for part in range(SPACE // 8):
            start = i * SPACE + part * 8
            fine_weight[start : start + 8] = line
        for part in range(SPACE // 16):
            start = i * (SPACE // 2) + part * 8
            coarse_weight[start : start + 8] = half

    if near:
        edge_y = jnp.where((ty == 0) | (ty == count_y - 1), 1, 0)
        edge_x = jnp.where((tx == 0) | (tx == count_x - 1), 1, 0)
        greeters = (3 - edge_y) * (3 - edge_x) - 1
        if count_y == 8:
            greeters = greeters + edge_y
        pl.semaphore_wait(barrier, greeters)
    else:
        pl.semaphore_wait(barrier, count - 1)

    def rows_of(travel):
        if travel == 0:
            return slice(0, height), slice(RIM, RIM + height)
        if travel > 0:
            return slice(height - RIM, height), low
        return slice(0, RIM), high

    def landing(travel_y, travel_x):
        ref = mid if travel_x == 0 else (left_side if travel_x > 0 else right_side)
        return ref.at[:, rows_of(travel_y)[1]]

    def exists(travel_y, travel_x):
        to_y, to_x = ty + travel_y, tx + travel_x
        return (to_y >= 0) & (to_y < count_y) & (to_x >= 0) & (to_x < count_x)

    for index, (travel_y, travel_x) in enumerate(travels):

        @pl.when(exists(travel_y, travel_x))
        def _():
            source_rows = rows_of(travel_y)[0]
            if travel_x == 0:
                lanes = slice(0, breadth)
            elif travel_x > 0:
                lanes = slice(breadth - 128, breadth)
            else:
                lanes = slice(0, 128)
            for image, ref in enumerate((fixed_hbm, moving_hbm)):
                pltpu.make_async_remote_copy(
                    src_ref=ref.at[source_rows, lanes],
                    dst_ref=landing(travel_y, travel_x).at[image],
                    send_sem=rim_send.at[index],
                    recv_sem=rim_recv.at[index],
                    device_id=(ty + travel_y, tx + travel_x),
                    device_id_type=MESH,
                ).start()

    for load in loads:
        load.wait()

    for index, (travel_y, travel_x) in enumerate(travels):

        @pl.when(exists(-travel_y, -travel_x))
        def _():
            place = landing(travel_y, travel_x)
            pltpu.make_async_copy(place, place, rim_recv.at[index]).wait()

    tiles = breadth // 128
    side_lane = lax.broadcasted_iota(jnp.int32, (height + 2 * RIM, 128), 1)
    for image in range(2):
        for tile in range(tiles):
            full[image * (tiles + 1) + tile] = mid[image, :, tile * 128 : (tile + 1) * 128]
        full[image * (tiles + 1) + tiles] = jnp.where(
            side_lane < 64, right_side[image], left_side[image]
        )

    def fine_image(image):
        base = image * (tiles + 1)
        return jnp.concatenate(
            [full[base + tile, 8 : height + 24] for tile in range(tiles + 1)], axis=1
        )

    def coarse_image(image):
        base = image * (tiles + 1)
        span = height // 2 + RIM
        summed = jnp.concatenate(
            [
                full[base + tile, pl.ds(0, span, stride=2), :]
                + full[base + tile, pl.ds(1, span, stride=2), :]
                for tile in range(tiles + 1)
            ],
            axis=1,
        )
        return 0.25 * (summed + moved(summed, 0, 1))

    terms_into(
        coarse_image(0), coarse_image(1), 2, 2, fixed_minds, moving_minds, coarse_terms, breadth
    )

    small_lane = lax.broadcasted_iota(jnp.int32, (8, 128), 1)
    small_row = lax.broadcasted_iota(jnp.int32, (8, 128), 0)
    knot = lax.rem(small_lane, SEGMENT)
    knot_x = tx * cells_x - 1 + knot
    knot_y = ty * cells_y - 1 + small_row
    valid = (knot < REACH_X) & (small_row < REACH_Y) & (knot_x >= 0) & (knot_x < knots)
    valid = valid & (knot_y >= 0) & (knot_y < count_y * cells_y)
    own = (small_lane < SET) & (knot >= 1) & (knot <= cells_x)
    own = own & (small_row >= 1) & (small_row <= cells_y)

    def displace(window, rows_ref, cols_ref, number=0):
        fields = []
        for member in range(2):
            line = None
            for k in range(REACH_X):
                at = number * SET + member * SEGMENT + k
                part = window[:, at : at + 1] * cols_ref[k]
                line = part if line is None else line + part
            field = None
            for r in range(REACH_Y):
                weights = jnp.concatenate([rows_ref[r]] * tiles, axis=1)
                part = weights * line[r : r + 1, :]
                field = part if field is None else field + part
            fields.append(field)
        return fields

    def gather_up(pixels, rows_ref, cols_ref, number=0):
        out = jnp.zeros((8, 128), F32)
        for member in range(2):
            lines = []
            for r in range(REACH_Y):
                weights = jnp.concatenate([rows_ref[r]] * tiles, axis=1)
                lines.append(jnp.sum(weights * pixels[member], axis=0, keepdims=True))
            lines.append(jnp.zeros((8 - REACH_Y, breadth), F32))
            line = jnp.concatenate(lines, axis=0)
            for k in range(REACH_X):
                column = jnp.sum(line * cols_ref[k], axis=1, keepdims=True)
                at = number * SET + member * SEGMENT + k
                out = jnp.where(small_lane == at, column, out)
        return out

    def slot_of(by_y, by_x):
        return (by_y + 2) * 3 + by_x + 1

    around = [(y, x) for y in range(-2, 3) for x in range(-1, 2) if (y, x) != (0, 0)]

    def send_tile(turn, tile):
        tiles_box[turn, OWN_SLOT] = tile
        for by_y, by_x in around:

            @pl.when(exists(by_y, by_x))
            def _():
                slot = slot_of(-by_y, -by_x)
                pltpu.make_async_remote_copy(
                    src_ref=tiles_box.at[turn, OWN_SLOT],
                    dst_ref=tiles_box.at[turn, slot],
                    send_sem=tile_send.at[slot],
                    recv_sem=tile_recv.at[turn, slot],
                    device_id=(ty + by_y, tx + by_x),
                    device_id_type=MESH,
                ).start()

    def collect_tiles(turn):
        for by_y, by_x in around:

            @pl.when(exists(by_y, by_x))
            def _():
                slot = slot_of(by_y, by_x)
                place = tiles_box.at[turn, slot]
                pltpu.make_async_copy(place, place, tile_recv.at[turn, slot]).wait()

        window = None
        for by_x in range(-1, 2):
            total = None
            for by_y in range(-2, 3):
                part = tiles_box[turn, slot_of(by_y, by_x)]
                if by_y:
                    part = pltpu.roll(part, (2 * by_y) % 8, 0)
                if by_y == 2:
                    part = jnp.where(small_row >= 4, part, 0.0)
                if by_y == -2:
                    part = jnp.where(small_row < 1, part, 0.0)
                total = part if total is None else total + part
            if by_x:
                total = pltpu.roll(total, (8 * by_x) % 128, 1)
                reached = (knot >= 8) if by_x > 0 else (knot < REACH_X - 8)
                total = jnp.where(reached, total, 0.0)
            window = total if window is None else window + total
        return jnp.where(valid, window, 0.0)

    def send_scalars(turn, row):
        scalar_box[turn, me] = row

        def act(device):
            pltpu.make_async_remote_copy(
                src_ref=scalar_box.at[turn, me],
                dst_ref=scalar_box.at[turn, me],
                send_sem=scalar_send.at[turn],
                recv_sem=scalar_recv.at[turn],
                device_id=device,
                device_id_type=MESH,
            ).start()

        for_peers(act)

    def collect_scalars(turn):
        part = scalar_box.at[turn, 0 : count - 1]
        pltpu.make_async_copy(part, part, scalar_recv.at[turn]).wait()
        row = jnp.sum(scalar_box[turn], axis=0)
        lanes = lax.broadcasted_iota(jnp.int32, (1, 128), 1)
        return [
            jnp.sum(
                jnp.where((lanes >= SET * i) & (lanes < SET * (i + 1)), row, 0.0), keepdims=True
            )
            for i in range(4)
        ]

    def scalars(first, second, dense):
        third = jnp.where(own, second * second, 0.0)
        middle = jnp.where(own, first * second, 0.0)
        lead = jnp.where(own, first * first, 0.0)
        packed = lead + pltpu.roll(middle, SET, 1) + pltpu.roll(third, 2 * SET, 1)
        row = jnp.sum(packed, axis=0, keepdims=True)
        dense = dense + pltpu.roll(dense, 64, 1)
        dense = dense + pltpu.roll(dense, 32, 1)
        lanes = lax.broadcasted_iota(jnp.int32, (1, 128), 1)
        return jnp.where(lanes >= 3 * SET, dense, row)

    def pulled(terms_ref, motion):
        return (
            terms_ref[2] * motion[0] + terms_ref[3] * motion[1],
            terms_ref[3] * motion[0] + terms_ref[4] * motion[1],
        )

    def weighted(weight_ref, pair):
        return [weight_ref[...] * pair[0], weight_ref[...] * pair[1]]

    def density_row(weight_ref, motion, pull):
        dense = weight_ref[...] * (motion[0] * pull[0] + motion[1] * pull[1])
        line = jnp.sum(dense, axis=0, keepdims=True)
        total = line[:, :128]
        for tile in range(1, tiles):
            total = total + line[:, tile * 128 : (tile + 1) * 128]
        return total

    def steps_of(first, middle, third, fourth):
        step = first / middle
        norm = first - 2.0 * step * middle + step * step * third
        curvature = middle - 2.0 * step * third + step * step * fourth
        return step, norm / curvature

    send_tile(
        0,
        gather_up(
            weighted(coarse_weight, (coarse_terms[0], coarse_terms[1])), coarse_rows, coarse_cols
        ),
    )
    terms_into(fine_image(0), fine_image(1), 1, 1, fixed_minds, moving_minds, fine_terms, breadth)
    fine_start = gather_up(
        weighted(fine_weight, (fine_terms[0], fine_terms[1])), fine_rows, fine_cols, 1
    )
    gradient0 = collect_tiles(0)

    motion = displace(gradient0, coarse_rows, coarse_cols)
    part = gather_up(
        weighted(coarse_weight, pulled(coarse_terms, motion)), coarse_rows, coarse_cols
    )
    send_tile(1, part + fine_start)
    fine_motion0 = displace(gradient0, fine_rows, fine_cols)
    fine_part0 = gather_up(
        weighted(fine_weight, pulled(fine_terms, fine_motion0)), fine_rows, fine_cols
    )
    gradient1 = collect_tiles(1)

    motion = displace(gradient1, coarse_rows, coarse_cols)
    dense = density_row(coarse_weight, motion, pulled(coarse_terms, motion))
    send_scalars(0, scalars(gradient0, gradient1, dense))
    fine_motion1 = displace(gradient1, fine_rows, fine_cols)
    fine_part1 = gather_up(
        weighted(fine_weight, pulled(fine_terms, fine_motion1)), fine_rows, fine_cols, 1
    )
    send_tile(2, fine_part0 + fine_part1)
    fine_gradient = pltpu.roll(gradient1, 128 - SET, 1)
    images = collect_tiles(2)
    step0, step1 = steps_of(*collect_scalars(0))
    near, far = -(step0 + step1), step0 * step1
    control = near * gradient0 + far * gradient1
    direction = fine_gradient + near * images + far * pltpu.roll(images, 128 - SET, 1)

    motion2 = displace(direction, fine_rows, fine_cols)
    send_tile(
        3,
        gather_up(weighted(fine_weight, pulled(fine_terms, motion2)), fine_rows, fine_cols),
    )
    field_y = near * fine_motion0[0] + far * fine_motion1[0]
    field_x = near * fine_motion0[1] + far * fine_motion1[1]
    image = collect_tiles(3)

    motion3 = displace(image, fine_rows, fine_cols)
    dense = density_row(fine_weight, motion3, pulled(fine_terms, motion3))
    send_scalars(1, scalars(direction, image, dense))
    step0, step1 = steps_of(*collect_scalars(1))
    near, far = -(step0 + step1), step0 * step1
    control = control + near * direction + far * image
    field_y = field_y + near * motion2[0] + far * motion3[0]
    field_x = field_x + near * motion2[1] + far * motion3[1]
    pull_y, pull_x = pulled(fine_terms, (field_y, field_x))
    mismatch_ref[...] = (
        fine_terms[5]
        + 2.0 * (fine_terms[0] * field_y + fine_terms[1] * field_x)
        + field_y * pull_y
        + field_x * pull_x
    )
    for member in range(2):
        start = member * SEGMENT + 1
        coef_ref[member] = control[1 : 1 + cells_y, start : start + cells_x]

    for index, (travel_y, travel_x) in enumerate(travels):

        @pl.when(exists(travel_y, travel_x))
        def _():
            place = landing(travel_y, travel_x)
            pltpu.make_async_copy(place, place, rim_send.at[index]).wait()

    for by_y, by_x in around:

        @pl.when(exists(by_y, by_x))
        def _():
            slot = slot_of(-by_y, -by_x)
            place = tiles_box.at[:, slot]
            pltpu.make_async_copy(place, place, tile_send.at[slot]).wait()

    for turn in range(2):
        part = scalar_box.at[turn, 0 : count - 1]
        pltpu.make_async_copy(part, part, scalar_send.at[turn]).wait()


def window_pairs(span):
    return [(k, k + d) for d in range(4) for k in range(span - d)]


def split(values):
    high = values.astype(B16)
    return high, (values - high.astype(F32)).astype(B16)


def spline_array(values):
    magnitude = np.abs(values)
    rest = 2.0 - magnitude
    near_part = 2.0 / 3.0 - magnitude**2 + 0.5 * magnitude**3
    far_part = rest**3 / 6.0
    return np.where(magnitude < 1.0, near_part, np.where(magnitude < 2.0, far_part, 0.0))


def split_array(values):
    values = values.astype(np.float32)
    high = values.astype(B16)
    return high, (values - high.astype(np.float32)).astype(B16)


def strided_columns(breadth, factor):
    lane, part = np.arange(128)[None, :], np.arange(PARTS)[:, None]
    if factor == 1:
        column = PARTS * lane + part - 8
        return column, (column >= 0) & (column < breadth)
    column = PARTS * (lane - 64) + part - 6
    return column, (lane >= 64) & (column >= 0) & (column < breadth // 2)


def natural_lane(column, breadth):
    return column if column >= 0 else breadth + 128 + column


def stride_tables(breadth):
    size = breadth + 128
    fine = np.zeros((size, PARTS * 128))
    for place in range(breadth + 16):
        fine[natural_lane(place - 8, breadth), place % PARTS * 128 + place // PARTS] = 1.0
    coarse = np.zeros((2, size, PARTS * 128))
    for image in range(2):
        for place in range(breadth // 2 + 12):
            at = place % PARTS * 128 + image * 64 + place // PARTS
            for side in range(2):
                coarse[image, natural_lane(2 * (place - 6) + side, breadth), at] = 0.25
    back = fine[:breadth].T
    return tuple(table.astype(B16) for table in (fine, coarse[0], coarse[1], back))


def level_tables(height, breadth, factor):
    row_at = factor * np.arange(height // factor) + (factor - 1) / 2.0
    column, taken = strided_columns(breadth, factor)
    col_at = (factor * column + (factor - 1) / 2.0).reshape(-1)
    rows = spline_array(row_at[None, :] / SPACE - (np.arange(REACH_Y)[:, None] - 1.0))
    cols = spline_array(col_at[:, None] / SPACE - (np.arange(REACH_X)[None, :] - 1.0))
    cols = cols * taken.reshape(-1, 1)
    row_pairs = np.zeros((BLOCK, row_at.size))
    for at, (r, other) in enumerate(window_pairs(REACH_Y)):
        row_pairs[at] = rows[r] * rows[other]
    lines = np.zeros((2, BLOCK, row_at.size))
    for member in range(2):
        lines[member, member * REACH_Y : (member + 1) * REACH_Y] = rows
    pairs = window_pairs(REACH_X)
    col_table = np.zeros((4, col_at.size, 128))
    for comp in range(3):
        for at, (k, other) in enumerate(pairs):
            col_table[comp, :, comp * len(pairs) + at] = cols[:, k] * cols[:, other]
    col_table[3, :, 3 * len(pairs) : 3 * len(pairs) + REACH_X] = cols

    def left(table):
        high, low = split_array(table)
        return np.concatenate([high, high, low], axis=1)

    high, low = split_array(col_table.reshape(4 * col_at.size, 128))
    return (
        left(row_pairs),
        np.concatenate([left(lines[0]), left(lines[1])], axis=1),
        np.concatenate([high, low], axis=1),
    )


def assembly_tables(count_y, count_x, cells_y, cells_x):
    knots_y, knots_x = count_y * cells_y, count_x * cells_x
    pairs = window_pairs(REACH_X)
    width = 8 * knots_x
    cols = np.zeros((count_x * 128, 3 * width + 128), np.float32)
    for tx in range(count_x):
        start = (tx % 2 * (count_x // 2) + tx // 2) * 128
        for comp in range(3):
            for at, (k, other) in enumerate(pairs):
                first, second = tx * cells_x - 1 + k, tx * cells_x - 1 + other
                if first < 0 or second >= knots_x:
                    continue
                source, gap = start + comp * len(pairs) + at, other - k
                cols[source, comp * width + (3 + gap) * knots_x + first] = 1.0
                cols[source, comp * width + (3 - gap) * knots_x + second] = 1.0
        for k in range(REACH_X):
            knot = tx * cells_x - 1 + k
            if 0 <= knot < knots_x:
                for group in range(128 // knots_x):
                    cols[start + 3 * len(pairs) + k, 3 * width + group * knots_x + knot] = 1.0
    rows = np.zeros((9 * knots_y, count_y * BLOCK), np.float32)
    for ty in range(count_y):
        for at, (r, other) in enumerate(window_pairs(REACH_Y)):
            first, second = ty * cells_y - 1 + r, ty * cells_y - 1 + other
            if first < 0 or second >= knots_y:
                continue
            rows[(3 + other - r) * knots_y + first, ty * BLOCK + at] = 1.0
            rows[(3 - other + r) * knots_y + second, ty * BLOCK + at] = 1.0
        for member in range(2):
            for r in range(REACH_Y):
                knot = ty * cells_y - 1 + r
                if 0 <= knot < knots_y:
                    rows[(7 + member) * knots_y + knot, ty * BLOCK + member * REACH_Y + r] = 1.0
    return cols.astype(B16), np.concatenate([rows, rows], axis=1).astype(B16)


def dot(left, right):
    return jnp.dot(left, right, preferred_element_type=F32)


def strided(parts, step):
    out = []
    for at in range(PARTS):
        carry, source = divmod(at + step, PARTS)
        part = parts[source]
        out.append(pltpu.roll(part, (-carry) % 128, 1) if carry else part)
    return out


def lowered(parts, step):
    return [pltpu.roll(part, (-step) % part.shape[0], 0) for part in parts] if step else parts


def split_three(values):
    high = values.astype(B16)
    rest = values - high.astype(F32)
    middle = rest.astype(B16)
    return [high, middle, (rest - middle.astype(F32)).astype(B16)]


def boxes_into(parts, boxes_ref):
    rows = parts[0].shape[0]
    turned = {step: strided(parts, step) for step in (2, -2, 4)}
    turned[0] = parts
    total = None
    for index, (offset_y, offset_x) in enumerate(half_offsets):
        other = lowered(turned[offset_x], offset_y)
        square = [(p - q) * (p - q) for p, q in zip(parts, other)]
        lines = [
            p + q + r for p, q, r in zip(square, lowered(square, 1), lowered(square, -1))
        ]
        box = [p + q + r for p, q, r in zip(lines, strided(lines, 1), strided(lines, -1))]
        back = lowered(strided(box, -offset_x) if offset_x else box, -offset_y)
        for at in range(PARTS):
            boxes_ref[2 * index, at, :rows] = box[at]
            boxes_ref[2 * index + 1, at, :rows] = back[at]
        both = [p + q for p, q in zip(box, back)]
        total = both if total is None else [p + q for p, q in zip(total, both)]
    return [-LOG2E / (part / 12.0 + 0.9) for part in total]


def minds_tiled(scale, boxes_ref, minds_ref):
    rows = scale[0].shape[0]
    for index in range(12):
        for at in range(PARTS):
            minds_ref[index, at, :rows] = jnp.exp2(boxes_ref[index, at, :rows] * scale[at])


def sums_into(minds_ref, fixed_of, factor, terms_ref):
    height = terms_ref.shape[1]
    once = 1.0 / (2.0 * factor)
    scales = (once, once, once * once, once * once, once * once, 1.0)
    for start in range(0, height, 8):
        base = 8 + start
        sums = None
        for index in range(12):
            own = [minds_ref[index, at, base : base + 8] for at in range(PARTS)]
            fixed = fixed_of(index, base, own)
            ahead, behind = strided(own, 1), strided(own, -1)
            parts = []
            for at in range(PARTS):
                differ = own[at] - fixed[at]
                slope_y = (
                    minds_ref[index, at, base + 1 : base + 9]
                    - minds_ref[index, at, base - 1 : base + 7]
                )
                slope_x = ahead[at] - behind[at]
                parts += [
                    differ * slope_y,
                    differ * slope_x,
                    slope_y * slope_y,
                    slope_y * slope_x,
                    slope_x * slope_x,
                    differ * differ,
                ]
            sums = parts if sums is None else [a + b for a, b in zip(sums, parts)]
        for at in range(PARTS):
            for term in range(6):
                terms_ref[term, start : start + 8, at * 128 : (at + 1) * 128] = (
                    sums[6 * at + term] * scales[term]
                )


def greeted_by(count_y, count_x, y, x):
    near = {(y + by_y, x + by_x) for by_y, by_x in travels}
    near = {(a, b) for a, b in near if 0 <= a < count_y and 0 <= b < count_x}
    return near | {((y + step) % count_y, x ^ 1) for step in far_greets}


def two_steps_reach(count_y, count_x):
    if count_y < 8 or count_x % 2:
        return False
    every = [(y, x) for y in range(count_y) for x in range(count_x)]
    greeted = {at: greeted_by(count_y, count_x, *at) for at in every}
    for y, x in every:
        known = greeted[y, x].union(*(greeted[at] for at in greeted[y, x]))
        if not {at for at in every if (at[1] - x) % 2 == 0 and at != (y, x)} <= known:
            return False
    return True


def gathered_kernel(
    count_y,
    count_x,
    tissue_hbm,
    fixed_hbm,
    moving_hbm,
    *rest,
):
    tables_hbm, rest = rest[:12], rest[12:]
    coef_ref, mismatch_ref = rest[:2]
    tables, rest = rest[2:14], rest[14:]
    (
        mid,
        left_side,
        right_side,
        full,
        fixed_boxes,
        boxes_ref,
        minds_ref,
        fixed_minds,
        fine_terms,
        coarse_terms,
        fine_weight,
        coarse_weight,
        tissue_ref,
        boxes,
        stencils,
        last_rows,
        last_cols,
        natural,
        load_sem,
        table_sem,
        rim_send,
        rim_recv,
        block_send,
        block_recv,
        relay_send,
        relay_recv,
        ready,
    ) = rest
    fine_tables, coarse_tables, (gather_cols, gather_rows) = tables[:3], tables[3:6], tables[6:8]
    fine_stride, fixed_stride, moving_stride, stride_back = tables[8:]
    ty = lax.axis_index("ty")
    tx = lax.axis_index("tx")
    count = count_y * count_x
    half = count // 2
    me = ty * count_x + tx
    parity = lax.rem(tx, 2)
    place = ty * (count_x // 2) + tx // 2
    sibling = (ty, tx + 1 - 2 * parity)
    height, breadth = fixed_hbm.shape
    cells_y, cells_x = height // SPACE, breadth // SPACE
    knots_y, knots_x = count_y * cells_y, count_x * cells_x
    width = 8 * knots_x
    used = len(window_pairs(REACH_Y))
    wide = PARTS * 128

    def exists(by_y, by_x):
        to_y, to_x = ty + by_y, tx + by_x
        return (to_y >= 0) & (to_y < count_y) & (to_x >= 0) & (to_x < count_x)

    few = two_steps_reach(count_y, count_x)

    def greet_far(semaphore):
        for step in far_greets:
            other = (lax.rem(ty + step + count_y, count_y), sibling[1])
            pl.semaphore_signal(semaphore, 1, device_id=other, device_id_type=MESH)

    barrier = pltpu.get_barrier_semaphore()
    if few:
        for by_y, by_x in travels:

            @pl.when(exists(by_y, by_x))
            def _():
                pl.semaphore_signal(
                    barrier, 1, device_id=(ty + by_y, tx + by_x), device_id_type=MESH
                )

        greet_far(barrier)
        edge_y = jnp.where((ty == 0) | (ty == count_y - 1), 1, 0)
        edge_x = jnp.where((tx == 0) | (tx == count_x - 1), 1, 0)
        greeters = (3 - edge_y) * (3 - edge_x) - 1 + len(far_greets)
    else:
        for step in range(1, count):
            other = lax.rem(me + step, count)
            other = (other // count_x, lax.rem(other, count_x))
            pl.semaphore_signal(barrier, 1, device_id=other, device_id_type=MESH)
        greeters = count - 1

    tissue_load = pltpu.make_async_copy(tissue_hbm, tissue_ref, load_sem.at[2])
    tissue_load.start()
    loads = []
    for image, ref in enumerate((fixed_hbm, moving_hbm)):
        loads.append(
            pltpu.make_async_copy(ref, mid.at[image, RIM : RIM + height], load_sem.at[image])
        )
        loads[image].start()

    boxes[:, :, :, used:] = jnp.zeros((2, 2, half, BLOCK - used, 128), F32)
    low, high = slice(0, RIM), slice(RIM + height, 2 * RIM + height)

    @pl.when(ty == 0)
    def _():
        for ref in (mid, left_side, right_side):
            ref[:, low] = jnp.zeros((2, RIM, ref.shape[2]), F32)

    @pl.when(ty == count_y - 1)
    def _():
        for ref in (mid, left_side, right_side):
            ref[:, high] = jnp.zeros((2, RIM, ref.shape[2]), F32)

    @pl.when(tx == 0)
    def _():
        left_side[...] = jnp.zeros(left_side.shape, F32)

    @pl.when(tx == count_x - 1)
    def _():
        right_side[...] = jnp.zeros(right_side.shape, F32)

    lane = lax.broadcasted_iota(jnp.int32, (8, 128), 1)
    tissue_load.wait()
    for i in range(cells_y):
        for at in range(PARTS):
            fine_at = PARTS * lane + at - 8
            coarse_at = jnp.where(lane < 64, -1, 2 * (PARTS * (lane - 64) + at - 6))
            fine_line = jnp.zeros((8, 128), F32)
            coarse_line = jnp.zeros((8, 128), F32)
            for j in range(cells_x):
                value = tissue_ref[i, j].astype(F32)
                low_x, high_x = j * SPACE, (j + 1) * SPACE
                inside = (fine_at >= low_x) & (fine_at < high_x)
                fine_line = jnp.where(inside, value, fine_line)
                inside = (coarse_at >= low_x) & (coarse_at < high_x)
                coarse_line = jnp.where(inside, value, coarse_line)
            lanes = slice(at * 128, (at + 1) * 128)
            for part in range(SPACE // 8):
                start = i * SPACE + part * 8
                fine_weight[start : start + 8, lanes] = fine_line
            for part in range(SPACE // 16):
                start = i * (SPACE // 2) + part * 8
                coarse_weight[start : start + 8, lanes] = coarse_line

    def rows_of(travel):
        if travel == 0:
            return slice(0, height), slice(RIM, RIM + height)
        if travel > 0:
            return slice(height - RIM, height), low
        return slice(0, RIM), high

    def landing(travel_y, travel_x):
        ref = mid if travel_x == 0 else (left_side if travel_x > 0 else right_side)
        return ref.at[:, rows_of(travel_y)[1]]

    for load in loads:
        load.wait()
    pl.semaphore_wait(barrier, greeters)

    for index, (travel_y, travel_x) in sorted(enumerate(travels), key=lambda item: -abs(item[1][1])):

        @pl.when(exists(travel_y, travel_x))
        def _():
            source_rows = rows_of(travel_y)[0]
            if travel_x == 0:
                lanes = slice(0, breadth)
            elif travel_x > 0:
                lanes = slice(breadth - 128, breadth)
            else:
                lanes = slice(0, 128)
            source_rows = slice(source_rows.start + RIM, source_rows.stop + RIM)
            pltpu.make_async_remote_copy(
                src_ref=mid.at[:, source_rows, lanes],
                dst_ref=landing(travel_y, travel_x),
                send_sem=rim_send.at[index],
                recv_sem=rim_recv.at[index],
                device_id=(ty + travel_y, tx + travel_x),
                device_id_type=MESH,
            ).start()

    if few:
        greet_far(ready)
    table_loads = []
    for index, (source, target) in enumerate(zip(tables_hbm, tables)):
        table_loads.append(pltpu.make_async_copy(source, target, table_sem.at[index]))
        table_loads[index].start()

    knot = lax.broadcasted_iota(jnp.int32, (128, breadth), 0)
    at_x = lax.broadcasted_iota(jnp.int32, (128, breadth), 1).astype(F32) / SPACE
    last = bspline(at_x - (knot - tx * cells_x).astype(F32))
    last_high, last_low = split(jnp.where(knot < knots_x, last, 0.0))
    last_cols[:, :breadth] = last_high
    last_cols[:, breadth:] = last_low
    knot = lax.broadcasted_iota(jnp.int32, (height, 128), 1)
    at_y = lax.broadcasted_iota(jnp.int32, (height, 128), 0).astype(F32) / SPACE
    third = knot // knots_y
    last_high, last_low = split(
        bspline(at_y - (lax.rem(knot, knots_y) - ty * cells_y).astype(F32))
    )
    kept = jnp.where(third < 2, last_high.astype(F32), last_low.astype(F32))
    last_rows[...] = jnp.where(third < 3, kept, 0.0).astype(B16)

    for index, (travel_y, travel_x) in enumerate(travels):

        @pl.when(exists(-travel_y, -travel_x))
        def _():
            spot = landing(travel_y, travel_x)
            pltpu.make_async_copy(spot, spot, rim_recv.at[index]).wait()

    tiles = breadth // 128
    side_lane = lax.broadcasted_iota(jnp.int32, (height + 2 * RIM, 128), 1)
    for image in range(2):
        for tile in range(tiles):
            full[image * (tiles + 1) + tile] = mid[image, :, tile * 128 : (tile + 1) * 128]
        full[image * (tiles + 1) + tiles] = jnp.where(
            side_lane < 64, right_side[image], left_side[image]
        )

    def fine_image(image):
        base = image * (tiles + 1)
        return jnp.concatenate(
            [full[base + tile, 8 : height + 24] for tile in range(tiles + 1)], axis=1
        )

    def coarse_image(image):
        base = image * (tiles + 1)
        span = height // 2 + RIM
        return jnp.concatenate(
            [
                full[base + tile, pl.ds(0, span, stride=2), :]
                + full[base + tile, pl.ds(1, span, stride=2), :]
                for tile in range(tiles + 1)
            ],
            axis=1,
        )

    def parts_of(values):
        return [values[:, at * 128 : (at + 1) * 128] for at in range(PARTS)]

    def coarse_terms_into():
        pair = None
        for image, table in enumerate((fixed_stride, moving_stride)):
            pieces = split_three(coarse_image(image))
            out = dot(jnp.concatenate(pieces, axis=0), table[...])
            rows = pieces[0].shape[0]
            out = out[:rows] + out[rows : 2 * rows] + out[2 * rows :]
            pair = out if pair is None else pair + out
        minds_tiled(boxes_into(parts_of(pair), boxes_ref), boxes_ref, minds_ref)

        def fixed_of(index, base, own):
            return [pltpu.roll(part, 64, 1) for part in own]

        sums_into(minds_ref, fixed_of, 2, coarse_terms)

    def fine_terms_into():
        pieces = split_three(jnp.concatenate([fine_image(0), fine_image(1)], axis=0))
        out = dot(jnp.concatenate(pieces, axis=0), fine_stride[...])
        rows = height + 16
        both = out[: 2 * rows] + out[2 * rows : 4 * rows] + out[4 * rows :]
        scale = boxes_into(parts_of(both[:rows]), fixed_boxes)
        for at in range(PARTS):
            fixed_minds[:, at * 128 : (at + 1) * 128] = scale[at][8 : 8 + height]
        minds_tiled(boxes_into(parts_of(both[rows:]), boxes_ref), boxes_ref, minds_ref)

        def fixed_of(index, base, own):
            return [
                jnp.exp2(
                    fixed_boxes[index, at, base : base + 8]
                    * fixed_minds[base - 8 : base, at * 128 : (at + 1) * 128]
                )
                for at in range(PARTS)
            ]

        sums_into(minds_ref, fixed_of, 1, fine_terms)

    def block_of(terms_ref, weight_ref, level):
        row_pairs, row_lines, col_table = level
        weight = weight_ref[...]
        upper, lower = split(
            jnp.concatenate([weight * terms_ref[index] for index in (2, 3, 4)], axis=1)
        )
        pairs = dot(row_pairs[...], jnp.concatenate([upper, lower, upper], axis=0))
        stack = []
        for member in range(2):
            upper, lower = split(weight * terms_ref[member])
            stack += [upper, lower, upper]
        lines = dot(row_lines[...], jnp.concatenate(stack, axis=0))
        upper, lower = split(jnp.concatenate([pairs, lines], axis=1))
        out = dot(jnp.concatenate([upper, lower], axis=0), col_table[...])
        return out[:BLOCK, :128] + out[BLOCK:, :128] + out[:BLOCK, 128:]

    def send_block(level, block):
        boxes[level, parity, place, 0:used] = block[:used]
        order = [(a, b) for a in range(count_y) for b in range(count_x // 2) if a + b]
        for step_y, step_x in sorted(order, key=lambda p: abs(p[0] - count_y // 2) - p[1]):
            if True:
                to_y = lax.rem(ty + step_y, count_y)
                to_x = 2 * lax.rem(tx // 2 + step_x, count_x // 2) + parity
                pltpu.make_async_remote_copy(
                    src_ref=boxes.at[level, parity, place, 0:used],
                    dst_ref=boxes.at[level, parity, place, 0:used],
                    send_sem=block_send.at[level],
                    recv_sem=block_recv.at[level],
                    device_id=(to_y, to_x),
                    device_id_type=MESH,
                ).start()

    def relay_of(level):
        return pltpu.make_async_remote_copy(
            src_ref=boxes.at[level, parity, :, 0:used],
            dst_ref=boxes.at[level, parity, :, 0:used],
            send_sem=relay_send.at[level],
            recv_sem=relay_recv.at[level],
            device_id=sibling,
            device_id_type=MESH,
        )

    def columns_of(level, side):
        across = count_x // 2
        columns = [
            jnp.concatenate(
                [boxes[level, side, to_y * across + to_x] for to_y in range(count_y)], axis=0
            )
            for to_x in range(across)
        ]
        upper, lower = split(jnp.concatenate(columns, axis=1))
        lines = pl.ds(pl.multiple_of(side * (across * 128), 128), across * 128)
        placed = dot(gather_rows[...], jnp.concatenate([upper, lower], axis=0))
        out = dot(jnp.concatenate(split(placed), axis=0), gather_cols[lines])
        return out[: placed.shape[0]] + out[placed.shape[0] :]

    def relay(level):
        part = boxes.at[level, 0, 0 : half - 1, 0:used]
        pltpu.make_async_copy(part, part, block_recv.at[level]).wait()
        relay_of(level).start()

    def assemble(level, own):
        spot = boxes.at[level, 1 - parity, :, 0:used]
        pltpu.make_async_copy(spot, spot, relay_recv.at[level]).wait()
        stencils[level] = own + columns_of(level, 1 - parity)

    group = lax.broadcasted_iota(jnp.int32, (knots_y, 128), 1) // knots_x

    def spread(values):
        halves = []
        for start in (-3, 1):
            out = None
            for index in range(4):
                gap = start + index
                rolled = pltpu.roll(values, (-gap) % 128, 1) if gap else values
                out = rolled if out is None else jnp.where(group >= index, rolled, out)
            halves.append(out)
        return halves

    def start_of(level):
        return [
            stencils[level, (7 + member) * knots_y : (8 + member) * knots_y, 3 * width :]
            for member in range(2)
        ]

    def pull(level, spreads):
        sums = [None, None]
        for gap in range(-3, 4):
            at = (gap + 3) * knots_y
            for source in range(2):
                for part in range(2):
                    shifted = spreads[source][part]
                    if gap:
                        shifted = pltpu.roll(shifted, (-gap) % knots_y, 0)
                    for member in range(2):
                        lanes = (member + source) * width + part * 128
                        term = stencils[level, at : at + knots_y, lanes : lanes + 128] * shifted
                        old = sums[member]
                        sums[member] = term if old is None else old + term
        out = []
        for total in sums:
            total = total + pltpu.roll(total, 64, 1)
            out.append(total + pltpu.roll(total, 32, 1))
        return out

    def inner(first, second):
        return jnp.sum(first[0] * second[0] + first[1] * second[1], keepdims=True)

    def descend(level, control, gradient):
        image = pull(level, [spread(values) for values in gradient])
        step = inner(gradient, gradient) / inner(gradient, image)
        control = [c - step * g for c, g in zip(control, gradient)]
        return control, [g - step * i for g, i in zip(gradient, image)]

    for load in table_loads:
        load.wait()
    coarse_terms_into()
    coarse_block = block_of(coarse_terms, coarse_weight, coarse_tables)
    if few:
        pl.semaphore_wait(ready, len(far_greets))
    send_block(0, coarse_block)
    fine_terms_into()
    send_block(1, block_of(fine_terms, fine_weight, fine_tables))

    for term in range(6):
        pieces = split_three(fine_terms[term])
        out = dot(jnp.concatenate(pieces, axis=0), stride_back[...])
        natural[term] = out[:height] + out[height : 2 * height] + out[2 * height :]

    relay(0)
    assemble(0, columns_of(0, parity))
    control = [jnp.zeros((knots_y, 128), F32)] * 2
    control, gradient = descend(0, control, start_of(0))
    relay(1)
    fine_own = columns_of(1, parity)
    control, _ = descend(0, control, gradient)
    spreads = [spread(values) for values in control]
    assemble(1, fine_own)
    gradient = [b + i for b, i in zip(start_of(1), pull(1, spreads))]
    control, gradient = descend(1, control, gradient)
    control, _ = descend(1, control, gradient)

    upper, lower = split(jnp.concatenate(control, axis=0))
    rows = 2 * knots_y
    out = dot(jnp.concatenate([upper, lower], axis=0), last_cols[...])
    lines = out[:rows, :breadth] + out[rows:, :breadth] + out[:rows, breadth:]
    upper, lower = split(jnp.concatenate([lines[:knots_y], lines[knots_y:]], axis=1))
    blank = jnp.zeros((128 - 3 * knots_y, 2 * breadth), B16)
    field = dot(last_rows[...], jnp.concatenate([upper, lower, upper, blank], axis=0))
    field_y, field_x = field[:, :breadth], field[:, breadth:]
    pull_y = natural[2] * field_y + natural[3] * field_x
    pull_x = natural[3] * field_y + natural[4] * field_x
    mismatch_ref[...] = (
        natural[5]
        + 2.0 * (natural[0] * field_y + natural[1] * field_x)
        + field_y * pull_y
        + field_x * pull_x
    )
    for member in range(2):
        own = pltpu.roll(control[member], lax.rem(128 - cells_x * tx, 128), 1)
        own = pltpu.roll(own, lax.rem(knots_y - cells_y * ty, knots_y), 0)
        coef_ref[member] = own[:cells_y, :cells_x]

    for index, (travel_y, travel_x) in enumerate(travels):

        @pl.when(exists(travel_y, travel_x))
        def _():
            spot = landing(travel_y, travel_x)
            pltpu.make_async_copy(spot, spot, rim_send.at[index]).wait()

    for level in range(2):
        part = boxes.at[level, 0, 0 : half - 1, 0:used]
        pltpu.make_async_copy(part, part, block_send.at[level]).wait()
        relay_of(level).wait_send()


def spread_call(count_y, count_x, tissue, fixed_image, moving_image):
    height, breadth = fixed_image.shape
    cells_y, cells_x = height // SPACE, breadth // SPACE
    count = count_y * count_x
    tall, full_lanes = height + 2 * RIM, breadth + 128
    vmem = pltpu.VMEM
    scratch = [
        vmem((2, tall, breadth), F32),
        vmem((2, tall, 128), F32),
        vmem((2, tall, 128), F32),
        vmem((2 * (breadth // 128 + 1), tall, 128), F32),
        vmem((12, height + 16, full_lanes), F32),
        vmem((12, height + 16, full_lanes), F32),
        vmem((6, height, breadth), F32),
        vmem((6, height // 2, breadth), F32),
        vmem((height, breadth), F32),
        vmem((height // 2, breadth), F32),
        vmem((REACH_Y, height, 128), F32),
        vmem((REACH_Y, height // 2, 128), F32),
        vmem((REACH_X, 8, breadth), F32),
        vmem((REACH_X, 8, breadth), F32),
        pltpu.SMEM((cells_y, cells_x), jnp.int32),
        vmem((4, 15, 8, 128), F32),
        vmem((2, count, 1, 128), F32),
        pltpu.SemaphoreType.DMA((3,)),
        pltpu.SemaphoreType.DMA((8,)),
        pltpu.SemaphoreType.DMA((8,)),
        pltpu.SemaphoreType.DMA((15,)),
        pltpu.SemaphoreType.DMA((4, 15)),
        pltpu.SemaphoreType.DMA((2,)),
        pltpu.SemaphoreType.DMA((2,)),
    ]
    return pl.pallas_call(
        functools.partial(spread_kernel, count_y, count_x),
        out_shape=(
            jax.ShapeDtypeStruct((2, cells_y, cells_x), F32),
            jax.ShapeDtypeStruct((height, breadth), F32),
        ),
        in_specs=[
            pl.BlockSpec(memory_space=pltpu.HBM),
            pl.BlockSpec(memory_space=pltpu.HBM),
            pl.BlockSpec(memory_space=pltpu.HBM),
        ],
        out_specs=(
            pl.BlockSpec(memory_space=pltpu.VMEM),
            pl.BlockSpec(memory_space=pltpu.VMEM),
        ),
        scratch_shapes=scratch,
        compiler_params=pltpu.CompilerParams(
            collective_id=0, has_side_effects=True, vmem_limit_bytes=16 * 1024 * 1024
        ),
    )(tissue, fixed_image, moving_image)


def closing(coef_in, mismatch_in, coef_out, mismatch_out, sem):
    loads = [
        pltpu.make_async_copy(mismatch_in, mismatch_out, sem.at[0]),
        pltpu.make_async_copy(coef_in, coef_out, sem.at[1]),
    ]
    for load in loads:
        load.start()
    for load in loads:
        load.wait()


def gathered_call(count_y, count_x, tissue, fixed_image, moving_image):
    height, breadth = fixed_image.shape
    cells_y, cells_x = height // SPACE, breadth // SPACE
    count = count_y * count_x
    tall, wide = height + 2 * RIM, PARTS * 128
    vmem, dma = pltpu.VMEM, pltpu.SemaphoreType.DMA
    tables = (
        level_tables(height, breadth, 1)
        + level_tables(height, breadth, 2)
        + assembly_tables(count_y, count_x, cells_y, cells_x)
        + stride_tables(breadth)
    )
    scratch = [vmem(table.shape, B16) for table in tables] + [
        vmem((2, tall, breadth), F32),
        vmem((2, tall, 128), F32),
        vmem((2, tall, 128), F32),
        vmem((2 * (breadth // 128 + 1), tall, 128), F32),
        vmem((12, PARTS, height + 16, 128), F32),
        vmem((12, PARTS, height + 16, 128), F32),
        vmem((12, PARTS, height + 16, 128), F32),
        vmem((height, wide), F32),
        vmem((6, height, wide), F32),
        vmem((6, height // 2, wide), F32),
        vmem((height, wide), F32),
        vmem((height // 2, wide), F32),
        pltpu.SMEM((cells_y, cells_x), jnp.int32),
        vmem((2, 2, count // 2, BLOCK, 128), F32),
        vmem((2, tables[7].shape[0], tables[6].shape[1]), F32),
        vmem((height, 128), B16),
        vmem((128, 2 * breadth), B16),
        vmem((6, height, breadth), F32),
        dma((3,)),
        dma((12,)),
        dma((8,)),
        dma((8,)),
        dma((2,)),
        dma((2,)),
        dma((2,)),
        dma((2,)),
        pltpu.SemaphoreType.REGULAR,
    ]
    held = [
        pltpu.with_memory_space_constraint(jnp.asarray(table), pltpu.HBM) for table in tables
    ]
    return pl.pallas_call(
        functools.partial(gathered_kernel, count_y, count_x),
        out_shape=(
            jax.ShapeDtypeStruct((2, cells_y, cells_x), F32),
            jax.ShapeDtypeStruct((height, breadth), F32),
        ),
        in_specs=[pl.BlockSpec(memory_space=pltpu.HBM)] * 15,
        out_specs=(
            pl.BlockSpec(memory_space=pltpu.VMEM),
            pl.BlockSpec(memory_space=pltpu.VMEM),
        ),
        scratch_shapes=scratch,
        compiler_params=pltpu.CompilerParams(
            collective_id=1, has_side_effects=True, vmem_limit_bytes=32 * 1024 * 1024
        ),
    )(tissue, fixed_image, moving_image, *held)


def shards(count_y, count_x, fixed_image, moving_image, tissue):
    held = [pltpu.with_memory_space_constraint(x, pltpu.HBM) for x in (tissue, fixed_image, moving_image)]
    height, breadth = fixed_image.shape
    fits = height == 2 * SPACE and breadth == 8 * SPACE and count_x % 2 == 0
    fits = fits and count_x * (breadth // SPACE) == 32 and count_y * count_x <= LARGEST
    call = gathered_call if fits else spread_call
    coef, mismatch = call(count_y, count_x, *held)
    return pl.pallas_call(
        closing,
        out_shape=(
            jax.ShapeDtypeStruct(coef.shape, F32),
            jax.ShapeDtypeStruct(mismatch.shape, F32),
        ),
        in_specs=[pl.BlockSpec(memory_space=pl.ANY)] * 2,
        out_specs=(pl.BlockSpec(memory_space=pltpu.HBM),) * 2,
        scratch_shapes=[pltpu.SemaphoreType.DMA((2,))],
        compiler_params=pltpu.CompilerParams(vmem_limit_bytes=4 * 1024 * 1024),
    )(coef, mismatch)


def solution(mesh):
    placed = (P("ty", "tx"), P("ty", "tx"), P("ty", "tx"))
    return jax.shard_map(
        functools.partial(shards, mesh.shape["ty"], mesh.shape["tx"]),
        mesh=mesh,
        in_specs=placed,
        out_specs=(P(None, "ty", "tx"), P("ty", "tx")),
        check_vma=False,
    )
```

```python
import functools

import jax
import jax.numpy as jnp
import numpy as np
from jax import lax
from jax.experimental import pallas as pl
from jax.experimental.pallas import tpu as pltpu
from jax.sharding import PartitionSpec as P

SPACE = 32
REACH_Y = 5
REACH_X = 11
RIM = 16
SEGMENT = 16
SET = 32
OWN_SLOT = 7
MESH = pl.DeviceIdType.MESH
F32 = jnp.float32
B16 = jnp.bfloat16
BLOCK = 16
PARTS = 3
LOG2E = 1.4426950408889634
LARGEST = 64

half_offsets = ((0, 2), (2, 0), (2, 2), (2, -2), (0, 4), (4, 0))
far_greets = (2, -2, 4)
travels = ((-1, 0), (1, 0), (0, -1), (0, 1), (-1, -1), (-1, 1), (1, -1), (1, 1))


def bspline(values):
    magnitude = jnp.abs(values)
    near_part = 2.0 / 3.0 - magnitude * magnitude + 0.5 * magnitude * magnitude * magnitude
    rest = 2.0 - magnitude
    far_part = rest * rest * rest / 6.0
    return jnp.where(magnitude < 1.0, near_part, jnp.where(magnitude < 2.0, far_part, 0.0))


def moved(values, by_y, by_x):
    rows, lanes = values.shape
    if by_x:
        values = pltpu.roll(values, (-by_x) % lanes, 1)
    if by_y:
        values = pltpu.roll(values, (-by_y) % rows, 0)
    return values


def minds_into(image, lane_step, out_ref):
    total = None
    for index, (offset_y, offset_x) in enumerate(half_offsets):
        gap = image - moved(image, offset_y, lane_step * offset_x)
        square = gap * gap
        rows = square + moved(square, 1, 0) + moved(square, -1, 0)
        box = rows + moved(rows, 0, lane_step) + moved(rows, 0, -lane_step)
        other = moved(box, -offset_y, -lane_step * offset_x)
        out_ref[2 * index, : image.shape[0]] = box
        out_ref[2 * index + 1, : image.shape[0]] = other
        both = box + other
        total = both if total is None else total + both
    return -1.0 / (total / 12.0 + 0.9)


def terms_into(fixed, moving, lane_step, factor, fixed_ref, moving_ref, terms_ref, wide):
    rows = fixed.shape[0]
    height = rows - 16
    fixed_scale = minds_into(fixed, lane_step, fixed_ref)[8 : 8 + height, :wide]
    moving_scale = minds_into(moving, lane_step, moving_ref)
    sums = None
    for index in range(12):
        fixed_mind = jnp.exp(fixed_ref[index, 8 : 8 + height, :wide] * fixed_scale)
        mind = jnp.exp(moving_ref[index, :rows] * moving_scale)
        differ = mind[8 : 8 + height, :wide] - fixed_mind
        slope_y = moved(mind[:, :wide], 1, 0) - moved(mind[:, :wide], -1, 0)
        slope_y = slope_y[8 : 8 + height]
        own = mind[8 : 8 + height]
        slope_x = (moved(own, 0, lane_step) - moved(own, 0, -lane_step))[:, :wide]
        parts = (
            differ * slope_y,
            differ * slope_x,
            slope_y * slope_y,
            slope_y * slope_x,
            slope_x * slope_x,
            differ * differ,
        )
        sums = parts if sums is None else tuple(a + b for a, b in zip(sums, parts))
    once = 1.0 / (2.0 * factor)
    scales = (once, once, once * once, once * once, once * once, 1.0)
    for index in range(6):
        terms_ref[index] = sums[index] * scales[index]


def spread_kernel(
    count_y,
    count_x,
    tissue_hbm,
    fixed_hbm,
    moving_hbm,
    coef_ref,
    mismatch_ref,
    mid,
    left_side,
    right_side,
    full,
    fixed_minds,
    moving_minds,
    fine_terms,
    coarse_terms,
    fine_weight,
    coarse_weight,
    fine_rows,
    coarse_rows,
    fine_cols,
    coarse_cols,
    tissue_ref,
    tiles_box,
    scalar_box,
    load_sem,
    rim_send,
    rim_recv,
    tile_send,
    tile_recv,
    scalar_send,
    scalar_recv,
):
    ty = lax.axis_index("ty")
    tx = lax.axis_index("tx")
    count = count_y * count_x
    me = ty * count_x + tx
    height, breadth = fixed_hbm.shape
    knots = count_x * (breadth // SPACE)
    cells_y, cells_x = height // SPACE, breadth // SPACE

    def peer(step):
        other = lax.rem(me + step, count)
        return (other // count_x, lax.rem(other, count_x))

    def for_peers(act):
        if count <= 64:
            for step in range(1, count):
                act(peer(step))
        else:

            def body(step, carry):
                act(peer(step))
                return carry

            lax.fori_loop(1, count, body, 0)

    tissue_load = pltpu.make_async_copy(tissue_hbm, tissue_ref, load_sem.at[2])
    tissue_load.start()
    loads = []
    for image, ref in enumerate((fixed_hbm, moving_hbm)):
        loads.append(
            pltpu.make_async_copy(ref, mid.at[image, RIM : RIM + height], load_sem.at[image])
        )
        loads[image].start()

    low, high = slice(0, RIM), slice(RIM + height, 2 * RIM + height)

    @pl.when(ty == 0)
    def _():
        for ref in (mid, left_side, right_side):
            ref[:, low] = jnp.zeros((2, RIM, ref.shape[2]), F32)

    @pl.when(ty == count_y - 1)
    def _():
        for ref in (mid, left_side, right_side):
            ref[:, high] = jnp.zeros((2, RIM, ref.shape[2]), F32)

    @pl.when(tx == 0)
    def _():
        left_side[...] = jnp.zeros(left_side.shape, F32)

    @pl.when(tx == count_x - 1)
    def _():
        right_side[...] = jnp.zeros(right_side.shape, F32)

    tiles_box[...] = jnp.zeros(tiles_box.shape, F32)

    barrier = pltpu.get_barrier_semaphore()
    near = 2 <= count_y <= 8 and 2 <= count_x <= 4
    greeted = [(y, x) for y in range(-1, 2) for x in range(-1, 2) if (y, x) != (0, 0)]
    if count_y == 8:
        greeted += [(1 - count_y, 0), (count_y - 1, 0)]

    def here(by_y, by_x):
        to_y, to_x = ty + by_y, tx + by_x
        return (to_y >= 0) & (to_y < count_y) & (to_x >= 0) & (to_x < count_x)

    def greet(device):
        pl.semaphore_signal(barrier, 1, device_id=device, device_id_type=MESH)

    if near:
        for by_y, by_x in greeted:

            @pl.when(here(by_y, by_x))
            def _():
                greet((ty + by_y, tx + by_x))

    else:
        for_peers(greet)

    lane = lax.broadcasted_iota(jnp.int32, (8, breadth), 1)
    for k in range(REACH_X):
        fine_cols[k] = bspline(lane.astype(F32) / SPACE - (k - 1.0))
        coarse_cols[k] = bspline((lane.astype(F32) + 0.5) / SPACE - (k - 1.0))
    row = lax.broadcasted_iota(jnp.int32, (height, 128), 0).astype(F32)
    coarse_row = lax.broadcasted_iota(jnp.int32, (height // 2, 128), 0).astype(F32)
    for r in range(REACH_Y):
        fine_rows[r] = bspline(row / SPACE - (r - 1.0))
        coarse_rows[r] = bspline((2.0 * coarse_row + 0.5) / SPACE - (r - 1.0))
    even = lax.rem(lane, 2) == 0
    tissue_load.wait()
    for i in range(cells_y):
        line = jnp.zeros((8, breadth), F32)
        for j in range(cells_x):
            value = tissue_ref[i, j].astype(F32)
            inside = (lane >= j * SPACE) & (lane < (j + 1) * SPACE)
            line = jnp.where(inside, value, line)
        half = jnp.where(even, line, 0.0)
        for part in range(SPACE // 8):
            start = i * SPACE + part * 8
            fine_weight[start : start + 8] = line
        for part in range(SPACE // 16):
            start = i * (SPACE // 2) + part * 8
            coarse_weight[start : start + 8] = half

    if near:
        edge_y = jnp.where((ty == 0) | (ty == count_y - 1), 1, 0)
        edge_x = jnp.where((tx == 0) | (tx == count_x - 1), 1, 0)
        greeters = (3 - edge_y) * (3 - edge_x) - 1
        if count_y == 8:
            greeters = greeters + edge_y
        pl.semaphore_wait(barrier, greeters)
    else:
        pl.semaphore_wait(barrier, count - 1)

    def rows_of(travel):
        if travel == 0:
            return slice(0, height), slice(RIM, RIM + height)
        if travel > 0:
            return slice(height - RIM, height), low
        return slice(0, RIM), high

    def landing(travel_y, travel_x):
        ref = mid if travel_x == 0 else (left_side if travel_x > 0 else right_side)
        return ref.at[:, rows_of(travel_y)[1]]

    def exists(travel_y, travel_x):
        to_y, to_x = ty + travel_y, tx + travel_x
        return (to_y >= 0) & (to_y < count_y) & (to_x >= 0) & (to_x < count_x)

    for index, (travel_y, travel_x) in enumerate(travels):

        @pl.when(exists(travel_y, travel_x))
        def _():
            source_rows = rows_of(travel_y)[0]
            if travel_x == 0:
                lanes = slice(0, breadth)
            elif travel_x > 0:
                lanes = slice(breadth - 128, breadth)
            else:
                lanes = slice(0, 128)
            for image, ref in enumerate((fixed_hbm, moving_hbm)):
                pltpu.make_async_remote_copy(
                    src_ref=ref.at[source_rows, lanes],
                    dst_ref=landing(travel_y, travel_x).at[image],
                    send_sem=rim_send.at[index],
                    recv_sem=rim_recv.at[index],
                    device_id=(ty + travel_y, tx + travel_x),
                    device_id_type=MESH,
                ).start()

    for load in loads:
        load.wait()

    for index, (travel_y, travel_x) in enumerate(travels):

        @pl.when(exists(-travel_y, -travel_x))
        def _():
            place = landing(travel_y, travel_x)
            pltpu.make_async_copy(place, place, rim_recv.at[index]).wait()

    tiles = breadth // 128
    side_lane = lax.broadcasted_iota(jnp.int32, (height + 2 * RIM, 128), 1)
    for image in range(2):
        for tile in range(tiles):
            full[image * (tiles + 1) + tile] = mid[image, :, tile * 128 : (tile + 1) * 128]
        full[image * (tiles + 1) + tiles] = jnp.where(
            side_lane < 64, right_side[image], left_side[image]
        )

    def fine_image(image):
        base = image * (tiles + 1)
        return jnp.concatenate(
            [full[base + tile, 8 : height + 24] for tile in range(tiles + 1)], axis=1
        )

    def coarse_image(image):
        base = image * (tiles + 1)
        span = height // 2 + RIM
        summed = jnp.concatenate(
            [
                full[base + tile, pl.ds(0, span, stride=2), :]
                + full[base + tile, pl.ds(1, span, stride=2), :]
                for tile in range(tiles + 1)
            ],
            axis=1,
        )
        return 0.25 * (summed + moved(summed, 0, 1))

    terms_into(
        coarse_image(0), coarse_image(1), 2, 2, fixed_minds, moving_minds, coarse_terms, breadth
    )

    small_lane = lax.broadcasted_iota(jnp.int32, (8, 128), 1)
    small_row = lax.broadcasted_iota(jnp.int32, (8, 128), 0)
    knot = lax.rem(small_lane, SEGMENT)
    knot_x = tx * cells_x - 1 + knot
    knot_y = ty * cells_y - 1 + small_row
    valid = (knot < REACH_X) & (small_row < REACH_Y) & (knot_x >= 0) & (knot_x < knots)
    valid = valid & (knot_y >= 0) & (knot_y < count_y * cells_y)
    own = (small_lane < SET) & (knot >= 1) & (knot <= cells_x)
    own = own & (small_row >= 1) & (small_row <= cells_y)

    def displace(window, rows_ref, cols_ref, number=0):
        fields = []
        for member in range(2):
            line = None
            for k in range(REACH_X):
                at = number * SET + member * SEGMENT + k
                part = window[:, at : at + 1] * cols_ref[k]
                line = part if line is None else line + part
            field = None
            for r in range(REACH_Y):
                weights = jnp.concatenate([rows_ref[r]] * tiles, axis=1)
                part = weights * line[r : r + 1, :]
                field = part if field is None else field + part
            fields.append(field)
        return fields

    def gather_up(pixels, rows_ref, cols_ref, number=0):
        out = jnp.zeros((8, 128), F32)
        for member in range(2):
            lines = []
            for r in range(REACH_Y):
                weights = jnp.concatenate([rows_ref[r]] * tiles, axis=1)
                lines.append(jnp.sum(weights * pixels[member], axis=0, keepdims=True))
            lines.append(jnp.zeros((8 - REACH_Y, breadth), F32))
            line = jnp.concatenate(lines, axis=0)
            for k in range(REACH_X):
                column = jnp.sum(line * cols_ref[k], axis=1, keepdims=True)
                at = number * SET + member * SEGMENT + k
                out = jnp.where(small_lane == at, column, out)
        return out

    def slot_of(by_y, by_x):
        return (by_y + 2) * 3 + by_x + 1

    around = [(y, x) for y in range(-2, 3) for x in range(-1, 2) if (y, x) != (0, 0)]

    def send_tile(turn, tile):
        tiles_box[turn, OWN_SLOT] = tile
        for by_y, by_x in around:

            @pl.when(exists(by_y, by_x))
            def _():
                slot = slot_of(-by_y, -by_x)
                pltpu.make_async_remote_copy(
                    src_ref=tiles_box.at[turn, OWN_SLOT],
                    dst_ref=tiles_box.at[turn, slot],
                    send_sem=tile_send.at[slot],
                    recv_sem=tile_recv.at[turn, slot],
                    device_id=(ty + by_y, tx + by_x),
                    device_id_type=MESH,
                ).start()

    def collect_tiles(turn):
        for by_y, by_x in around:

            @pl.when(exists(by_y, by_x))
            def _():
                slot = slot_of(by_y, by_x)
                place = tiles_box.at[turn, slot]
                pltpu.make_async_copy(place, place, tile_recv.at[turn, slot]).wait()

        window = None
        for by_x in range(-1, 2):
            total = None
            for by_y in range(-2, 3):
                part = tiles_box[turn, slot_of(by_y, by_x)]
                if by_y:
                    part = pltpu.roll(part, (2 * by_y) % 8, 0)
                if by_y == 2:
                    part = jnp.where(small_row >= 4, part, 0.0)
                if by_y == -2:
                    part = jnp.where(small_row < 1, part, 0.0)
                total = part if total is None else total + part
            if by_x:
                total = pltpu.roll(total, (8 * by_x) % 128, 1)
                reached = (knot >= 8) if by_x > 0 else (knot < REACH_X - 8)
                total = jnp.where(reached, total, 0.0)
            window = total if window is None else window + total
        return jnp.where(valid, window, 0.0)

    def send_scalars(turn, row):
        scalar_box[turn, me] = row

        def act(device):
            pltpu.make_async_remote_copy(
                src_ref=scalar_box.at[turn, me],
                dst_ref=scalar_box.at[turn, me],
                send_sem=scalar_send.at[turn],
                recv_sem=scalar_recv.at[turn],
                device_id=device,
                device_id_type=MESH,
            ).start()

        for_peers(act)

    def collect_scalars(turn):
        part = scalar_box.at[turn, 0 : count - 1]
        pltpu.make_async_copy(part, part, scalar_recv.at[turn]).wait()
        row = jnp.sum(scalar_box[turn], axis=0)
        lanes = lax.broadcasted_iota(jnp.int32, (1, 128), 1)
        return [
            jnp.sum(
                jnp.where((lanes >= SET * i) & (lanes < SET * (i + 1)), row, 0.0), keepdims=True
            )
            for i in range(4)
        ]

    def scalars(first, second, dense):
        third = jnp.where(own, second * second, 0.0)
        middle = jnp.where(own, first * second, 0.0)
        lead = jnp.where(own, first * first, 0.0)
        packed = lead + pltpu.roll(middle, SET, 1) + pltpu.roll(third, 2 * SET, 1)
        row = jnp.sum(packed, axis=0, keepdims=True)
        dense = dense + pltpu.roll(dense, 64, 1)
        dense = dense + pltpu.roll(dense, 32, 1)
        lanes = lax.broadcasted_iota(jnp.int32, (1, 128), 1)
        return jnp.where(lanes >= 3 * SET, dense, row)

    def pulled(terms_ref, motion):
        return (
            terms_ref[2] * motion[0] + terms_ref[3] * motion[1],
            terms_ref[3] * motion[0] + terms_ref[4] * motion[1],
        )

    def weighted(weight_ref, pair):
        return [weight_ref[...] * pair[0], weight_ref[...] * pair[1]]

    def density_row(weight_ref, motion, pull):
        dense = weight_ref[...] * (motion[0] * pull[0] + motion[1] * pull[1])
        line = jnp.sum(dense, axis=0, keepdims=True)
        total = line[:, :128]
        for tile in range(1, tiles):
            total = total + line[:, tile * 128 : (tile + 1) * 128]
        return total

    def steps_of(first, middle, third, fourth):
        step = first / middle
        norm = first - 2.0 * step * middle + step * step * third
        curvature = middle - 2.0 * step * third + step * step * fourth
        return step, norm / curvature

    send_tile(
        0,
        gather_up(
            weighted(coarse_weight, (coarse_terms[0], coarse_terms[1])), coarse_rows, coarse_cols
        ),
    )
    terms_into(fine_image(0), fine_image(1), 1, 1, fixed_minds, moving_minds, fine_terms, breadth)
    fine_start = gather_up(
        weighted(fine_weight, (fine_terms[0], fine_terms[1])), fine_rows, fine_cols, 1
    )
    gradient0 = collect_tiles(0)

    motion = displace(gradient0, coarse_rows, coarse_cols)
    part = gather_up(
        weighted(coarse_weight, pulled(coarse_terms, motion)), coarse_rows, coarse_cols
    )
    send_tile(1, part + fine_start)
    fine_motion0 = displace(gradient0, fine_rows, fine_cols)
    fine_part0 = gather_up(
        weighted(fine_weight, pulled(fine_terms, fine_motion0)), fine_rows, fine_cols
    )
    gradient1 = collect_tiles(1)

    motion = displace(gradient1, coarse_rows, coarse_cols)
    dense = density_row(coarse_weight, motion, pulled(coarse_terms, motion))
    send_scalars(0, scalars(gradient0, gradient1, dense))
    fine_motion1 = displace(gradient1, fine_rows, fine_cols)
    fine_part1 = gather_up(
        weighted(fine_weight, pulled(fine_terms, fine_motion1)), fine_rows, fine_cols, 1
    )
    send_tile(2, fine_part0 + fine_part1)
    fine_gradient = pltpu.roll(gradient1, 128 - SET, 1)
    images = collect_tiles(2)
    step0, step1 = steps_of(*collect_scalars(0))
    near, far = -(step0 + step1), step0 * step1
    control = near * gradient0 + far * gradient1
    direction = fine_gradient + near * images + far * pltpu.roll(images, 128 - SET, 1)

    motion2 = displace(direction, fine_rows, fine_cols)
    send_tile(
        3,
        gather_up(weighted(fine_weight, pulled(fine_terms, motion2)), fine_rows, fine_cols),
    )
    field_y = near * fine_motion0[0] + far * fine_motion1[0]
    field_x = near * fine_motion0[1] + far * fine_motion1[1]
    image = collect_tiles(3)

    motion3 = displace(image, fine_rows, fine_cols)
    dense = density_row(fine_weight, motion3, pulled(fine_terms, motion3))
    send_scalars(1, scalars(direction, image, dense))
    step0, step1 = steps_of(*collect_scalars(1))
    near, far = -(step0 + step1), step0 * step1
    control = control + near * direction + far * image
    field_y = field_y + near * motion2[0] + far * motion3[0]
    field_x = field_x + near * motion2[1] + far * motion3[1]
    pull_y, pull_x = pulled(fine_terms, (field_y, field_x))
    mismatch_ref[...] = (
        fine_terms[5]
        + 2.0 * (fine_terms[0] * field_y + fine_terms[1] * field_x)
        + field_y * pull_y
        + field_x * pull_x
    )
    for member in range(2):
        start = member * SEGMENT + 1
        coef_ref[member] = control[1 : 1 + cells_y, start : start + cells_x]

    for index, (travel_y, travel_x) in enumerate(travels):

        @pl.when(exists(travel_y, travel_x))
        def _():
            place = landing(travel_y, travel_x)
            pltpu.make_async_copy(place, place, rim_send.at[index]).wait()

    for by_y, by_x in around:

        @pl.when(exists(by_y, by_x))
        def _():
            slot = slot_of(-by_y, -by_x)
            place = tiles_box.at[:, slot]
            pltpu.make_async_copy(place, place, tile_send.at[slot]).wait()

    for turn in range(2):
        part = scalar_box.at[turn, 0 : count - 1]
        pltpu.make_async_copy(part, part, scalar_send.at[turn]).wait()


def window_pairs(span):
    return [(k, k + d) for d in range(4) for k in range(span - d)]


def split(values):
    high = values.astype(B16)
    return high, (values - high.astype(F32)).astype(B16)


def spline_array(values):
    magnitude = np.abs(values)
    rest = 2.0 - magnitude
    near_part = 2.0 / 3.0 - magnitude**2 + 0.5 * magnitude**3
    far_part = rest**3 / 6.0
    return np.where(magnitude < 1.0, near_part, np.where(magnitude < 2.0, far_part, 0.0))


def split_array(values):
    values = values.astype(np.float32)
    high = values.astype(B16)
    return high, (values - high.astype(np.float32)).astype(B16)


def strided_columns(breadth, factor):
    lane, part = np.arange(128)[None, :], np.arange(PARTS)[:, None]
    if factor == 1:
        column = PARTS * lane + part - 8
        return column, (column >= 0) & (column < breadth)
    column = PARTS * (lane - 64) + part - 6
    return column, (lane >= 64) & (column >= 0) & (column < breadth // 2)


def natural_lane(column, breadth):
    return column if column >= 0 else breadth + 128 + column


def stride_tables(breadth):
    size = breadth + 128
    fine = np.zeros((size, PARTS * 128))
    for place in range(breadth + 16):
        fine[natural_lane(place - 8, breadth), place % PARTS * 128 + place // PARTS] = 1.0
    coarse = np.zeros((2, size, PARTS * 128))
    for image in range(2):
        for place in range(breadth // 2 + 12):
            at = place % PARTS * 128 + image * 64 + place // PARTS
            for side in range(2):
                coarse[image, natural_lane(2 * (place - 6) + side, breadth), at] = 0.25
    back = fine[:breadth].T
    return tuple(table.astype(B16) for table in (fine, coarse.reshape(-1, PARTS * 128), back))


def level_tables(height, breadth, factor):
    row_at = factor * np.arange(height // factor) + (factor - 1) / 2.0
    column, taken = strided_columns(breadth, factor)
    col_at = (factor * column + (factor - 1) / 2.0).reshape(-1)
    rows = spline_array(row_at[None, :] / SPACE - (np.arange(REACH_Y)[:, None] - 1.0))
    cols = spline_array(col_at[:, None] / SPACE - (np.arange(REACH_X)[None, :] - 1.0))
    cols = cols * taken.reshape(-1, 1)
    row_pairs = np.zeros((BLOCK, row_at.size))
    for at, (r, other) in enumerate(window_pairs(REACH_Y)):
        row_pairs[at] = rows[r] * rows[other]
    lines = np.zeros((2, BLOCK, row_at.size))
    for member in range(2):
        lines[member, member * REACH_Y : (member + 1) * REACH_Y] = rows
    pairs = window_pairs(REACH_X)
    col_table = np.zeros((4, col_at.size, 128))
    for comp in range(3):
        for at, (k, other) in enumerate(pairs):
            col_table[comp, :, comp * len(pairs) + at] = cols[:, k] * cols[:, other]
    col_table[3, :, 3 * len(pairs) : 3 * len(pairs) + REACH_X] = cols

    def left(table):
        high, low = split_array(table)
        return np.concatenate([high, high, low], axis=1)

    high, low = split_array(col_table.reshape(4 * col_at.size, 128))
    return (
        left(row_pairs),
        np.concatenate([left(lines[0]), left(lines[1])], axis=1),
        np.concatenate([high, low], axis=1),
    )


def assembly_tables(count_y, count_x, cells_y, cells_x):
    knots_y, knots_x = count_y * cells_y, count_x * cells_x
    pairs = window_pairs(REACH_X)
    width = 8 * knots_x
    cols = np.zeros((count_x * 128, 3 * width + 128), np.float32)
    for tx in range(count_x):
        start = (tx % 2 * (count_x // 2) + tx // 2) * 128
        for comp in range(3):
            for at, (k, other) in enumerate(pairs):
                first, second = tx * cells_x - 1 + k, tx * cells_x - 1 + other
                if first < 0 or second >= knots_x:
                    continue
                source, gap = start + comp * len(pairs) + at, other - k
                cols[source, comp * width + (3 + gap) * knots_x + first] = 1.0
                cols[source, comp * width + (3 - gap) * knots_x + second] = 1.0
        for k in range(REACH_X):
            knot = tx * cells_x - 1 + k
            if 0 <= knot < knots_x:
                for group in range(128 // knots_x):
                    cols[start + 3 * len(pairs) + k, 3 * width + group * knots_x + knot] = 1.0
    rows = np.zeros((9 * knots_y, count_y * BLOCK), np.float32)
    for ty in range(count_y):
        for at, (r, other) in enumerate(window_pairs(REACH_Y)):
            first, second = ty * cells_y - 1 + r, ty * cells_y - 1 + other
            if first < 0 or second >= knots_y:
                continue
            rows[(3 + other - r) * knots_y + first, ty * BLOCK + at] = 1.0
            rows[(3 - other + r) * knots_y + second, ty * BLOCK + at] = 1.0
        for member in range(2):
            for r in range(REACH_Y):
                knot = ty * cells_y - 1 + r
                if 0 <= knot < knots_y:
                    rows[(7 + member) * knots_y + knot, ty * BLOCK + member * REACH_Y + r] = 1.0
    return cols.astype(B16), np.concatenate([rows, rows], axis=1).astype(B16)


def dot(left, right):
    return jnp.dot(left, right, preferred_element_type=F32)


def strided(parts, step):
    out = []
    for at in range(PARTS):
        carry, source = divmod(at + step, PARTS)
        part = parts[source]
        out.append(pltpu.roll(part, (-carry) % 128, 1) if carry else part)
    return out


def lowered(parts, step):
    return [pltpu.roll(part, (-step) % part.shape[0], 0) for part in parts] if step else parts


def split_three(values):
    high = values.astype(B16)
    rest = values - high.astype(F32)
    middle = rest.astype(B16)
    return [high, middle, (rest - middle.astype(F32)).astype(B16)]


def boxes_into(parts, boxes_ref):
    rows = parts[0].shape[0]
    turned = {step: strided(parts, step) for step in (2, -2, 4)}
    turned[0] = parts
    total = None
    for index, (offset_y, offset_x) in enumerate(half_offsets):
        other = lowered(turned[offset_x], offset_y)
        square = [(p - q) * (p - q) for p, q in zip(parts, other)]
        lines = [
            p + q + r for p, q, r in zip(square, lowered(square, 1), lowered(square, -1))
        ]
        box = [p + q + r for p, q, r in zip(lines, strided(lines, 1), strided(lines, -1))]
        back = lowered(strided(box, -offset_x) if offset_x else box, -offset_y)
        for at in range(PARTS):
            boxes_ref[2 * index, at, :rows] = box[at]
            boxes_ref[2 * index + 1, at, :rows] = back[at]
        both = [p + q for p, q in zip(box, back)]
        total = both if total is None else [p + q for p, q in zip(total, both)]
    return [-LOG2E / (part / 12.0 + 0.9) for part in total]


def minds_tiled(scale, boxes_ref, minds_ref):
    rows = scale[0].shape[0]
    for index in range(12):
        for at in range(PARTS):
            minds_ref[index, at, :rows] = jnp.exp2(boxes_ref[index, at, :rows] * scale[at])


def sums_into(minds_ref, fixed_of, factor, terms_ref):
    height = terms_ref.shape[1]
    once = 1.0 / (2.0 * factor)
    scales = (once, once, once * once, once * once, once * once, 1.0)
    for start in range(0, height, 8):
        base = 8 + start
        sums = None
        for index in range(12):
            own = [minds_ref[index, at, base : base + 8] for at in range(PARTS)]
            fixed = fixed_of(index, base, own)
            ahead, behind = strided(own, 1), strided(own, -1)
            parts = []
            for at in range(PARTS):
                differ = own[at] - fixed[at]
                slope_y = (
                    minds_ref[index, at, base + 1 : base + 9]
                    - minds_ref[index, at, base - 1 : base + 7]
                )
                slope_x = ahead[at] - behind[at]
                parts += [
                    differ * slope_y,
                    differ * slope_x,
                    slope_y * slope_y,
                    slope_y * slope_x,
                    slope_x * slope_x,
                    differ * differ,
                ]
            sums = parts if sums is None else [a + b for a, b in zip(sums, parts)]
        for at in range(PARTS):
            for term in range(6):
                terms_ref[term, start : start + 8, at * 128 : (at + 1) * 128] = (
                    sums[6 * at + term] * scales[term]
                )


def greeted_by(count_y, count_x, y, x):
    near = {(y + by_y, x + by_x) for by_y, by_x in travels}
    near = {(a, b) for a, b in near if 0 <= a < count_y and 0 <= b < count_x}
    return near | {((y + step) % count_y, x ^ 1) for step in far_greets}


def two_steps_reach(count_y, count_x):
    if count_y < 8 or count_x % 2:
        return False
    every = [(y, x) for y in range(count_y) for x in range(count_x)]
    greeted = {at: greeted_by(count_y, count_x, *at) for at in every}
    for y, x in every:
        known = greeted[y, x].union(*(greeted[at] for at in greeted[y, x]))
        if not {at for at in every if (at[1] - x) % 2 == 0 and at != (y, x)} <= known:
            return False
    return True


def gathered_kernel(
    count_y,
    count_x,
    tissue_hbm,
    fixed_hbm,
    moving_hbm,
    *rest,
):
    tables_hbm, rest = rest[:11], rest[11:]
    coef_ref, mismatch_ref = rest[:2]
    tables, rest = rest[2:13], rest[13:]
    (
        mid,
        left_side,
        right_side,
        full,
        fixed_boxes,
        boxes_ref,
        minds_ref,
        fixed_minds,
        fine_terms,
        coarse_terms,
        fine_weight,
        coarse_weight,
        tissue_ref,
        boxes,
        stencils,
        last_rows,
        last_cols,
        natural,
        load_sem,
        table_sem,
        rim_send,
        rim_recv,
        block_send,
        block_recv,
        relay_send,
        relay_recv,
        ready,
    ) = rest
    fine_tables, coarse_tables, (gather_cols, gather_rows) = tables[:3], tables[3:6], tables[6:8]
    fine_stride, coarse_stride, stride_back = tables[8:]
    ty = lax.axis_index("ty")
    tx = lax.axis_index("tx")
    count = count_y * count_x
    half = count // 2
    me = ty * count_x + tx
    parity = lax.rem(tx, 2)
    place = ty * (count_x // 2) + tx // 2
    sibling = (ty, tx + 1 - 2 * parity)
    height, breadth = fixed_hbm.shape
    cells_y, cells_x = height // SPACE, breadth // SPACE
    knots_y, knots_x = count_y * cells_y, count_x * cells_x
    width = 8 * knots_x
    used = len(window_pairs(REACH_Y))
    wide = PARTS * 128

    def exists(by_y, by_x):
        to_y, to_x = ty + by_y, tx + by_x
        return (to_y >= 0) & (to_y < count_y) & (to_x >= 0) & (to_x < count_x)

    few = two_steps_reach(count_y, count_x)

    def greet_far(semaphore):
        for step in far_greets:
            other = (lax.rem(ty + step + count_y, count_y), sibling[1])
            pl.semaphore_signal(semaphore, 1, device_id=other, device_id_type=MESH)

    barrier = pltpu.get_barrier_semaphore()
    if few:
        for by_y, by_x in travels:

            @pl.when(exists(by_y, by_x))
            def _():
                pl.semaphore_signal(
                    barrier, 1, device_id=(ty + by_y, tx + by_x), device_id_type=MESH
                )

        greet_far(barrier)
        edge_y = jnp.where((ty == 0) | (ty == count_y - 1), 1, 0)
        edge_x = jnp.where((tx == 0) | (tx == count_x - 1), 1, 0)
        greeters = (3 - edge_y) * (3 - edge_x) - 1 + len(far_greets)
    else:
        for step in range(1, count):
            other = lax.rem(me + step, count)
            other = (other // count_x, lax.rem(other, count_x))
            pl.semaphore_signal(barrier, 1, device_id=other, device_id_type=MESH)
        greeters = count - 1

    tissue_load = pltpu.make_async_copy(tissue_hbm, tissue_ref, load_sem.at[2])
    tissue_load.start()
    loads = []
    for image, ref in enumerate((fixed_hbm, moving_hbm)):
        loads.append(
            pltpu.make_async_copy(ref, mid.at[image, RIM : RIM + height], load_sem.at[image])
        )
        loads[image].start()

    boxes[:, :, :, used:] = jnp.zeros((2, 2, half, BLOCK - used, 128), F32)
    low, high = slice(0, RIM), slice(RIM + height, 2 * RIM + height)

    @pl.when(ty == 0)
    def _():
        for ref in (mid, left_side, right_side):
            ref[:, low] = jnp.zeros((2, RIM, ref.shape[2]), F32)

    @pl.when(ty == count_y - 1)
    def _():
        for ref in (mid, left_side, right_side):
            ref[:, high] = jnp.zeros((2, RIM, ref.shape[2]), F32)

    @pl.when(tx == 0)
    def _():
        left_side[...] = jnp.zeros(left_side.shape, F32)

    @pl.when(tx == count_x - 1)
    def _():
        right_side[...] = jnp.zeros(right_side.shape, F32)

    lane = lax.broadcasted_iota(jnp.int32, (8, 128), 1)
    tissue_load.wait()
    for i in range(cells_y):
        for at in range(PARTS):
            fine_at = PARTS * lane + at - 8
            coarse_at = jnp.where(lane < 64, -1, 2 * (PARTS * (lane - 64) + at - 6))
            fine_line = jnp.zeros((8, 128), F32)
            coarse_line = jnp.zeros((8, 128), F32)
            for j in range(cells_x):
                value = tissue_ref[i, j].astype(F32)
                low_x, high_x = j * SPACE, (j + 1) * SPACE
                inside = (fine_at >= low_x) & (fine_at < high_x)
                fine_line = jnp.where(inside, value, fine_line)
                inside = (coarse_at >= low_x) & (coarse_at < high_x)
                coarse_line = jnp.where(inside, value, coarse_line)
            lanes = slice(at * 128, (at + 1) * 128)
            for part in range(SPACE // 8):
                start = i * SPACE + part * 8
                fine_weight[start : start + 8, lanes] = fine_line
            for part in range(SPACE // 16):
                start = i * (SPACE // 2) + part * 8
                coarse_weight[start : start + 8, lanes] = coarse_line

    def rows_of(travel):
        if travel == 0:
            return slice(0, height), slice(RIM, RIM + height)
        if travel > 0:
            return slice(height - RIM, height), low
        return slice(0, RIM), high

    def landing(travel_y, travel_x):
        ref = mid if travel_x == 0 else (left_side if travel_x > 0 else right_side)
        return ref.at[:, rows_of(travel_y)[1]]

    for load in loads:
        load.wait()
    pl.semaphore_wait(barrier, greeters)

    for index, (travel_y, travel_x) in sorted(enumerate(travels), key=lambda item: -abs(item[1][1])):

        @pl.when(exists(travel_y, travel_x))
        def _():
            source_rows = rows_of(travel_y)[0]
            if travel_x == 0:
                lanes = slice(0, breadth)
            elif travel_x > 0:
                lanes = slice(breadth - 128, breadth)
            else:
                lanes = slice(0, 128)
            source_rows = slice(source_rows.start + RIM, source_rows.stop + RIM)
            pltpu.make_async_remote_copy(
                src_ref=mid.at[:, source_rows, lanes],
                dst_ref=landing(travel_y, travel_x),
                send_sem=rim_send.at[index],
                recv_sem=rim_recv.at[index],
                device_id=(ty + travel_y, tx + travel_x),
                device_id_type=MESH,
            ).start()

    if few:
        greet_far(ready)
    table_loads = []
    for index, (source, target) in enumerate(zip(tables_hbm, tables)):
        table_loads.append(pltpu.make_async_copy(source, target, table_sem.at[index]))
        table_loads[index].start()

    knot = lax.broadcasted_iota(jnp.int32, (128, breadth), 0)
    at_x = lax.broadcasted_iota(jnp.int32, (128, breadth), 1).astype(F32) / SPACE
    last = bspline(at_x - (knot - tx * cells_x).astype(F32))
    last_high, last_low = split(jnp.where(knot < knots_x, last, 0.0))
    last_cols[:, :breadth] = last_high
    last_cols[:, breadth:] = last_low
    knot = lax.broadcasted_iota(jnp.int32, (height, 128), 1)
    at_y = lax.broadcasted_iota(jnp.int32, (height, 128), 0).astype(F32) / SPACE
    third = knot // knots_y
    last_high, last_low = split(
        bspline(at_y - (lax.rem(knot, knots_y) - ty * cells_y).astype(F32))
    )
    kept = jnp.where(third < 2, last_high.astype(F32), last_low.astype(F32))
    last_rows[...] = jnp.where(third < 3, kept, 0.0).astype(B16)

    for index, (travel_y, travel_x) in enumerate(travels):

        @pl.when(exists(-travel_y, -travel_x))
        def _():
            spot = landing(travel_y, travel_x)
            pltpu.make_async_copy(spot, spot, rim_recv.at[index]).wait()

    tiles = breadth // 128
    side_lane = lax.broadcasted_iota(jnp.int32, (height + 2 * RIM, 128), 1)
    for image in range(2):
        for tile in range(tiles):
            full[image * (tiles + 1) + tile] = mid[image, :, tile * 128 : (tile + 1) * 128]
        full[image * (tiles + 1) + tiles] = jnp.where(
            side_lane < 64, right_side[image], left_side[image]
        )

    def fine_image(image):
        base = image * (tiles + 1)
        return jnp.concatenate(
            [full[base + tile, 8 : height + 24] for tile in range(tiles + 1)], axis=1
        )

    def coarse_image(image):
        base = image * (tiles + 1)
        span = height // 2 + RIM
        return jnp.concatenate(
            [
                full[base + tile, pl.ds(0, span, stride=2), :]
                + full[base + tile, pl.ds(1, span, stride=2), :]
                for tile in range(tiles + 1)
            ],
            axis=1,
        )

    def parts_of(values):
        return [values[:, at * 128 : (at + 1) * 128] for at in range(PARTS)]

    def coarse_terms_into():
        pieces = split_three(jnp.concatenate([coarse_image(0), coarse_image(1)], axis=1))
        out = dot(jnp.concatenate(pieces, axis=0), coarse_stride[...])
        rows = pieces[0].shape[0]
        pair = out[:rows] + out[rows : 2 * rows] + out[2 * rows :]
        minds_tiled(boxes_into(parts_of(pair), boxes_ref), boxes_ref, minds_ref)

        def fixed_of(index, base, own):
            return [pltpu.roll(part, 64, 1) for part in own]

        sums_into(minds_ref, fixed_of, 2, coarse_terms)

    def fine_terms_into():
        pieces = split_three(jnp.concatenate([fine_image(0), fine_image(1)], axis=0))
        out = dot(jnp.concatenate(pieces, axis=0), fine_stride[...])
        rows = height + 16
        both = out[: 2 * rows] + out[2 * rows : 4 * rows] + out[4 * rows :]
        scale = boxes_into(parts_of(both[:rows]), fixed_boxes)
        for at in range(PARTS):
            fixed_minds[:, at * 128 : (at + 1) * 128] = scale[at][8 : 8 + height]
        minds_tiled(boxes_into(parts_of(both[rows:]), boxes_ref), boxes_ref, minds_ref)

        def fixed_of(index, base, own):
            return [
                jnp.exp2(
                    fixed_boxes[index, at, base : base + 8]
                    * fixed_minds[base - 8 : base, at * 128 : (at + 1) * 128]
                )
                for at in range(PARTS)
            ]

        sums_into(minds_ref, fixed_of, 1, fine_terms)

    def block_of(terms_ref, weight_ref, level):
        row_pairs, row_lines, col_table = level
        weight = weight_ref[...]
        upper, lower = split(
            jnp.concatenate([weight * terms_ref[index] for index in (2, 3, 4)], axis=1)
        )
        pairs = dot(row_pairs[...], jnp.concatenate([upper, lower, upper], axis=0))
        stack = []
        for member in range(2):
            upper, lower = split(weight * terms_ref[member])
            stack += [upper, lower, upper]
        lines = dot(row_lines[...], jnp.concatenate(stack, axis=0))
        upper, lower = split(jnp.concatenate([pairs, lines], axis=1))
        out = dot(jnp.concatenate([upper, lower], axis=0), col_table[...])
        return out[:BLOCK, :128] + out[BLOCK:, :128] + out[:BLOCK, 128:]

    def send_block(level, block):
        boxes[level, parity, place, 0:used] = block[:used]
        for step_y in [*range(1, count_y), 0]:
            for step_x in reversed(range(count_x // 2)):
                if step_y + step_x == 0:
                    continue
                to_y = lax.rem(ty + step_y, count_y)
                to_x = 2 * lax.rem(tx // 2 + step_x, count_x // 2) + parity
                pltpu.make_async_remote_copy(
                    src_ref=boxes.at[level, parity, place, 0:used],
                    dst_ref=boxes.at[level, parity, place, 0:used],
                    send_sem=block_send.at[level],
                    recv_sem=block_recv.at[level],
                    device_id=(to_y, to_x),
                    device_id_type=MESH,
                ).start()

    def relay_of(level):
        return pltpu.make_async_remote_copy(
            src_ref=boxes.at[level, parity, :, 0:used],
            dst_ref=boxes.at[level, parity, :, 0:used],
            send_sem=relay_send.at[level],
            recv_sem=relay_recv.at[level],
            device_id=sibling,
            device_id_type=MESH,
        )

    def columns_of(level, side):
        across = count_x // 2
        columns = [
            jnp.concatenate(
                [boxes[level, side, to_y * across + to_x] for to_y in range(count_y)], axis=0
            )
            for to_x in range(across)
        ]
        upper, lower = split(jnp.concatenate(columns, axis=1))
        lines = pl.ds(pl.multiple_of(side * (across * 128), 128), across * 128)
        placed = dot(gather_rows[...], jnp.concatenate([upper, lower], axis=0))
        out = dot(jnp.concatenate(split(placed), axis=0), gather_cols[lines])
        return out[: placed.shape[0]] + out[placed.shape[0] :]

    def relay(level):
        part = boxes.at[level, 0, 0 : half - 1, 0:used]
        pltpu.make_async_copy(part, part, block_recv.at[level]).wait()
        relay_of(level).start()

    def assemble(level, own):
        spot = boxes.at[level, 1 - parity, :, 0:used]
        pltpu.make_async_copy(spot, spot, relay_recv.at[level]).wait()
        stencils[level] = own + columns_of(level, 1 - parity)

    group = lax.broadcasted_iota(jnp.int32, (knots_y, 128), 1) // knots_x

    def spread(values):
        halves = []
        for start in (-3, 1):
            out = None
            for index in range(4):
                gap = start + index
                rolled = pltpu.roll(values, (-gap) % 128, 1) if gap else values
                out = rolled if out is None else jnp.where(group >= index, rolled, out)
            halves.append(out)
        return halves

    def start_of(level):
        return [
            stencils[level, (7 + member) * knots_y : (8 + member) * knots_y, 3 * width :]
            for member in range(2)
        ]

    def pull(level, spreads):
        sums = [None, None]
        for gap in range(-3, 4):
            at = (gap + 3) * knots_y
            for source in range(2):
                for part in range(2):
                    shifted = spreads[source][part]
                    if gap:
                        shifted = pltpu.roll(shifted, (-gap) % knots_y, 0)
                    for member in range(2):
                        lanes = (member + source) * width + part * 128
                        term = stencils[level, at : at + knots_y, lanes : lanes + 128] * shifted
                        old = sums[member]
                        sums[member] = term if old is None else old + term
        out = []
        for total in sums:
            total = total + pltpu.roll(total, 64, 1)
            out.append(total + pltpu.roll(total, 32, 1))
        return out

    def inner(first, second):
        return jnp.sum(first[0] * second[0] + first[1] * second[1], keepdims=True)

    def descend(level, control, gradient):
        image = pull(level, [spread(values) for values in gradient])
        step = inner(gradient, gradient) / inner(gradient, image)
        control = [c - step * g for c, g in zip(control, gradient)]
        return control, [g - step * i for g, i in zip(gradient, image)]

    for load in table_loads:
        load.wait()
    coarse_terms_into()
    coarse_block = block_of(coarse_terms, coarse_weight, coarse_tables)
    if few:
        pl.semaphore_wait(ready, len(far_greets))
    send_block(0, coarse_block)
    fine_terms_into()
    send_block(1, block_of(fine_terms, fine_weight, fine_tables))

    for term in range(6):
        pieces = split_three(fine_terms[term])
        out = dot(jnp.concatenate(pieces, axis=0), stride_back[...])
        natural[term] = out[:height] + out[height : 2 * height] + out[2 * height :]

    relay(0)
    assemble(0, columns_of(0, parity))
    control = [jnp.zeros((knots_y, 128), F32)] * 2
    control, gradient = descend(0, control, start_of(0))
    relay(1)
    fine_own = columns_of(1, parity)
    control, _ = descend(0, control, gradient)
    spreads = [spread(values) for values in control]
    assemble(1, fine_own)
    gradient = [b + i for b, i in zip(start_of(1), pull(1, spreads))]
    control, gradient = descend(1, control, gradient)
    control, _ = descend(1, control, gradient)

    upper, lower = split(jnp.concatenate(control, axis=0))
    rows = 2 * knots_y
    out = dot(jnp.concatenate([upper, lower], axis=0), last_cols[...])
    lines = out[:rows, :breadth] + out[rows:, :breadth] + out[:rows, breadth:]
    upper, lower = split(jnp.concatenate([lines[:knots_y], lines[knots_y:]], axis=1))
    blank = jnp.zeros((128 - 3 * knots_y, 2 * breadth), B16)
    field = dot(last_rows[...], jnp.concatenate([upper, lower, upper, blank], axis=0))
    field_y, field_x = field[:, :breadth], field[:, breadth:]
    pull_y = natural[2] * field_y + natural[3] * field_x
    pull_x = natural[3] * field_y + natural[4] * field_x
    mismatch_ref[...] = (
        natural[5]
        + 2.0 * (natural[0] * field_y + natural[1] * field_x)
        + field_y * pull_y
        + field_x * pull_x
    )
    for member in range(2):
        own = pltpu.roll(control[member], lax.rem(128 - cells_x * tx, 128), 1)
        own = pltpu.roll(own, lax.rem(knots_y - cells_y * ty, knots_y), 0)
        coef_ref[member] = own[:cells_y, :cells_x]

    for index, (travel_y, travel_x) in enumerate(travels):

        @pl.when(exists(travel_y, travel_x))
        def _():
            spot = landing(travel_y, travel_x)
            pltpu.make_async_copy(spot, spot, rim_send.at[index]).wait()

    for level in range(2):
        part = boxes.at[level, 0, 0 : half - 1, 0:used]
        pltpu.make_async_copy(part, part, block_send.at[level]).wait()
        relay_of(level).wait_send()


def spread_call(count_y, count_x, tissue, fixed_image, moving_image):
    height, breadth = fixed_image.shape
    cells_y, cells_x = height // SPACE, breadth // SPACE
    count = count_y * count_x
    tall, full_lanes = height + 2 * RIM, breadth + 128
    vmem = pltpu.VMEM
    scratch = [
        vmem((2, tall, breadth), F32),
        vmem((2, tall, 128), F32),
        vmem((2, tall, 128), F32),
        vmem((2 * (breadth // 128 + 1), tall, 128), F32),
        vmem((12, height + 16, full_lanes), F32),
        vmem((12, height + 16, full_lanes), F32),
        vmem((6, height, breadth), F32),
        vmem((6, height // 2, breadth), F32),
        vmem((height, breadth), F32),
        vmem((height // 2, breadth), F32),
        vmem((REACH_Y, height, 128), F32),
        vmem((REACH_Y, height // 2, 128), F32),
        vmem((REACH_X, 8, breadth), F32),
        vmem((REACH_X, 8, breadth), F32),
        pltpu.SMEM((cells_y, cells_x), jnp.int32),
        vmem((4, 15, 8, 128), F32),
        vmem((2, count, 1, 128), F32),
        pltpu.SemaphoreType.DMA((3,)),
        pltpu.SemaphoreType.DMA((8,)),
        pltpu.SemaphoreType.DMA((8,)),
        pltpu.SemaphoreType.DMA((15,)),
        pltpu.SemaphoreType.DMA((4, 15)),
        pltpu.SemaphoreType.DMA((2,)),
        pltpu.SemaphoreType.DMA((2,)),
    ]
    return pl.pallas_call(
        functools.partial(spread_kernel, count_y, count_x),
        out_shape=(
            jax.ShapeDtypeStruct((2, cells_y, cells_x), F32),
            jax.ShapeDtypeStruct((height, breadth), F32),
        ),
        in_specs=[
            pl.BlockSpec(memory_space=pltpu.HBM),
            pl.BlockSpec(memory_space=pltpu.HBM),
            pl.BlockSpec(memory_space=pltpu.HBM),
        ],
        out_specs=(
            pl.BlockSpec(memory_space=pltpu.VMEM),
            pl.BlockSpec(memory_space=pltpu.VMEM),
        ),
        scratch_shapes=scratch,
        compiler_params=pltpu.CompilerParams(
            collective_id=0, has_side_effects=True, vmem_limit_bytes=16 * 1024 * 1024
        ),
    )(tissue, fixed_image, moving_image)


def closing(coef_in, mismatch_in, coef_out, mismatch_out, sem):
    loads = [
        pltpu.make_async_copy(mismatch_in, mismatch_out, sem.at[0]),
        pltpu.make_async_copy(coef_in, coef_out, sem.at[1]),
    ]
    for load in loads:
        load.start()
    for load in loads:
        load.wait()


def gathered_call(count_y, count_x, tissue, fixed_image, moving_image):
    height, breadth = fixed_image.shape
    cells_y, cells_x = height // SPACE, breadth // SPACE
    count = count_y * count_x
    tall, wide = height + 2 * RIM, PARTS * 128
    vmem, dma = pltpu.VMEM, pltpu.SemaphoreType.DMA
    tables = (
        level_tables(height, breadth, 1)
        + level_tables(height, breadth, 2)
        + assembly_tables(count_y, count_x, cells_y, cells_x)
        + stride_tables(breadth)
    )
    scratch = [vmem(table.shape, B16) for table in tables] + [
        vmem((2, tall, breadth), F32),
        vmem((2, tall, 128), F32),
        vmem((2, tall, 128), F32),
        vmem((2 * (breadth // 128 + 1), tall, 128), F32),
        vmem((12, PARTS, height + 16, 128), F32),
        vmem((12, PARTS, height + 16, 128), F32),
        vmem((12, PARTS, height + 16, 128), F32),
        vmem((height, wide), F32),
        vmem((6, height, wide), F32),
        vmem((6, height // 2, wide), F32),
        vmem((height, wide), F32),
        vmem((height // 2, wide), F32),
        pltpu.SMEM((cells_y, cells_x), jnp.int32),
        vmem((2, 2, count // 2, BLOCK, 128), F32),
        vmem((2, tables[7].shape[0], tables[6].shape[1]), F32),
        vmem((height, 128), B16),
        vmem((128, 2 * breadth), B16),
        vmem((6, height, breadth), F32),
        dma((3,)),
        dma((12,)),
        dma((8,)),
        dma((8,)),
        dma((2,)),
        dma((2,)),
        dma((2,)),
        dma((2,)),
        pltpu.SemaphoreType.REGULAR,
    ]
    held = [
        pltpu.with_memory_space_constraint(jnp.asarray(table), pltpu.HBM) for table in tables
    ]
    return pl.pallas_call(
        functools.partial(gathered_kernel, count_y, count_x),
        out_shape=(
            jax.ShapeDtypeStruct((2, cells_y, cells_x), F32),
            jax.ShapeDtypeStruct((height, breadth), F32),
        ),
        in_specs=[pl.BlockSpec(memory_space=pltpu.HBM)] * 14,
        out_specs=(
            pl.BlockSpec(memory_space=pltpu.VMEM),
            pl.BlockSpec(memory_space=pltpu.VMEM),
        ),
        scratch_shapes=scratch,
        compiler_params=pltpu.CompilerParams(
            collective_id=1, has_side_effects=True, vmem_limit_bytes=32 * 1024 * 1024
        ),
    )(tissue, fixed_image, moving_image, *held)


def shards(count_y, count_x, fixed_image, moving_image, tissue):
    held = [pltpu.with_memory_space_constraint(x, pltpu.HBM) for x in (tissue, fixed_image, moving_image)]
    height, breadth = fixed_image.shape
    fits = height == 2 * SPACE and breadth == 8 * SPACE and count_x % 2 == 0
    fits = fits and count_x * (breadth // SPACE) == 32 and count_y * count_x <= LARGEST
    call = gathered_call if fits else spread_call
    coef, mismatch = call(count_y, count_x, *held)
    return pl.pallas_call(
        closing,
        out_shape=(
            jax.ShapeDtypeStruct(coef.shape, F32),
            jax.ShapeDtypeStruct(mismatch.shape, F32),
        ),
        in_specs=[pl.BlockSpec(memory_space=pl.ANY)] * 2,
        out_specs=(pl.BlockSpec(memory_space=pltpu.HBM),) * 2,
        scratch_shapes=[pltpu.SemaphoreType.DMA((2,))],
        compiler_params=pltpu.CompilerParams(vmem_limit_bytes=4 * 1024 * 1024),
    )(coef, mismatch)


def solution(mesh):
    placed = (P("ty", "tx"), P("ty", "tx"), P("ty", "tx"))
    return jax.shard_map(
        functools.partial(shards, mesh.shape["ty"], mesh.shape["tx"]),
        mesh=mesh,
        in_specs=placed,
        out_specs=(P(None, "ty", "tx"), P("ty", "tx")),
        check_vma=False,
    )
```

```python
import functools

import jax
import jax.numpy as jnp
import numpy as np
from jax import lax
from jax.experimental import pallas as pl
from jax.experimental.pallas import tpu as pltpu
from jax.sharding import PartitionSpec as P

SPACE = 32
REACH_Y = 5
REACH_X = 11
RIM = 16
SEGMENT = 16
SET = 32
OWN_SLOT = 7
MESH = pl.DeviceIdType.MESH
F32 = jnp.float32
B16 = jnp.bfloat16
BLOCK = 16
PARTS = 3
LOG2E = 1.4426950408889634
LARGEST = 64

half_offsets = ((0, 2), (2, 0), (2, 2), (2, -2), (0, 4), (4, 0))
far_greets = (2, -2, 4)
travels = ((-1, 0), (1, 0), (0, -1), (0, 1), (-1, -1), (-1, 1), (1, -1), (1, 1))


def bspline(values):
    magnitude = jnp.abs(values)
    near_part = 2.0 / 3.0 - magnitude * magnitude + 0.5 * magnitude * magnitude * magnitude
    rest = 2.0 - magnitude
    far_part = rest * rest * rest / 6.0
    return jnp.where(magnitude < 1.0, near_part, jnp.where(magnitude < 2.0, far_part, 0.0))


def moved(values, by_y, by_x):
    rows, lanes = values.shape
    if by_x:
        values = pltpu.roll(values, (-by_x) % lanes, 1)
    if by_y:
        values = pltpu.roll(values, (-by_y) % rows, 0)
    return values


def minds_into(image, lane_step, out_ref):
    total = None
    for index, (offset_y, offset_x) in enumerate(half_offsets):
        gap = image - moved(image, offset_y, lane_step * offset_x)
        square = gap * gap
        rows = square + moved(square, 1, 0) + moved(square, -1, 0)
        box = rows + moved(rows, 0, lane_step) + moved(rows, 0, -lane_step)
        other = moved(box, -offset_y, -lane_step * offset_x)
        out_ref[2 * index, : image.shape[0]] = box
        out_ref[2 * index + 1, : image.shape[0]] = other
        both = box + other
        total = both if total is None else total + both
    return -1.0 / (total / 12.0 + 0.9)


def terms_into(fixed, moving, lane_step, factor, fixed_ref, moving_ref, terms_ref, wide):
    rows = fixed.shape[0]
    height = rows - 16
    fixed_scale = minds_into(fixed, lane_step, fixed_ref)[8 : 8 + height, :wide]
    moving_scale = minds_into(moving, lane_step, moving_ref)
    sums = None
    for index in range(12):
        fixed_mind = jnp.exp(fixed_ref[index, 8 : 8 + height, :wide] * fixed_scale)
        mind = jnp.exp(moving_ref[index, :rows] * moving_scale)
        differ = mind[8 : 8 + height, :wide] - fixed_mind
        slope_y = moved(mind[:, :wide], 1, 0) - moved(mind[:, :wide], -1, 0)
        slope_y = slope_y[8 : 8 + height]
        own = mind[8 : 8 + height]
        slope_x = (moved(own, 0, lane_step) - moved(own, 0, -lane_step))[:, :wide]
        parts = (
            differ * slope_y,
            differ * slope_x,
            slope_y * slope_y,
            slope_y * slope_x,
            slope_x * slope_x,
            differ * differ,
        )
        sums = parts if sums is None else tuple(a + b for a, b in zip(sums, parts))
    once = 1.0 / (2.0 * factor)
    scales = (once, once, once * once, once * once, once * once, 1.0)
    for index in range(6):
        terms_ref[index] = sums[index] * scales[index]


def spread_kernel(
    count_y,
    count_x,
    tissue_hbm,
    fixed_hbm,
    moving_hbm,
    coef_ref,
    mismatch_ref,
    mid,
    left_side,
    right_side,
    full,
    fixed_minds,
    moving_minds,
    fine_terms,
    coarse_terms,
    fine_weight,
    coarse_weight,
    fine_rows,
    coarse_rows,
    fine_cols,
    coarse_cols,
    tissue_ref,
    tiles_box,
    scalar_box,
    load_sem,
    rim_send,
    rim_recv,
    tile_send,
    tile_recv,
    scalar_send,
    scalar_recv,
):
    ty = lax.axis_index("ty")
    tx = lax.axis_index("tx")
    count = count_y * count_x
    me = ty * count_x + tx
    height, breadth = fixed_hbm.shape
    knots = count_x * (breadth // SPACE)
    cells_y, cells_x = height // SPACE, breadth // SPACE

    def peer(step):
        other = lax.rem(me + step, count)
        return (other // count_x, lax.rem(other, count_x))

    def for_peers(act):
        if count <= 64:
            for step in range(1, count):
                act(peer(step))
        else:

            def body(step, carry):
                act(peer(step))
                return carry

            lax.fori_loop(1, count, body, 0)

    tissue_load = pltpu.make_async_copy(tissue_hbm, tissue_ref, load_sem.at[2])
    tissue_load.start()
    loads = []
    for image, ref in enumerate((fixed_hbm, moving_hbm)):
        loads.append(
            pltpu.make_async_copy(ref, mid.at[image, RIM : RIM + height], load_sem.at[image])
        )
        loads[image].start()

    low, high = slice(0, RIM), slice(RIM + height, 2 * RIM + height)

    @pl.when(ty == 0)
    def _():
        for ref in (mid, left_side, right_side):
            ref[:, low] = jnp.zeros((2, RIM, ref.shape[2]), F32)

    @pl.when(ty == count_y - 1)
    def _():
        for ref in (mid, left_side, right_side):
            ref[:, high] = jnp.zeros((2, RIM, ref.shape[2]), F32)

    @pl.when(tx == 0)
    def _():
        left_side[...] = jnp.zeros(left_side.shape, F32)

    @pl.when(tx == count_x - 1)
    def _():
        right_side[...] = jnp.zeros(right_side.shape, F32)

    tiles_box[...] = jnp.zeros(tiles_box.shape, F32)

    barrier = pltpu.get_barrier_semaphore()
    near = 2 <= count_y <= 8 and 2 <= count_x <= 4
    greeted = [(y, x) for y in range(-1, 2) for x in range(-1, 2) if (y, x) != (0, 0)]
    if count_y == 8:
        greeted += [(1 - count_y, 0), (count_y - 1, 0)]

    def here(by_y, by_x):
        to_y, to_x = ty + by_y, tx + by_x
        return (to_y >= 0) & (to_y < count_y) & (to_x >= 0) & (to_x < count_x)

    def greet(device):
        pl.semaphore_signal(barrier, 1, device_id=device, device_id_type=MESH)

    if near:
        for by_y, by_x in greeted:

            @pl.when(here(by_y, by_x))
            def _():
                greet((ty + by_y, tx + by_x))

    else:
        for_peers(greet)

    lane = lax.broadcasted_iota(jnp.int32, (8, breadth), 1)
    for k in range(REACH_X):
        fine_cols[k] = bspline(lane.astype(F32) / SPACE - (k - 1.0))
        coarse_cols[k] = bspline((lane.astype(F32) + 0.5) / SPACE - (k - 1.0))
    row = lax.broadcasted_iota(jnp.int32, (height, 128), 0).astype(F32)
    coarse_row = lax.broadcasted_iota(jnp.int32, (height // 2, 128), 0).astype(F32)
    for r in range(REACH_Y):
        fine_rows[r] = bspline(row / SPACE - (r - 1.0))
        coarse_rows[r] = bspline((2.0 * coarse_row + 0.5) / SPACE - (r - 1.0))
    even = lax.rem(lane, 2) == 0
    tissue_load.wait()
    for i in range(cells_y):
        line = jnp.zeros((8, breadth), F32)
        for j in range(cells_x):
            value = tissue_ref[i, j].astype(F32)
            inside = (lane >= j * SPACE) & (lane < (j + 1) * SPACE)
            line = jnp.where(inside, value, line)
        half = jnp.where(even, line, 0.0)
        for part in range(SPACE // 8):
            start = i * SPACE + part * 8
            fine_weight[start : start + 8] = line
        for part in range(SPACE // 16):
            start = i * (SPACE // 2) + part * 8
            coarse_weight[start : start + 8] = half

    if near:
        edge_y = jnp.where((ty == 0) | (ty == count_y - 1), 1, 0)
        edge_x = jnp.where((tx == 0) | (tx == count_x - 1), 1, 0)
        greeters = (3 - edge_y) * (3 - edge_x) - 1
        if count_y == 8:
            greeters = greeters + edge_y
        pl.semaphore_wait(barrier, greeters)
    else:
        pl.semaphore_wait(barrier, count - 1)

    def rows_of(travel):
        if travel == 0:
            return slice(0, height), slice(RIM, RIM + height)
        if travel > 0:
            return slice(height - RIM, height), low
        return slice(0, RIM), high

    def landing(travel_y, travel_x):
        ref = mid if travel_x == 0 else (left_side if travel_x > 0 else right_side)
        return ref.at[:, rows_of(travel_y)[1]]

    def exists(travel_y, travel_x):
        to_y, to_x = ty + travel_y, tx + travel_x
        return (to_y >= 0) & (to_y < count_y) & (to_x >= 0) & (to_x < count_x)

    for index, (travel_y, travel_x) in enumerate(travels):

        @pl.when(exists(travel_y, travel_x))
        def _():
            source_rows = rows_of(travel_y)[0]
            if travel_x == 0:
                lanes = slice(0, breadth)
            elif travel_x > 0:
                lanes = slice(breadth - 128, breadth)
            else:
                lanes = slice(0, 128)
            for image, ref in enumerate((fixed_hbm, moving_hbm)):
                pltpu.make_async_remote_copy(
                    src_ref=ref.at[source_rows, lanes],
                    dst_ref=landing(travel_y, travel_x).at[image],
                    send_sem=rim_send.at[index],
                    recv_sem=rim_recv.at[index],
                    device_id=(ty + travel_y, tx + travel_x),
                    device_id_type=MESH,
                ).start()

    for load in loads:
        load.wait()

    for index, (travel_y, travel_x) in enumerate(travels):

        @pl.when(exists(-travel_y, -travel_x))
        def _():
            place = landing(travel_y, travel_x)
            pltpu.make_async_copy(place, place, rim_recv.at[index]).wait()

    tiles = breadth // 128
    side_lane = lax.broadcasted_iota(jnp.int32, (height + 2 * RIM, 128), 1)
    for image in range(2):
        for tile in range(tiles):
            full[image * (tiles + 1) + tile] = mid[image, :, tile * 128 : (tile + 1) * 128]
        full[image * (tiles + 1) + tiles] = jnp.where(
            side_lane < 64, right_side[image], left_side[image]
        )

    def fine_image(image):
        base = image * (tiles + 1)
        return jnp.concatenate(
            [full[base + tile, 8 : height + 24] for tile in range(tiles + 1)], axis=1
        )

    def coarse_image(image):
        base = image * (tiles + 1)
        span = height // 2 + RIM
        summed = jnp.concatenate(
            [
                full[base + tile, pl.ds(0, span, stride=2), :]
                + full[base + tile, pl.ds(1, span, stride=2), :]
                for tile in range(tiles + 1)
            ],
            axis=1,
        )
        return 0.25 * (summed + moved(summed, 0, 1))

    terms_into(
        coarse_image(0), coarse_image(1), 2, 2, fixed_minds, moving_minds, coarse_terms, breadth
    )

    small_lane = lax.broadcasted_iota(jnp.int32, (8, 128), 1)
    small_row = lax.broadcasted_iota(jnp.int32, (8, 128), 0)
    knot = lax.rem(small_lane, SEGMENT)
    knot_x = tx * cells_x - 1 + knot
    knot_y = ty * cells_y - 1 + small_row
    valid = (knot < REACH_X) & (small_row < REACH_Y) & (knot_x >= 0) & (knot_x < knots)
    valid = valid & (knot_y >= 0) & (knot_y < count_y * cells_y)
    own = (small_lane < SET) & (knot >= 1) & (knot <= cells_x)
    own = own & (small_row >= 1) & (small_row <= cells_y)

    def displace(window, rows_ref, cols_ref, number=0):
        fields = []
        for member in range(2):
            line = None
            for k in range(REACH_X):
                at = number * SET + member * SEGMENT + k
                part = window[:, at : at + 1] * cols_ref[k]
                line = part if line is None else line + part
            field = None
            for r in range(REACH_Y):
                weights = jnp.concatenate([rows_ref[r]] * tiles, axis=1)
                part = weights * line[r : r + 1, :]
                field = part if field is None else field + part
            fields.append(field)
        return fields

    def gather_up(pixels, rows_ref, cols_ref, number=0):
        out = jnp.zeros((8, 128), F32)
        for member in range(2):
            lines = []
            for r in range(REACH_Y):
                weights = jnp.concatenate([rows_ref[r]] * tiles, axis=1)
                lines.append(jnp.sum(weights * pixels[member], axis=0, keepdims=True))
            lines.append(jnp.zeros((8 - REACH_Y, breadth), F32))
            line = jnp.concatenate(lines, axis=0)
            for k in range(REACH_X):
                column = jnp.sum(line * cols_ref[k], axis=1, keepdims=True)
                at = number * SET + member * SEGMENT + k
                out = jnp.where(small_lane == at, column, out)
        return out

    def slot_of(by_y, by_x):
        return (by_y + 2) * 3 + by_x + 1

    around = [(y, x) for y in range(-2, 3) for x in range(-1, 2) if (y, x) != (0, 0)]

    def send_tile(turn, tile):
        tiles_box[turn, OWN_SLOT] = tile
        for by_y, by_x in around:

            @pl.when(exists(by_y, by_x))
            def _():
                slot = slot_of(-by_y, -by_x)
                pltpu.make_async_remote_copy(
                    src_ref=tiles_box.at[turn, OWN_SLOT],
                    dst_ref=tiles_box.at[turn, slot],
                    send_sem=tile_send.at[slot],
                    recv_sem=tile_recv.at[turn, slot],
                    device_id=(ty + by_y, tx + by_x),
                    device_id_type=MESH,
                ).start()

    def collect_tiles(turn):
        for by_y, by_x in around:

            @pl.when(exists(by_y, by_x))
            def _():
                slot = slot_of(by_y, by_x)
                place = tiles_box.at[turn, slot]
                pltpu.make_async_copy(place, place, tile_recv.at[turn, slot]).wait()

        window = None
        for by_x in range(-1, 2):
            total = None
            for by_y in range(-2, 3):
                part = tiles_box[turn, slot_of(by_y, by_x)]
                if by_y:
                    part = pltpu.roll(part, (2 * by_y) % 8, 0)
                if by_y == 2:
                    part = jnp.where(small_row >= 4, part, 0.0)
                if by_y == -2:
                    part = jnp.where(small_row < 1, part, 0.0)
                total = part if total is None else total + part
            if by_x:
                total = pltpu.roll(total, (8 * by_x) % 128, 1)
                reached = (knot >= 8) if by_x > 0 else (knot < REACH_X - 8)
                total = jnp.where(reached, total, 0.0)
            window = total if window is None else window + total
        return jnp.where(valid, window, 0.0)

    def send_scalars(turn, row):
        scalar_box[turn, me] = row

        def act(device):
            pltpu.make_async_remote_copy(
                src_ref=scalar_box.at[turn, me],
                dst_ref=scalar_box.at[turn, me],
                send_sem=scalar_send.at[turn],
                recv_sem=scalar_recv.at[turn],
                device_id=device,
                device_id_type=MESH,
            ).start()

        for_peers(act)

    def collect_scalars(turn):
        part = scalar_box.at[turn, 0 : count - 1]
        pltpu.make_async_copy(part, part, scalar_recv.at[turn]).wait()
        row = jnp.sum(scalar_box[turn], axis=0)
        lanes = lax.broadcasted_iota(jnp.int32, (1, 128), 1)
        return [
            jnp.sum(
                jnp.where((lanes >= SET * i) & (lanes < SET * (i + 1)), row, 0.0), keepdims=True
            )
            for i in range(4)
        ]

    def scalars(first, second, dense):
        third = jnp.where(own, second * second, 0.0)
        middle = jnp.where(own, first * second, 0.0)
        lead = jnp.where(own, first * first, 0.0)
        packed = lead + pltpu.roll(middle, SET, 1) + pltpu.roll(third, 2 * SET, 1)
        row = jnp.sum(packed, axis=0, keepdims=True)
        dense = dense + pltpu.roll(dense, 64, 1)
        dense = dense + pltpu.roll(dense, 32, 1)
        lanes = lax.broadcasted_iota(jnp.int32, (1, 128), 1)
        return jnp.where(lanes >= 3 * SET, dense, row)

    def pulled(terms_ref, motion):
        return (
            terms_ref[2] * motion[0] + terms_ref[3] * motion[1],
            terms_ref[3] * motion[0] + terms_ref[4] * motion[1],
        )

    def weighted(weight_ref, pair):
        return [weight_ref[...] * pair[0], weight_ref[...] * pair[1]]

    def density_row(weight_ref, motion, pull):
        dense = weight_ref[...] * (motion[0] * pull[0] + motion[1] * pull[1])
        line = jnp.sum(dense, axis=0, keepdims=True)
        total = line[:, :128]
        for tile in range(1, tiles):
            total = total + line[:, tile * 128 : (tile + 1) * 128]
        return total

    def steps_of(first, middle, third, fourth):
        step = first / middle
        norm = first - 2.0 * step * middle + step * step * third
        curvature = middle - 2.0 * step * third + step * step * fourth
        return step, norm / curvature

    send_tile(
        0,
        gather_up(
            weighted(coarse_weight, (coarse_terms[0], coarse_terms[1])), coarse_rows, coarse_cols
        ),
    )
    terms_into(fine_image(0), fine_image(1), 1, 1, fixed_minds, moving_minds, fine_terms, breadth)
    fine_start = gather_up(
        weighted(fine_weight, (fine_terms[0], fine_terms[1])), fine_rows, fine_cols, 1
    )
    gradient0 = collect_tiles(0)

    motion = displace(gradient0, coarse_rows, coarse_cols)
    part = gather_up(
        weighted(coarse_weight, pulled(coarse_terms, motion)), coarse_rows, coarse_cols
    )
    send_tile(1, part + fine_start)
    fine_motion0 = displace(gradient0, fine_rows, fine_cols)
    fine_part0 = gather_up(
        weighted(fine_weight, pulled(fine_terms, fine_motion0)), fine_rows, fine_cols
    )
    gradient1 = collect_tiles(1)

    motion = displace(gradient1, coarse_rows, coarse_cols)
    dense = density_row(coarse_weight, motion, pulled(coarse_terms, motion))
    send_scalars(0, scalars(gradient0, gradient1, dense))
    fine_motion1 = displace(gradient1, fine_rows, fine_cols)
    fine_part1 = gather_up(
        weighted(fine_weight, pulled(fine_terms, fine_motion1)), fine_rows, fine_cols, 1
    )
    send_tile(2, fine_part0 + fine_part1)
    fine_gradient = pltpu.roll(gradient1, 128 - SET, 1)
    images = collect_tiles(2)
    step0, step1 = steps_of(*collect_scalars(0))
    near, far = -(step0 + step1), step0 * step1
    control = near * gradient0 + far * gradient1
    direction = fine_gradient + near * images + far * pltpu.roll(images, 128 - SET, 1)

    motion2 = displace(direction, fine_rows, fine_cols)
    send_tile(
        3,
        gather_up(weighted(fine_weight, pulled(fine_terms, motion2)), fine_rows, fine_cols),
    )
    field_y = near * fine_motion0[0] + far * fine_motion1[0]
    field_x = near * fine_motion0[1] + far * fine_motion1[1]
    image = collect_tiles(3)

    motion3 = displace(image, fine_rows, fine_cols)
    dense = density_row(fine_weight, motion3, pulled(fine_terms, motion3))
    send_scalars(1, scalars(direction, image, dense))
    step0, step1 = steps_of(*collect_scalars(1))
    near, far = -(step0 + step1), step0 * step1
    control = control + near * direction + far * image
    field_y = field_y + near * motion2[0] + far * motion3[0]
    field_x = field_x + near * motion2[1] + far * motion3[1]
    pull_y, pull_x = pulled(fine_terms, (field_y, field_x))
    mismatch_ref[...] = (
        fine_terms[5]
        + 2.0 * (fine_terms[0] * field_y + fine_terms[1] * field_x)
        + field_y * pull_y
        + field_x * pull_x
    )
    for member in range(2):
        start = member * SEGMENT + 1
        coef_ref[member] = control[1 : 1 + cells_y, start : start + cells_x]

    for index, (travel_y, travel_x) in enumerate(travels):

        @pl.when(exists(travel_y, travel_x))
        def _():
            place = landing(travel_y, travel_x)
            pltpu.make_async_copy(place, place, rim_send.at[index]).wait()

    for by_y, by_x in around:

        @pl.when(exists(by_y, by_x))
        def _():
            slot = slot_of(-by_y, -by_x)
            place = tiles_box.at[:, slot]
            pltpu.make_async_copy(place, place, tile_send.at[slot]).wait()

    for turn in range(2):
        part = scalar_box.at[turn, 0 : count - 1]
        pltpu.make_async_copy(part, part, scalar_send.at[turn]).wait()


def window_pairs(span):
    return [(k, k + d) for d in range(4) for k in range(span - d)]


def split(values):
    high = values.astype(B16)
    return high, (values - high.astype(F32)).astype(B16)


def spline_array(values):
    magnitude = np.abs(values)
    rest = 2.0 - magnitude
    near_part = 2.0 / 3.0 - magnitude**2 + 0.5 * magnitude**3
    far_part = rest**3 / 6.0
    return np.where(magnitude < 1.0, near_part, np.where(magnitude < 2.0, far_part, 0.0))


def split_array(values):
    values = values.astype(np.float32)
    high = values.astype(B16)
    return high, (values - high.astype(np.float32)).astype(B16)


def strided_columns(breadth, factor):
    lane, part = np.arange(128)[None, :], np.arange(PARTS)[:, None]
    if factor == 1:
        column = PARTS * lane + part - 8
        return column, (column >= 0) & (column < breadth)
    column = PARTS * (lane - 64) + part - 6
    return column, (lane >= 64) & (column >= 0) & (column < breadth // 2)


def natural_lane(column, breadth):
    return column if column >= 0 else breadth + 128 + column


def stride_tables(breadth):
    size = breadth + 128
    fine = np.zeros((size, PARTS * 128))
    for place in range(breadth + 16):
        fine[natural_lane(place - 8, breadth), place % PARTS * 128 + place // PARTS] = 1.0
    coarse = np.zeros((2, size, PARTS * 128))
    for image in range(2):
        for place in range(breadth // 2 + 12):
            at = place % PARTS * 128 + image * 64 + place // PARTS
            for side in range(2):
                coarse[image, natural_lane(2 * (place - 6) + side, breadth), at] = 0.25
    back = fine[:breadth].T
    return tuple(table.astype(B16) for table in (fine, coarse.reshape(-1, PARTS * 128), back))


def level_tables(height, breadth, factor):
    row_at = factor * np.arange(height // factor) + (factor - 1) / 2.0
    column, taken = strided_columns(breadth, factor)
    col_at = (factor * column + (factor - 1) / 2.0).reshape(-1)
    rows = spline_array(row_at[None, :] / SPACE - (np.arange(REACH_Y)[:, None] - 1.0))
    cols = spline_array(col_at[:, None] / SPACE - (np.arange(REACH_X)[None, :] - 1.0))
    cols = cols * taken.reshape(-1, 1)
    row_pairs = np.zeros((BLOCK, row_at.size))
    for at, (r, other) in enumerate(window_pairs(REACH_Y)):
        row_pairs[at] = rows[r] * rows[other]
    lines = np.zeros((2, BLOCK, row_at.size))
    for member in range(2):
        lines[member, member * REACH_Y : (member + 1) * REACH_Y] = rows
    pairs = window_pairs(REACH_X)
    col_table = np.zeros((4, col_at.size, 128))
    for comp in range(3):
        for at, (k, other) in enumerate(pairs):
            col_table[comp, :, comp * len(pairs) + at] = cols[:, k] * cols[:, other]
    col_table[3, :, 3 * len(pairs) : 3 * len(pairs) + REACH_X] = cols

    def left(table):
        high, low = split_array(table)
        return np.concatenate([high, high, low], axis=1)

    high, low = split_array(col_table.reshape(4 * col_at.size, 128))
    return (
        left(row_pairs),
        np.concatenate([left(lines[0]), left(lines[1])], axis=1),
        np.concatenate([high, low], axis=1),
    )


def assembly_tables(count_y, count_x, cells_y, cells_x):
    knots_y, knots_x = count_y * cells_y, count_x * cells_x
    pairs = window_pairs(REACH_X)
    width = 8 * knots_x
    cols = np.zeros((count_x * 128, 3 * width + 128), np.float32)
    for tx in range(count_x):
        start = (tx % 2 * (count_x // 2) + tx // 2) * 128
        for comp in range(3):
            for at, (k, other) in enumerate(pairs):
                first, second = tx * cells_x - 1 + k, tx * cells_x - 1 + other
                if first < 0 or second >= knots_x:
                    continue
                source, gap = start + comp * len(pairs) + at, other - k
                cols[source, comp * width + (3 + gap) * knots_x + first] = 1.0
                cols[source, comp * width + (3 - gap) * knots_x + second] = 1.0
        for k in range(REACH_X):
            knot = tx * cells_x - 1 + k
            if 0 <= knot < knots_x:
                for group in range(128 // knots_x):
                    cols[start + 3 * len(pairs) + k, 3 * width + group * knots_x + knot] = 1.0
    rows = np.zeros((9 * knots_y, count_y * BLOCK), np.float32)
    for ty in range(count_y):
        for at, (r, other) in enumerate(window_pairs(REACH_Y)):
            first, second = ty * cells_y - 1 + r, ty * cells_y - 1 + other
            if first < 0 or second >= knots_y:
                continue
            rows[(3 + other - r) * knots_y + first, ty * BLOCK + at] = 1.0
            rows[(3 - other + r) * knots_y + second, ty * BLOCK + at] = 1.0
        for member in range(2):
            for r in range(REACH_Y):
                knot = ty * cells_y - 1 + r
                if 0 <= knot < knots_y:
                    rows[(7 + member) * knots_y + knot, ty * BLOCK + member * REACH_Y + r] = 1.0
    return cols.astype(B16), np.concatenate([rows, rows], axis=1).astype(B16)


def dot(left, right):
    return jnp.dot(left, right, preferred_element_type=F32)


def strided(parts, step):
    out = []
    for at in range(PARTS):
        carry, source = divmod(at + step, PARTS)
        part = parts[source]
        out.append(pltpu.roll(part, (-carry) % 128, 1) if carry else part)
    return out


def lowered(parts, step):
    return [pltpu.roll(part, (-step) % part.shape[0], 0) for part in parts] if step else parts


def split_three(values):
    high = values.astype(B16)
    rest = values - high.astype(F32)
    middle = rest.astype(B16)
    return [high, middle, (rest - middle.astype(F32)).astype(B16)]


def boxes_into(parts, boxes_ref):
    rows = parts[0].shape[0]
    turned = {step: strided(parts, step) for step in (2, -2, 4)}
    turned[0] = parts
    total = None
    for index, (offset_y, offset_x) in enumerate(half_offsets):
        other = lowered(turned[offset_x], offset_y)
        square = [(p - q) * (p - q) for p, q in zip(parts, other)]
        lines = [
            p + q + r for p, q, r in zip(square, lowered(square, 1), lowered(square, -1))
        ]
        box = [p + q + r for p, q, r in zip(lines, strided(lines, 1), strided(lines, -1))]
        back = lowered(strided(box, -offset_x) if offset_x else box, -offset_y)
        for at in range(PARTS):
            boxes_ref[2 * index, at, :rows] = box[at]
            boxes_ref[2 * index + 1, at, :rows] = back[at]
        both = [p + q for p, q in zip(box, back)]
        total = both if total is None else [p + q for p, q in zip(total, both)]
    return [-LOG2E / (part / 12.0 + 0.9) for part in total]


def minds_tiled(scale, boxes_ref, minds_ref):
    rows = scale[0].shape[0]
    for index in range(12):
        for at in range(PARTS):
            minds_ref[index, at, :rows] = jnp.exp2(boxes_ref[index, at, :rows] * scale[at])


def sums_into(minds_ref, fixed_of, factor, terms_ref):
    height = terms_ref.shape[1]
    once = 1.0 / (2.0 * factor)
    scales = (once, once, once * once, once * once, once * once, 1.0)
    for start in range(0, height, 8):
        base = 8 + start
        sums = None
        for index in range(12):
            own = [minds_ref[index, at, base : base + 8] for at in range(PARTS)]
            fixed = fixed_of(index, base, own)
            ahead, behind = strided(own, 1), strided(own, -1)
            parts = []
            for at in range(PARTS):
                differ = own[at] - fixed[at]
                slope_y = (
                    minds_ref[index, at, base + 1 : base + 9]
                    - minds_ref[index, at, base - 1 : base + 7]
                )
                slope_x = ahead[at] - behind[at]
                parts += [
                    differ * slope_y,
                    differ * slope_x,
                    slope_y * slope_y,
                    slope_y * slope_x,
                    slope_x * slope_x,
                    differ * differ,
                ]
            sums = parts if sums is None else [a + b for a, b in zip(sums, parts)]
        for at in range(PARTS):
            for term in range(6):
                terms_ref[term, start : start + 8, at * 128 : (at + 1) * 128] = (
                    sums[6 * at + term] * scales[term]
                )


def greeted_by(count_y, count_x, y, x):
    near = {(y + by_y, x + by_x) for by_y, by_x in travels}
    near = {(a, b) for a, b in near if 0 <= a < count_y and 0 <= b < count_x}
    return near | {((y + step) % count_y, x ^ 1) for step in far_greets}


def two_steps_reach(count_y, count_x):
    if count_y < 8 or count_x % 2:
        return False
    every = [(y, x) for y in range(count_y) for x in range(count_x)]
    greeted = {at: greeted_by(count_y, count_x, *at) for at in every}
    for y, x in every:
        known = greeted[y, x].union(*(greeted[at] for at in greeted[y, x]))
        if not {at for at in every if (at[1] - x) % 2 == 0 and at != (y, x)} <= known:
            return False
    return True


def gathered_kernel(
    count_y,
    count_x,
    tissue_hbm,
    fixed_hbm,
    moving_hbm,
    *rest,
):
    tables_hbm, rest = rest[:11], rest[11:]
    coef_ref, mismatch_ref = rest[:2]
    tables, rest = rest[2:13], rest[13:]
    (
        mid,
        left_side,
        right_side,
        full,
        fixed_boxes,
        boxes_ref,
        minds_ref,
        fixed_minds,
        fine_terms,
        coarse_terms,
        fine_weight,
        coarse_weight,
        tissue_ref,
        boxes,
        stencils,
        last_rows,
        last_cols,
        natural,
        load_sem,
        table_sem,
        rim_send,
        rim_recv,
        block_send,
        block_recv,
        relay_send,
        relay_recv,
        ready,
    ) = rest
    fine_tables, coarse_tables, (gather_cols, gather_rows) = tables[:3], tables[3:6], tables[6:8]
    fine_stride, coarse_stride, stride_back = tables[8:]
    ty = lax.axis_index("ty")
    tx = lax.axis_index("tx")
    count = count_y * count_x
    half = count // 2
    me = ty * count_x + tx
    parity = lax.rem(tx, 2)
    place = ty * (count_x // 2) + tx // 2
    sibling = (ty, tx + 1 - 2 * parity)
    height, breadth = fixed_hbm.shape
    cells_y, cells_x = height // SPACE, breadth // SPACE
    knots_y, knots_x = count_y * cells_y, count_x * cells_x
    width = 8 * knots_x
    used = len(window_pairs(REACH_Y))
    wide = PARTS * 128

    def exists(by_y, by_x):
        to_y, to_x = ty + by_y, tx + by_x
        return (to_y >= 0) & (to_y < count_y) & (to_x >= 0) & (to_x < count_x)

    few = two_steps_reach(count_y, count_x)

    def greet_far(semaphore):
        for step in far_greets:
            other = (lax.rem(ty + step + count_y, count_y), sibling[1])
            pl.semaphore_signal(semaphore, 1, device_id=other, device_id_type=MESH)

    barrier = pltpu.get_barrier_semaphore()
    if few:
        for by_y, by_x in travels:

            @pl.when(exists(by_y, by_x))
            def _():
                pl.semaphore_signal(
                    barrier, 1, device_id=(ty + by_y, tx + by_x), device_id_type=MESH
                )

        greet_far(barrier)
        edge_y = jnp.where((ty == 0) | (ty == count_y - 1), 1, 0)
        edge_x = jnp.where((tx == 0) | (tx == count_x - 1), 1, 0)
        greeters = (3 - edge_y) * (3 - edge_x) - 1 + len(far_greets)
    else:
        for step in range(1, count):
            other = lax.rem(me + step, count)
            other = (other // count_x, lax.rem(other, count_x))
            pl.semaphore_signal(barrier, 1, device_id=other, device_id_type=MESH)
        greeters = count - 1

    tissue_load = pltpu.make_async_copy(tissue_hbm, tissue_ref, load_sem.at[2])
    tissue_load.start()
    loads = []
    for image, ref in enumerate((fixed_hbm, moving_hbm)):
        loads.append(
            pltpu.make_async_copy(ref, mid.at[image, RIM : RIM + height], load_sem.at[image])
        )
        loads[image].start()

    low, high = slice(0, RIM), slice(RIM + height, 2 * RIM + height)

    @pl.when(ty == 0)
    def _():
        for ref in (mid, left_side, right_side):
            ref[:, low] = jnp.zeros((2, RIM, ref.shape[2]), F32)

    @pl.when(ty == count_y - 1)
    def _():
        for ref in (mid, left_side, right_side):
            ref[:, high] = jnp.zeros((2, RIM, ref.shape[2]), F32)

    @pl.when(tx == 0)
    def _():
        left_side[...] = jnp.zeros(left_side.shape, F32)

    @pl.when(tx == count_x - 1)
    def _():
        right_side[...] = jnp.zeros(right_side.shape, F32)

    def rows_of(travel):
        if travel == 0:
            return slice(0, height), slice(RIM, RIM + height)
        if travel > 0:
            return slice(height - RIM, height), low
        return slice(0, RIM), high

    def landing(travel_y, travel_x):
        ref = mid if travel_x == 0 else (left_side if travel_x > 0 else right_side)
        return ref.at[:, rows_of(travel_y)[1]]

    for load in loads:
        load.wait()
    pl.semaphore_wait(barrier, greeters)

    for index, (travel_y, travel_x) in sorted(enumerate(travels), key=lambda item: -abs(item[1][1])):

        @pl.when(exists(travel_y, travel_x))
        def _():
            source_rows = rows_of(travel_y)[0]
            if travel_x == 0:
                lanes = slice(0, breadth)
            elif travel_x > 0:
                lanes = slice(breadth - 128, breadth)
            else:
                lanes = slice(0, 128)
            source_rows = slice(source_rows.start + RIM, source_rows.stop + RIM)
            pltpu.make_async_remote_copy(
                src_ref=mid.at[:, source_rows, lanes],
                dst_ref=landing(travel_y, travel_x),
                send_sem=rim_send.at[index],
                recv_sem=rim_recv.at[index],
                device_id=(ty + travel_y, tx + travel_x),
                device_id_type=MESH,
            ).start()

    if few:
        greet_far(ready)
    table_loads = []
    for index, (source, target) in enumerate(zip(tables_hbm, tables)):
        table_loads.append(pltpu.make_async_copy(source, target, table_sem.at[index]))
        table_loads[index].start()

    boxes[:, :, :, used:] = jnp.zeros((2, 2, half, BLOCK - used, 128), F32)
    lane = lax.broadcasted_iota(jnp.int32, (8, 128), 1)
    tissue_load.wait()
    for i in range(cells_y):
        for at in range(PARTS):
            fine_at = PARTS * lane + at - 8
            coarse_at = jnp.where(lane < 64, -1, 2 * (PARTS * (lane - 64) + at - 6))
            fine_line = jnp.zeros((8, 128), F32)
            coarse_line = jnp.zeros((8, 128), F32)
            for j in range(cells_x):
                value = tissue_ref[i, j].astype(F32)
                low_x, high_x = j * SPACE, (j + 1) * SPACE
                inside = (fine_at >= low_x) & (fine_at < high_x)
                fine_line = jnp.where(inside, value, fine_line)
                inside = (coarse_at >= low_x) & (coarse_at < high_x)
                coarse_line = jnp.where(inside, value, coarse_line)
            lanes = slice(at * 128, (at + 1) * 128)
            for part in range(SPACE // 8):
                start = i * SPACE + part * 8
                fine_weight[start : start + 8, lanes] = fine_line
            for part in range(SPACE // 16):
                start = i * (SPACE // 2) + part * 8
                coarse_weight[start : start + 8, lanes] = coarse_line

    knot = lax.broadcasted_iota(jnp.int32, (128, breadth), 0)
    at_x = lax.broadcasted_iota(jnp.int32, (128, breadth), 1).astype(F32) / SPACE
    last = bspline(at_x - (knot - tx * cells_x).astype(F32))
    last_high, last_low = split(jnp.where(knot < knots_x, last, 0.0))
    last_cols[:, :breadth] = last_high
    last_cols[:, breadth:] = last_low
    knot = lax.broadcasted_iota(jnp.int32, (height, 128), 1)
    at_y = lax.broadcasted_iota(jnp.int32, (height, 128), 0).astype(F32) / SPACE
    third = knot // knots_y
    last_high, last_low = split(
        bspline(at_y - (lax.rem(knot, knots_y) - ty * cells_y).astype(F32))
    )
    kept = jnp.where(third < 2, last_high.astype(F32), last_low.astype(F32))
    last_rows[...] = jnp.where(third < 3, kept, 0.0).astype(B16)

    for index, (travel_y, travel_x) in enumerate(travels):

        @pl.when(exists(-travel_y, -travel_x))
        def _():
            spot = landing(travel_y, travel_x)
            pltpu.make_async_copy(spot, spot, rim_recv.at[index]).wait()

    tiles = breadth // 128
    side_lane = lax.broadcasted_iota(jnp.int32, (height + 2 * RIM, 128), 1)
    for image in range(2):
        for tile in range(tiles):
            full[image * (tiles + 1) + tile] = mid[image, :, tile * 128 : (tile + 1) * 128]
        full[image * (tiles + 1) + tiles] = jnp.where(
            side_lane < 64, right_side[image], left_side[image]
        )

    def fine_image(image):
        base = image * (tiles + 1)
        return jnp.concatenate(
            [full[base + tile, 8 : height + 24] for tile in range(tiles + 1)], axis=1
        )

    def coarse_image(image):
        base = image * (tiles + 1)
        span = height // 2 + RIM
        return jnp.concatenate(
            [
                full[base + tile, pl.ds(0, span, stride=2), :]
                + full[base + tile, pl.ds(1, span, stride=2), :]
                for tile in range(tiles + 1)
            ],
            axis=1,
        )

    def parts_of(values):
        return [values[:, at * 128 : (at + 1) * 128] for at in range(PARTS)]

    def coarse_terms_into():
        pieces = split_three(jnp.concatenate([coarse_image(0), coarse_image(1)], axis=1))
        out = dot(jnp.concatenate(pieces, axis=0), coarse_stride[...])
        rows = pieces[0].shape[0]
        pair = out[:rows] + out[rows : 2 * rows] + out[2 * rows :]
        minds_tiled(boxes_into(parts_of(pair), boxes_ref), boxes_ref, minds_ref)

        def fixed_of(index, base, own):
            return [pltpu.roll(part, 64, 1) for part in own]

        sums_into(minds_ref, fixed_of, 2, coarse_terms)

    def fine_terms_into():
        rows = height + 16
        turned = []
        for image in range(2):
            pieces = split_three(fine_image(image))
            out = dot(jnp.concatenate(pieces, axis=0), fine_stride[...])
            turned.append(parts_of(out[:rows] + out[rows : 2 * rows] + out[2 * rows :]))
        scale = boxes_into(turned[0], fixed_boxes)
        for at in range(PARTS):
            fixed_minds[:, at * 128 : (at + 1) * 128] = scale[at][8 : 8 + height]
        minds_tiled(boxes_into(turned[1], boxes_ref), boxes_ref, minds_ref)

        def fixed_of(index, base, own):
            return [
                jnp.exp2(
                    fixed_boxes[index, at, base : base + 8]
                    * fixed_minds[base - 8 : base, at * 128 : (at + 1) * 128]
                )
                for at in range(PARTS)
            ]

        sums_into(minds_ref, fixed_of, 1, fine_terms)

    def block_of(terms_ref, weight_ref, level):
        row_pairs, row_lines, col_table = level
        weight = weight_ref[...]
        upper, lower = split(
            jnp.concatenate([weight * terms_ref[index] for index in (2, 3, 4)], axis=1)
        )
        pairs = dot(row_pairs[...], jnp.concatenate([upper, lower, upper], axis=0))
        stack = []
        for member in range(2):
            upper, lower = split(weight * terms_ref[member])
            stack += [upper, lower, upper]
        lines = dot(row_lines[...], jnp.concatenate(stack, axis=0))
        upper, lower = split(jnp.concatenate([pairs, lines], axis=1))
        out = dot(jnp.concatenate([upper, lower], axis=0), col_table[...])
        return out[:BLOCK, :128] + out[BLOCK:, :128] + out[:BLOCK, 128:]

    def send_block(level, block):
        boxes[level, parity, place, 0:used] = block[:used]
        for step_y in [*range(1, count_y), 0]:
            for step_x in reversed(range(count_x // 2)):
                if step_y + step_x == 0:
                    continue
                to_y = lax.rem(ty + step_y, count_y)
                to_x = 2 * lax.rem(tx // 2 + step_x, count_x // 2) + parity
                pltpu.make_async_remote_copy(
                    src_ref=boxes.at[level, parity, place, 0:used],
                    dst_ref=boxes.at[level, parity, place, 0:used],
                    send_sem=block_send.at[level],
                    recv_sem=block_recv.at[level],
                    device_id=(to_y, to_x),
                    device_id_type=MESH,
                ).start()

    def relay_of(level):
        return pltpu.make_async_remote_copy(
            src_ref=boxes.at[level, parity, :, 0:used],
            dst_ref=boxes.at[level, parity, :, 0:used],
            send_sem=relay_send.at[level],
            recv_sem=relay_recv.at[level],
            device_id=sibling,
            device_id_type=MESH,
        )

    def columns_of(level, side):
        across = count_x // 2
        columns = [
            jnp.concatenate(
                [boxes[level, side, to_y * across + to_x] for to_y in range(count_y)], axis=0
            )
            for to_x in range(across)
        ]
        upper, lower = split(jnp.concatenate(columns, axis=1))
        lines = pl.ds(pl.multiple_of(side * (across * 128), 128), across * 128)
        placed = dot(gather_rows[...], jnp.concatenate([upper, lower], axis=0))
        out = dot(jnp.concatenate(split(placed), axis=0), gather_cols[lines])
        return out[: placed.shape[0]] + out[placed.shape[0] :]

    def relay(level):
        part = boxes.at[level, 0, 0 : half - 1, 0:used]
        pltpu.make_async_copy(part, part, block_recv.at[level]).wait()
        relay_of(level).start()

    def assemble(level, own):
        spot = boxes.at[level, 1 - parity, :, 0:used]
        pltpu.make_async_copy(spot, spot, relay_recv.at[level]).wait()
        stencils[level] = own + columns_of(level, 1 - parity)

    group = lax.broadcasted_iota(jnp.int32, (knots_y, 128), 1) // knots_x

    def spread(values):
        halves = []
        for start in (-3, 1):
            out = None
            for index in range(4):
                gap = start + index
                rolled = pltpu.roll(values, (-gap) % 128, 1) if gap else values
                out = rolled if out is None else jnp.where(group >= index, rolled, out)
            halves.append(out)
        return halves

    def start_of(level):
        return [
            stencils[level, (7 + member) * knots_y : (8 + member) * knots_y, 3 * width :]
            for member in range(2)
        ]

    def pull(level, spreads):
        sums = [None, None]
        for gap in range(-3, 4):
            at = (gap + 3) * knots_y
            for source in range(2):
                for part in range(2):
                    shifted = spreads[source][part]
                    if gap:
                        shifted = pltpu.roll(shifted, (-gap) % knots_y, 0)
                    for member in range(2):
                        lanes = (member + source) * width + part * 128
                        term = stencils[level, at : at + knots_y, lanes : lanes + 128] * shifted
                        old = sums[member]
                        sums[member] = term if old is None else old + term
        out = []
        for total in sums:
            total = total + pltpu.roll(total, 64, 1)
            out.append(total + pltpu.roll(total, 32, 1))
        return out

    def inner(first, second):
        return jnp.sum(first[0] * second[0] + first[1] * second[1], keepdims=True)

    def descend(level, control, gradient):
        image = pull(level, [spread(values) for values in gradient])
        step = inner(gradient, gradient) / inner(gradient, image)
        control = [c - step * g for c, g in zip(control, gradient)]
        return control, [g - step * i for g, i in zip(gradient, image)]

    for load in table_loads:
        load.wait()
    coarse_terms_into()
    coarse_block = block_of(coarse_terms, coarse_weight, coarse_tables)
    if few:
        pl.semaphore_wait(ready, len(far_greets))
    send_block(0, coarse_block)
    fine_terms_into()
    send_block(1, block_of(fine_terms, fine_weight, fine_tables))

    for term in range(6):
        pieces = split_three(fine_terms[term])
        out = dot(jnp.concatenate(pieces, axis=0), stride_back[...])
        natural[term] = out[:height] + out[height : 2 * height] + out[2 * height :]

    relay(0)
    assemble(0, columns_of(0, parity))
    control = [jnp.zeros((knots_y, 128), F32)] * 2
    control, gradient = descend(0, control, start_of(0))
    relay(1)
    fine_own = columns_of(1, parity)
    control, _ = descend(0, control, gradient)
    spreads = [spread(values) for values in control]
    assemble(1, fine_own)
    gradient = [b + i for b, i in zip(start_of(1), pull(1, spreads))]
    control, gradient = descend(1, control, gradient)
    control, _ = descend(1, control, gradient)

    upper, lower = split(jnp.concatenate(control, axis=0))
    rows = 2 * knots_y
    out = dot(jnp.concatenate([upper, lower], axis=0), last_cols[...])
    lines = out[:rows, :breadth] + out[rows:, :breadth] + out[:rows, breadth:]
    upper, lower = split(jnp.concatenate([lines[:knots_y], lines[knots_y:]], axis=1))
    blank = jnp.zeros((128 - 3 * knots_y, 2 * breadth), B16)
    field = dot(last_rows[...], jnp.concatenate([upper, lower, upper, blank], axis=0))
    field_y, field_x = field[:, :breadth], field[:, breadth:]
    pull_y = natural[2] * field_y + natural[3] * field_x
    pull_x = natural[3] * field_y + natural[4] * field_x
    mismatch_ref[...] = (
        natural[5]
        + 2.0 * (natural[0] * field_y + natural[1] * field_x)
        + field_y * pull_y
        + field_x * pull_x
    )
    for member in range(2):
        own = pltpu.roll(control[member], lax.rem(128 - cells_x * tx, 128), 1)
        own = pltpu.roll(own, lax.rem(knots_y - cells_y * ty, knots_y), 0)
        coef_ref[member] = own[:cells_y, :cells_x]

    for index, (travel_y, travel_x) in enumerate(travels):

        @pl.when(exists(travel_y, travel_x))
        def _():
            spot = landing(travel_y, travel_x)
            pltpu.make_async_copy(spot, spot, rim_send.at[index]).wait()

    for level in range(2):
        part = boxes.at[level, 0, 0 : half - 1, 0:used]
        pltpu.make_async_copy(part, part, block_send.at[level]).wait()
        relay_of(level).wait_send()


def spread_call(count_y, count_x, tissue, fixed_image, moving_image):
    height, breadth = fixed_image.shape
    cells_y, cells_x = height // SPACE, breadth // SPACE
    count = count_y * count_x
    tall, full_lanes = height + 2 * RIM, breadth + 128
    vmem = pltpu.VMEM
    scratch = [
        vmem((2, tall, breadth), F32),
        vmem((2, tall, 128), F32),
        vmem((2, tall, 128), F32),
        vmem((2 * (breadth // 128 + 1), tall, 128), F32),
        vmem((12, height + 16, full_lanes), F32),
        vmem((12, height + 16, full_lanes), F32),
        vmem((6, height, breadth), F32),
        vmem((6, height // 2, breadth), F32),
        vmem((height, breadth), F32),
        vmem((height // 2, breadth), F32),
        vmem((REACH_Y, height, 128), F32),
        vmem((REACH_Y, height // 2, 128), F32),
        vmem((REACH_X, 8, breadth), F32),
        vmem((REACH_X, 8, breadth), F32),
        pltpu.SMEM((cells_y, cells_x), jnp.int32),
        vmem((4, 15, 8, 128), F32),
        vmem((2, count, 1, 128), F32),
        pltpu.SemaphoreType.DMA((3,)),
        pltpu.SemaphoreType.DMA((8,)),
        pltpu.SemaphoreType.DMA((8,)),
        pltpu.SemaphoreType.DMA((15,)),
        pltpu.SemaphoreType.DMA((4, 15)),
        pltpu.SemaphoreType.DMA((2,)),
        pltpu.SemaphoreType.DMA((2,)),
    ]
    return pl.pallas_call(
        functools.partial(spread_kernel, count_y, count_x),
        out_shape=(
            jax.ShapeDtypeStruct((2, cells_y, cells_x), F32),
            jax.ShapeDtypeStruct((height, breadth), F32),
        ),
        in_specs=[
            pl.BlockSpec(memory_space=pltpu.HBM),
            pl.BlockSpec(memory_space=pltpu.HBM),
            pl.BlockSpec(memory_space=pltpu.HBM),
        ],
        out_specs=(
            pl.BlockSpec(memory_space=pltpu.VMEM),
            pl.BlockSpec(memory_space=pltpu.VMEM),
        ),
        scratch_shapes=scratch,
        compiler_params=pltpu.CompilerParams(
            collective_id=0, has_side_effects=True, vmem_limit_bytes=16 * 1024 * 1024
        ),
    )(tissue, fixed_image, moving_image)


def closing(coef_in, mismatch_in, coef_out, mismatch_out, sem):
    loads = [
        pltpu.make_async_copy(mismatch_in, mismatch_out, sem.at[0]),
        pltpu.make_async_copy(coef_in, coef_out, sem.at[1]),
    ]
    for load in loads:
        load.start()
    for load in loads:
        load.wait()


def gathered_call(count_y, count_x, tissue, fixed_image, moving_image):
    height, breadth = fixed_image.shape
    cells_y, cells_x = height // SPACE, breadth // SPACE
    count = count_y * count_x
    tall, wide = height + 2 * RIM, PARTS * 128
    vmem, dma = pltpu.VMEM, pltpu.SemaphoreType.DMA
    tables = (
        level_tables(height, breadth, 1)
        + level_tables(height, breadth, 2)
        + assembly_tables(count_y, count_x, cells_y, cells_x)
        + stride_tables(breadth)
    )
    scratch = [vmem(table.shape, B16) for table in tables] + [
        vmem((2, tall, breadth), F32),
        vmem((2, tall, 128), F32),
        vmem((2, tall, 128), F32),
        vmem((2 * (breadth // 128 + 1), tall, 128), F32),
        vmem((12, PARTS, height + 16, 128), F32),
        vmem((12, PARTS, height + 16, 128), F32),
        vmem((12, PARTS, height + 16, 128), F32),
        vmem((height, wide), F32),
        vmem((6, height, wide), F32),
        vmem((6, height // 2, wide), F32),
        vmem((height, wide), F32),
        vmem((height // 2, wide), F32),
        pltpu.SMEM((cells_y, cells_x), jnp.int32),
        vmem((2, 2, count // 2, BLOCK, 128), F32),
        vmem((2, tables[7].shape[0], tables[6].shape[1]), F32),
        vmem((height, 128), B16),
        vmem((128, 2 * breadth), B16),
        vmem((6, height, breadth), F32),
        dma((3,)),
        dma((12,)),
        dma((8,)),
        dma((8,)),
        dma((2,)),
        dma((2,)),
        dma((2,)),
        dma((2,)),
        pltpu.SemaphoreType.REGULAR,
    ]
    held = [
        pltpu.with_memory_space_constraint(jnp.asarray(table), pltpu.HBM) for table in tables
    ]
    return pl.pallas_call(
        functools.partial(gathered_kernel, count_y, count_x),
        out_shape=(
            jax.ShapeDtypeStruct((2, cells_y, cells_x), F32),
            jax.ShapeDtypeStruct((height, breadth), F32),
        ),
        in_specs=[pl.BlockSpec(memory_space=pltpu.HBM)] * 14,
        out_specs=(
            pl.BlockSpec(memory_space=pltpu.VMEM),
            pl.BlockSpec(memory_space=pltpu.VMEM),
        ),
        scratch_shapes=scratch,
        compiler_params=pltpu.CompilerParams(
            collective_id=1, has_side_effects=True, vmem_limit_bytes=32 * 1024 * 1024
        ),
    )(tissue, fixed_image, moving_image, *held)


def shards(count_y, count_x, fixed_image, moving_image, tissue):
    held = [pltpu.with_memory_space_constraint(x, pltpu.HBM) for x in (tissue, fixed_image, moving_image)]
    height, breadth = fixed_image.shape
    fits = height == 2 * SPACE and breadth == 8 * SPACE and count_x % 2 == 0
    fits = fits and count_x * (breadth // SPACE) == 32 and count_y * count_x <= LARGEST
    call = gathered_call if fits else spread_call
    coef, mismatch = call(count_y, count_x, *held)
    return pl.pallas_call(
        closing,
        out_shape=(
            jax.ShapeDtypeStruct(coef.shape, F32),
            jax.ShapeDtypeStruct(mismatch.shape, F32),
        ),
        in_specs=[pl.BlockSpec(memory_space=pl.ANY)] * 2,
        out_specs=(pl.BlockSpec(memory_space=pltpu.HBM),) * 2,
        scratch_shapes=[pltpu.SemaphoreType.DMA((2,))],
        compiler_params=pltpu.CompilerParams(vmem_limit_bytes=4 * 1024 * 1024),
    )(coef, mismatch)


def solution(mesh):
    placed = (P("ty", "tx"), P("ty", "tx"), P("ty", "tx"))
    return jax.shard_map(
        functools.partial(shards, mesh.shape["ty"], mesh.shape["tx"]),
        mesh=mesh,
        in_specs=placed,
        out_specs=(P(None, "ty", "tx"), P("ty", "tx")),
        check_vma=False,
    )
```

```python
import functools

import jax
import jax.numpy as jnp
import numpy as np
from jax import lax
from jax.experimental import pallas as pl
from jax.experimental.pallas import tpu as pltpu
from jax.sharding import PartitionSpec as P

SPACE = 32
REACH_Y = 5
REACH_X = 11
RIM = 16
SEGMENT = 16
SET = 32
OWN_SLOT = 7
MESH = pl.DeviceIdType.MESH
F32 = jnp.float32
B16 = jnp.bfloat16
BLOCK = 16
PARTS = 3
LOG2E = 1.4426950408889634
LARGEST = 64

half_offsets = ((0, 2), (2, 0), (2, 2), (2, -2), (0, 4), (4, 0))
far_greets = (2, -2, 4)
travels = ((-1, 0), (1, 0), (0, -1), (0, 1), (-1, -1), (-1, 1), (1, -1), (1, 1))


def bspline(values):
    magnitude = jnp.abs(values)
    near_part = 2.0 / 3.0 - magnitude * magnitude + 0.5 * magnitude * magnitude * magnitude
    rest = 2.0 - magnitude
    far_part = rest * rest * rest / 6.0
    return jnp.where(magnitude < 1.0, near_part, jnp.where(magnitude < 2.0, far_part, 0.0))


def moved(values, by_y, by_x):
    rows, lanes = values.shape
    if by_x:
        values = pltpu.roll(values, (-by_x) % lanes, 1)
    if by_y:
        values = pltpu.roll(values, (-by_y) % rows, 0)
    return values


def minds_into(image, lane_step, out_ref):
    total = None
    for index, (offset_y, offset_x) in enumerate(half_offsets):
        gap = image - moved(image, offset_y, lane_step * offset_x)
        square = gap * gap
        rows = square + moved(square, 1, 0) + moved(square, -1, 0)
        box = rows + moved(rows, 0, lane_step) + moved(rows, 0, -lane_step)
        other = moved(box, -offset_y, -lane_step * offset_x)
        out_ref[2 * index, : image.shape[0]] = box
        out_ref[2 * index + 1, : image.shape[0]] = other
        both = box + other
        total = both if total is None else total + both
    return -1.0 / (total / 12.0 + 0.9)


def terms_into(fixed, moving, lane_step, factor, fixed_ref, moving_ref, terms_ref, wide):
    rows = fixed.shape[0]
    height = rows - 16
    fixed_scale = minds_into(fixed, lane_step, fixed_ref)[8 : 8 + height, :wide]
    moving_scale = minds_into(moving, lane_step, moving_ref)
    sums = None
    for index in range(12):
        fixed_mind = jnp.exp(fixed_ref[index, 8 : 8 + height, :wide] * fixed_scale)
        mind = jnp.exp(moving_ref[index, :rows] * moving_scale)
        differ = mind[8 : 8 + height, :wide] - fixed_mind
        slope_y = moved(mind[:, :wide], 1, 0) - moved(mind[:, :wide], -1, 0)
        slope_y = slope_y[8 : 8 + height]
        own = mind[8 : 8 + height]
        slope_x = (moved(own, 0, lane_step) - moved(own, 0, -lane_step))[:, :wide]
        parts = (
            differ * slope_y,
            differ * slope_x,
            slope_y * slope_y,
            slope_y * slope_x,
            slope_x * slope_x,
            differ * differ,
        )
        sums = parts if sums is None else tuple(a + b for a, b in zip(sums, parts))
    once = 1.0 / (2.0 * factor)
    scales = (once, once, once * once, once * once, once * once, 1.0)
    for index in range(6):
        terms_ref[index] = sums[index] * scales[index]


def spread_kernel(
    count_y,
    count_x,
    tissue_hbm,
    fixed_hbm,
    moving_hbm,
    coef_ref,
    mismatch_ref,
    mid,
    left_side,
    right_side,
    full,
    fixed_minds,
    moving_minds,
    fine_terms,
    coarse_terms,
    fine_weight,
    coarse_weight,
    fine_rows,
    coarse_rows,
    fine_cols,
    coarse_cols,
    tissue_ref,
    tiles_box,
    scalar_box,
    load_sem,
    rim_send,
    rim_recv,
    tile_send,
    tile_recv,
    scalar_send,
    scalar_recv,
):
    ty = lax.axis_index("ty")
    tx = lax.axis_index("tx")
    count = count_y * count_x
    me = ty * count_x + tx
    height, breadth = fixed_hbm.shape
    knots = count_x * (breadth // SPACE)
    cells_y, cells_x = height // SPACE, breadth // SPACE

    def peer(step):
        other = lax.rem(me + step, count)
        return (other // count_x, lax.rem(other, count_x))

    def for_peers(act):
        if count <= 64:
            for step in range(1, count):
                act(peer(step))
        else:

            def body(step, carry):
                act(peer(step))
                return carry

            lax.fori_loop(1, count, body, 0)

    tissue_load = pltpu.make_async_copy(tissue_hbm, tissue_ref, load_sem.at[2])
    tissue_load.start()
    loads = []
    for image, ref in enumerate((fixed_hbm, moving_hbm)):
        loads.append(
            pltpu.make_async_copy(ref, mid.at[image, RIM : RIM + height], load_sem.at[image])
        )
        loads[image].start()

    low, high = slice(0, RIM), slice(RIM + height, 2 * RIM + height)

    @pl.when(ty == 0)
    def _():
        for ref in (mid, left_side, right_side):
            ref[:, low] = jnp.zeros((2, RIM, ref.shape[2]), F32)

    @pl.when(ty == count_y - 1)
    def _():
        for ref in (mid, left_side, right_side):
            ref[:, high] = jnp.zeros((2, RIM, ref.shape[2]), F32)

    @pl.when(tx == 0)
    def _():
        left_side[...] = jnp.zeros(left_side.shape, F32)

    @pl.when(tx == count_x - 1)
    def _():
        right_side[...] = jnp.zeros(right_side.shape, F32)

    tiles_box[...] = jnp.zeros(tiles_box.shape, F32)

    barrier = pltpu.get_barrier_semaphore()
    near = 2 <= count_y <= 8 and 2 <= count_x <= 4
    greeted = [(y, x) for y in range(-1, 2) for x in range(-1, 2) if (y, x) != (0, 0)]
    if count_y == 8:
        greeted += [(1 - count_y, 0), (count_y - 1, 0)]

    def here(by_y, by_x):
        to_y, to_x = ty + by_y, tx + by_x
        return (to_y >= 0) & (to_y < count_y) & (to_x >= 0) & (to_x < count_x)

    def greet(device):
        pl.semaphore_signal(barrier, 1, device_id=device, device_id_type=MESH)

    if near:
        for by_y, by_x in greeted:

            @pl.when(here(by_y, by_x))
            def _():
                greet((ty + by_y, tx + by_x))

    else:
        for_peers(greet)

    lane = lax.broadcasted_iota(jnp.int32, (8, breadth), 1)
    for k in range(REACH_X):
        fine_cols[k] = bspline(lane.astype(F32) / SPACE - (k - 1.0))
        coarse_cols[k] = bspline((lane.astype(F32) + 0.5) / SPACE - (k - 1.0))
    row = lax.broadcasted_iota(jnp.int32, (height, 128), 0).astype(F32)
    coarse_row = lax.broadcasted_iota(jnp.int32, (height // 2, 128), 0).astype(F32)
    for r in range(REACH_Y):
        fine_rows[r] = bspline(row / SPACE - (r - 1.0))
        coarse_rows[r] = bspline((2.0 * coarse_row + 0.5) / SPACE - (r - 1.0))
    even = lax.rem(lane, 2) == 0
    tissue_load.wait()
    for i in range(cells_y):
        line = jnp.zeros((8, breadth), F32)
        for j in range(cells_x):
            value = tissue_ref[i, j].astype(F32)
            inside = (lane >= j * SPACE) & (lane < (j + 1) * SPACE)
            line = jnp.where(inside, value, line)
        half = jnp.where(even, line, 0.0)
        for part in range(SPACE // 8):
            start = i * SPACE + part * 8
            fine_weight[start : start + 8] = line
        for part in range(SPACE // 16):
            start = i * (SPACE // 2) + part * 8
            coarse_weight[start : start + 8] = half

    if near:
        edge_y = jnp.where((ty == 0) | (ty == count_y - 1), 1, 0)
        edge_x = jnp.where((tx == 0) | (tx == count_x - 1), 1, 0)
        greeters = (3 - edge_y) * (3 - edge_x) - 1
        if count_y == 8:
            greeters = greeters + edge_y
        pl.semaphore_wait(barrier, greeters)
    else:
        pl.semaphore_wait(barrier, count - 1)

    def rows_of(travel):
        if travel == 0:
            return slice(0, height), slice(RIM, RIM + height)
        if travel > 0:
            return slice(height - RIM, height), low
        return slice(0, RIM), high

    def landing(travel_y, travel_x):
        ref = mid if travel_x == 0 else (left_side if travel_x > 0 else right_side)
        return ref.at[:, rows_of(travel_y)[1]]

    def exists(travel_y, travel_x):
        to_y, to_x = ty + travel_y, tx + travel_x
        return (to_y >= 0) & (to_y < count_y) & (to_x >= 0) & (to_x < count_x)

    for index, (travel_y, travel_x) in enumerate(travels):

        @pl.when(exists(travel_y, travel_x))
        def _():
            source_rows = rows_of(travel_y)[0]
            if travel_x == 0:
                lanes = slice(0, breadth)
            elif travel_x > 0:
                lanes = slice(breadth - 128, breadth)
            else:
                lanes = slice(0, 128)
            for image, ref in enumerate((fixed_hbm, moving_hbm)):
                pltpu.make_async_remote_copy(
                    src_ref=ref.at[source_rows, lanes],
                    dst_ref=landing(travel_y, travel_x).at[image],
                    send_sem=rim_send.at[index],
                    recv_sem=rim_recv.at[index],
                    device_id=(ty + travel_y, tx + travel_x),
                    device_id_type=MESH,
                ).start()

    for load in loads:
        load.wait()

    for index, (travel_y, travel_x) in enumerate(travels):

        @pl.when(exists(-travel_y, -travel_x))
        def _():
            place = landing(travel_y, travel_x)
            pltpu.make_async_copy(place, place, rim_recv.at[index]).wait()

    tiles = breadth // 128
    side_lane = lax.broadcasted_iota(jnp.int32, (height + 2 * RIM, 128), 1)
    for image in range(2):
        for tile in range(tiles):
            full[image * (tiles + 1) + tile] = mid[image, :, tile * 128 : (tile + 1) * 128]
        full[image * (tiles + 1) + tiles] = jnp.where(
            side_lane < 64, right_side[image], left_side[image]
        )

    def fine_image(image):
        base = image * (tiles + 1)
        return jnp.concatenate(
            [full[base + tile, 8 : height + 24] for tile in range(tiles + 1)], axis=1
        )

    def coarse_image(image):
        base = image * (tiles + 1)
        span = height // 2 + RIM
        summed = jnp.concatenate(
            [
                full[base + tile, pl.ds(0, span, stride=2), :]
                + full[base + tile, pl.ds(1, span, stride=2), :]
                for tile in range(tiles + 1)
            ],
            axis=1,
        )
        return 0.25 * (summed + moved(summed, 0, 1))

    terms_into(
        coarse_image(0), coarse_image(1), 2, 2, fixed_minds, moving_minds, coarse_terms, breadth
    )

    small_lane = lax.broadcasted_iota(jnp.int32, (8, 128), 1)
    small_row = lax.broadcasted_iota(jnp.int32, (8, 128), 0)
    knot = lax.rem(small_lane, SEGMENT)
    knot_x = tx * cells_x - 1 + knot
    knot_y = ty * cells_y - 1 + small_row
    valid = (knot < REACH_X) & (small_row < REACH_Y) & (knot_x >= 0) & (knot_x < knots)
    valid = valid & (knot_y >= 0) & (knot_y < count_y * cells_y)
    own = (small_lane < SET) & (knot >= 1) & (knot <= cells_x)
    own = own & (small_row >= 1) & (small_row <= cells_y)

    def displace(window, rows_ref, cols_ref, number=0):
        fields = []
        for member in range(2):
            line = None
            for k in range(REACH_X):
                at = number * SET + member * SEGMENT + k
                part = window[:, at : at + 1] * cols_ref[k]
                line = part if line is None else line + part
            field = None
            for r in range(REACH_Y):
                weights = jnp.concatenate([rows_ref[r]] * tiles, axis=1)
                part = weights * line[r : r + 1, :]
                field = part if field is None else field + part
            fields.append(field)
        return fields

    def gather_up(pixels, rows_ref, cols_ref, number=0):
        out = jnp.zeros((8, 128), F32)
        for member in range(2):
            lines = []
            for r in range(REACH_Y):
                weights = jnp.concatenate([rows_ref[r]] * tiles, axis=1)
                lines.append(jnp.sum(weights * pixels[member], axis=0, keepdims=True))
            lines.append(jnp.zeros((8 - REACH_Y, breadth), F32))
            line = jnp.concatenate(lines, axis=0)
            for k in range(REACH_X):
                column = jnp.sum(line * cols_ref[k], axis=1, keepdims=True)
                at = number * SET + member * SEGMENT + k
                out = jnp.where(small_lane == at, column, out)
        return out

    def slot_of(by_y, by_x):
        return (by_y + 2) * 3 + by_x + 1

    around = [(y, x) for y in range(-2, 3) for x in range(-1, 2) if (y, x) != (0, 0)]

    def send_tile(turn, tile):
        tiles_box[turn, OWN_SLOT] = tile
        for by_y, by_x in around:

            @pl.when(exists(by_y, by_x))
            def _():
                slot = slot_of(-by_y, -by_x)
                pltpu.make_async_remote_copy(
                    src_ref=tiles_box.at[turn, OWN_SLOT],
                    dst_ref=tiles_box.at[turn, slot],
                    send_sem=tile_send.at[slot],
                    recv_sem=tile_recv.at[turn, slot],
                    device_id=(ty + by_y, tx + by_x),
                    device_id_type=MESH,
                ).start()

    def collect_tiles(turn):
        for by_y, by_x in around:

            @pl.when(exists(by_y, by_x))
            def _():
                slot = slot_of(by_y, by_x)
                place = tiles_box.at[turn, slot]
                pltpu.make_async_copy(place, place, tile_recv.at[turn, slot]).wait()

        window = None
        for by_x in range(-1, 2):
            total = None
            for by_y in range(-2, 3):
                part = tiles_box[turn, slot_of(by_y, by_x)]
                if by_y:
                    part = pltpu.roll(part, (2 * by_y) % 8, 0)
                if by_y == 2:
                    part = jnp.where(small_row >= 4, part, 0.0)
                if by_y == -2:
                    part = jnp.where(small_row < 1, part, 0.0)
                total = part if total is None else total + part
            if by_x:
                total = pltpu.roll(total, (8 * by_x) % 128, 1)
                reached = (knot >= 8) if by_x > 0 else (knot < REACH_X - 8)
                total = jnp.where(reached, total, 0.0)
            window = total if window is None else window + total
        return jnp.where(valid, window, 0.0)

    def send_scalars(turn, row):
        scalar_box[turn, me] = row

        def act(device):
            pltpu.make_async_remote_copy(
                src_ref=scalar_box.at[turn, me],
                dst_ref=scalar_box.at[turn, me],
                send_sem=scalar_send.at[turn],
                recv_sem=scalar_recv.at[turn],
                device_id=device,
                device_id_type=MESH,
            ).start()

        for_peers(act)

    def collect_scalars(turn):
        part = scalar_box.at[turn, 0 : count - 1]
        pltpu.make_async_copy(part, part, scalar_recv.at[turn]).wait()
        row = jnp.sum(scalar_box[turn], axis=0)
        lanes = lax.broadcasted_iota(jnp.int32, (1, 128), 1)
        return [
            jnp.sum(
                jnp.where((lanes >= SET * i) & (lanes < SET * (i + 1)), row, 0.0), keepdims=True
            )
            for i in range(4)
        ]

    def scalars(first, second, dense):
        third = jnp.where(own, second * second, 0.0)
        middle = jnp.where(own, first * second, 0.0)
        lead = jnp.where(own, first * first, 0.0)
        packed = lead + pltpu.roll(middle, SET, 1) + pltpu.roll(third, 2 * SET, 1)
        row = jnp.sum(packed, axis=0, keepdims=True)
        dense = dense + pltpu.roll(dense, 64, 1)
        dense = dense + pltpu.roll(dense, 32, 1)
        lanes = lax.broadcasted_iota(jnp.int32, (1, 128), 1)
        return jnp.where(lanes >= 3 * SET, dense, row)

    def pulled(terms_ref, motion):
        return (
            terms_ref[2] * motion[0] + terms_ref[3] * motion[1],
            terms_ref[3] * motion[0] + terms_ref[4] * motion[1],
        )

    def weighted(weight_ref, pair):
        return [weight_ref[...] * pair[0], weight_ref[...] * pair[1]]

    def density_row(weight_ref, motion, pull):
        dense = weight_ref[...] * (motion[0] * pull[0] + motion[1] * pull[1])
        line = jnp.sum(dense, axis=0, keepdims=True)
        total = line[:, :128]
        for tile in range(1, tiles):
            total = total + line[:, tile * 128 : (tile + 1) * 128]
        return total

    def steps_of(first, middle, third, fourth):
        step = first / middle
        norm = first - 2.0 * step * middle + step * step * third
        curvature = middle - 2.0 * step * third + step * step * fourth
        return step, norm / curvature

    send_tile(
        0,
        gather_up(
            weighted(coarse_weight, (coarse_terms[0], coarse_terms[1])), coarse_rows, coarse_cols
        ),
    )
    terms_into(fine_image(0), fine_image(1), 1, 1, fixed_minds, moving_minds, fine_terms, breadth)
    fine_start = gather_up(
        weighted(fine_weight, (fine_terms[0], fine_terms[1])), fine_rows, fine_cols, 1
    )
    gradient0 = collect_tiles(0)

    motion = displace(gradient0, coarse_rows, coarse_cols)
    part = gather_up(
        weighted(coarse_weight, pulled(coarse_terms, motion)), coarse_rows, coarse_cols
    )
    send_tile(1, part + fine_start)
    fine_motion0 = displace(gradient0, fine_rows, fine_cols)
    fine_part0 = gather_up(
        weighted(fine_weight, pulled(fine_terms, fine_motion0)), fine_rows, fine_cols
    )
    gradient1 = collect_tiles(1)

    motion = displace(gradient1, coarse_rows, coarse_cols)
    dense = density_row(coarse_weight, motion, pulled(coarse_terms, motion))
    send_scalars(0, scalars(gradient0, gradient1, dense))
    fine_motion1 = displace(gradient1, fine_rows, fine_cols)
    fine_part1 = gather_up(
        weighted(fine_weight, pulled(fine_terms, fine_motion1)), fine_rows, fine_cols, 1
    )
    send_tile(2, fine_part0 + fine_part1)
    fine_gradient = pltpu.roll(gradient1, 128 - SET, 1)
    images = collect_tiles(2)
    step0, step1 = steps_of(*collect_scalars(0))
    near, far = -(step0 + step1), step0 * step1
    control = near * gradient0 + far * gradient1
    direction = fine_gradient + near * images + far * pltpu.roll(images, 128 - SET, 1)

    motion2 = displace(direction, fine_rows, fine_cols)
    send_tile(
        3,
        gather_up(weighted(fine_weight, pulled(fine_terms, motion2)), fine_rows, fine_cols),
    )
    field_y = near * fine_motion0[0] + far * fine_motion1[0]
    field_x = near * fine_motion0[1] + far * fine_motion1[1]
    image = collect_tiles(3)

    motion3 = displace(image, fine_rows, fine_cols)
    dense = density_row(fine_weight, motion3, pulled(fine_terms, motion3))
    send_scalars(1, scalars(direction, image, dense))
    step0, step1 = steps_of(*collect_scalars(1))
    near, far = -(step0 + step1), step0 * step1
    control = control + near * direction + far * image
    field_y = field_y + near * motion2[0] + far * motion3[0]
    field_x = field_x + near * motion2[1] + far * motion3[1]
    pull_y, pull_x = pulled(fine_terms, (field_y, field_x))
    mismatch_ref[...] = (
        fine_terms[5]
        + 2.0 * (fine_terms[0] * field_y + fine_terms[1] * field_x)
        + field_y * pull_y
        + field_x * pull_x
    )
    for member in range(2):
        start = member * SEGMENT + 1
        coef_ref[member] = control[1 : 1 + cells_y, start : start + cells_x]

    for index, (travel_y, travel_x) in enumerate(travels):

        @pl.when(exists(travel_y, travel_x))
        def _():
            place = landing(travel_y, travel_x)
            pltpu.make_async_copy(place, place, rim_send.at[index]).wait()

    for by_y, by_x in around:

        @pl.when(exists(by_y, by_x))
        def _():
            slot = slot_of(-by_y, -by_x)
            place = tiles_box.at[:, slot]
            pltpu.make_async_copy(place, place, tile_send.at[slot]).wait()

    for turn in range(2):
        part = scalar_box.at[turn, 0 : count - 1]
        pltpu.make_async_copy(part, part, scalar_send.at[turn]).wait()


def window_pairs(span):
    return [(k, k + d) for d in range(4) for k in range(span - d)]


def split(values):
    high = values.astype(B16)
    return high, (values - high.astype(F32)).astype(B16)


def spline_array(values):
    magnitude = np.abs(values)
    rest = 2.0 - magnitude
    near_part = 2.0 / 3.0 - magnitude**2 + 0.5 * magnitude**3
    far_part = rest**3 / 6.0
    return np.where(magnitude < 1.0, near_part, np.where(magnitude < 2.0, far_part, 0.0))


def split_array(values):
    values = values.astype(np.float32)
    high = values.astype(B16)
    return high, (values - high.astype(np.float32)).astype(B16)


def strided_columns(breadth, factor):
    lane, part = np.arange(128)[None, :], np.arange(PARTS)[:, None]
    if factor == 1:
        column = PARTS * lane + part - 8
        return column, (column >= 0) & (column < breadth)
    column = PARTS * (lane - 64) + part - 6
    return column, (lane >= 64) & (column >= 0) & (column < breadth // 2)


def natural_lane(column, breadth):
    return column if column >= 0 else breadth + 128 + column


def stride_tables(breadth):
    size = breadth + 128
    fine = np.zeros((size, PARTS * 128))
    for place in range(breadth + 16):
        fine[natural_lane(place - 8, breadth), place % PARTS * 128 + place // PARTS] = 1.0
    coarse = np.zeros((2, size, PARTS * 128))
    for image in range(2):
        for place in range(breadth // 2 + 12):
            at = place % PARTS * 128 + image * 64 + place // PARTS
            for side in range(2):
                coarse[image, natural_lane(2 * (place - 6) + side, breadth), at] = 0.25
    back = fine[:breadth].T
    return tuple(table.astype(B16) for table in (fine, coarse.reshape(-1, PARTS * 128), back))


def level_tables(height, breadth, factor):
    row_at = factor * np.arange(height // factor) + (factor - 1) / 2.0
    column, taken = strided_columns(breadth, factor)
    col_at = (factor * column + (factor - 1) / 2.0).reshape(-1)
    rows = spline_array(row_at[None, :] / SPACE - (np.arange(REACH_Y)[:, None] - 1.0))
    cols = spline_array(col_at[:, None] / SPACE - (np.arange(REACH_X)[None, :] - 1.0))
    cols = cols * taken.reshape(-1, 1)
    row_pairs = np.zeros((BLOCK, row_at.size))
    for at, (r, other) in enumerate(window_pairs(REACH_Y)):
        row_pairs[at] = rows[r] * rows[other]
    lines = np.zeros((2, BLOCK, row_at.size))
    for member in range(2):
        lines[member, member * REACH_Y : (member + 1) * REACH_Y] = rows
    pairs = window_pairs(REACH_X)
    col_table = np.zeros((4, col_at.size, 128))
    for comp in range(3):
        for at, (k, other) in enumerate(pairs):
            col_table[comp, :, comp * len(pairs) + at] = cols[:, k] * cols[:, other]
    col_table[3, :, 3 * len(pairs) : 3 * len(pairs) + REACH_X] = cols

    def left(table):
        high, low = split_array(table)
        return np.concatenate([high, high, low], axis=1)

    high, low = split_array(col_table.reshape(4 * col_at.size, 128))
    return (
        left(row_pairs),
        np.concatenate([left(lines[0]), left(lines[1])], axis=1),
        np.concatenate([high, low], axis=1),
    )


def assembly_tables(count_y, count_x, cells_y, cells_x):
    knots_y, knots_x = count_y * cells_y, count_x * cells_x
    pairs = window_pairs(REACH_X)
    width = 8 * knots_x
    cols = np.zeros((count_x * 128, 3 * width + 128), np.float32)
    for tx in range(count_x):
        start = (tx % 2 * (count_x // 2) + tx // 2) * 128
        for comp in range(3):
            for at, (k, other) in enumerate(pairs):
                first, second = tx * cells_x - 1 + k, tx * cells_x - 1 + other
                if first < 0 or second >= knots_x:
                    continue
                source, gap = start + comp * len(pairs) + at, other - k
                cols[source, comp * width + (3 + gap) * knots_x + first] = 1.0
                cols[source, comp * width + (3 - gap) * knots_x + second] = 1.0
        for k in range(REACH_X):
            knot = tx * cells_x - 1 + k
            if 0 <= knot < knots_x:
                for group in range(128 // knots_x):
                    cols[start + 3 * len(pairs) + k, 3 * width + group * knots_x + knot] = 1.0
    rows = np.zeros((9 * knots_y, count_y * BLOCK), np.float32)
    for ty in range(count_y):
        for at, (r, other) in enumerate(window_pairs(REACH_Y)):
            first, second = ty * cells_y - 1 + r, ty * cells_y - 1 + other
            if first < 0 or second >= knots_y:
                continue
            rows[(3 + other - r) * knots_y + first, ty * BLOCK + at] = 1.0
            rows[(3 - other + r) * knots_y + second, ty * BLOCK + at] = 1.0
        for member in range(2):
            for r in range(REACH_Y):
                knot = ty * cells_y - 1 + r
                if 0 <= knot < knots_y:
                    rows[(7 + member) * knots_y + knot, ty * BLOCK + member * REACH_Y + r] = 1.0
    return cols.astype(B16), np.concatenate([rows, rows], axis=1).astype(B16)


def dot(left, right):
    return jnp.dot(left, right, preferred_element_type=F32)


def strided(parts, step):
    out = []
    for at in range(PARTS):
        carry, source = divmod(at + step, PARTS)
        part = parts[source]
        out.append(pltpu.roll(part, (-carry) % 128, 1) if carry else part)
    return out


def lowered(parts, step):
    return [pltpu.roll(part, (-step) % part.shape[0], 0) for part in parts] if step else parts


def split_three(values):
    high = values.astype(B16)
    rest = values - high.astype(F32)
    middle = rest.astype(B16)
    return [high, middle, (rest - middle.astype(F32)).astype(B16)]


def boxes_into(parts, boxes_ref):
    rows = parts[0].shape[0]
    turned = {step: strided(parts, step) for step in (2, -2, 4)}
    turned[0] = parts
    total = None
    for index, (offset_y, offset_x) in enumerate(half_offsets):
        other = lowered(turned[offset_x], offset_y)
        square = [(p - q) * (p - q) for p, q in zip(parts, other)]
        lines = [
            p + q + r for p, q, r in zip(square, lowered(square, 1), lowered(square, -1))
        ]
        box = [p + q + r for p, q, r in zip(lines, strided(lines, 1), strided(lines, -1))]
        back = lowered(strided(box, -offset_x) if offset_x else box, -offset_y)
        for at in range(PARTS):
            boxes_ref[2 * index, at, :rows] = box[at]
            boxes_ref[2 * index + 1, at, :rows] = back[at]
        both = [p + q for p, q in zip(box, back)]
        total = both if total is None else [p + q for p, q in zip(total, both)]
    return [-LOG2E / (part / 12.0 + 0.9) for part in total]


def minds_tiled(scale, boxes_ref, minds_ref):
    rows = scale[0].shape[0]
    for index in range(12):
        for at in range(PARTS):
            minds_ref[index, at, :rows] = jnp.exp2(boxes_ref[index, at, :rows] * scale[at])


def sums_into(minds_ref, fixed_of, factor, terms_ref):
    height = terms_ref.shape[1]
    once = 1.0 / (2.0 * factor)
    scales = (once, once, once * once, once * once, once * once, 1.0)
    for start in range(0, height, 8):
        base = 8 + start
        sums = None
        for index in range(12):
            own = [minds_ref[index, at, base : base + 8] for at in range(PARTS)]
            fixed = fixed_of(index, base, own)
            ahead, behind = strided(own, 1), strided(own, -1)
            parts = []
            for at in range(PARTS):
                differ = own[at] - fixed[at]
                slope_y = (
                    minds_ref[index, at, base + 1 : base + 9]
                    - minds_ref[index, at, base - 1 : base + 7]
                )
                slope_x = ahead[at] - behind[at]
                parts += [
                    differ * slope_y,
                    differ * slope_x,
                    slope_y * slope_y,
                    slope_y * slope_x,
                    slope_x * slope_x,
                    differ * differ,
                ]
            sums = parts if sums is None else [a + b for a, b in zip(sums, parts)]
        for at in range(PARTS):
            for term in range(6):
                terms_ref[term, start : start + 8, at * 128 : (at + 1) * 128] = (
                    sums[6 * at + term] * scales[term]
                )


def greeted_by(count_y, count_x, y, x):
    near = {(y + by_y, x + by_x) for by_y, by_x in travels}
    near = {(a, b) for a, b in near if 0 <= a < count_y and 0 <= b < count_x}
    return near | {((y + step) % count_y, x ^ 1) for step in far_greets}


def two_steps_reach(count_y, count_x):
    if count_y < 8 or count_x % 2:
        return False
    every = [(y, x) for y in range(count_y) for x in range(count_x)]
    greeted = {at: greeted_by(count_y, count_x, *at) for at in every}
    for y, x in every:
        known = greeted[y, x].union(*(greeted[at] for at in greeted[y, x]))
        if not {at for at in every if (at[1] - x) % 2 == 0 and at != (y, x)} <= known:
            return False
    return True


def gathered_kernel(
    count_y,
    count_x,
    tissue_hbm,
    fixed_hbm,
    moving_hbm,
    *rest,
):
    tables_hbm, rest = rest[:11], rest[11:]
    coef_ref, mismatch_ref = rest[:2]
    tables, rest = rest[2:13], rest[13:]
    (
        mid,
        left_side,
        right_side,
        full,
        fixed_boxes,
        boxes_ref,
        minds_ref,
        fixed_minds,
        fine_terms,
        coarse_terms,
        fine_weight,
        coarse_weight,
        tissue_ref,
        boxes,
        stencils,
        last_rows,
        last_cols,
        natural,
        load_sem,
        table_sem,
        rim_send,
        rim_recv,
        block_send,
        block_recv,
        relay_send,
        relay_recv,
        ready,
    ) = rest
    fine_tables, coarse_tables, (gather_cols, gather_rows) = tables[:3], tables[3:6], tables[6:8]
    fine_stride, coarse_stride, stride_back = tables[8:]
    ty = lax.axis_index("ty")
    tx = lax.axis_index("tx")
    count = count_y * count_x
    half = count // 2
    me = ty * count_x + tx
    parity = lax.rem(tx, 2)
    place = ty * (count_x // 2) + tx // 2
    sibling = (ty, tx + 1 - 2 * parity)
    height, breadth = fixed_hbm.shape
    cells_y, cells_x = height // SPACE, breadth // SPACE
    knots_y, knots_x = count_y * cells_y, count_x * cells_x
    width = 8 * knots_x
    used = len(window_pairs(REACH_Y))
    wide = PARTS * 128

    def exists(by_y, by_x):
        to_y, to_x = ty + by_y, tx + by_x
        return (to_y >= 0) & (to_y < count_y) & (to_x >= 0) & (to_x < count_x)

    few = two_steps_reach(count_y, count_x)

    def greet_far(semaphore):
        for step in far_greets:
            other = (lax.rem(ty + step + count_y, count_y), sibling[1])
            pl.semaphore_signal(semaphore, 1, device_id=other, device_id_type=MESH)

    barrier = pltpu.get_barrier_semaphore()
    if few:
        for by_y, by_x in travels:

            @pl.when(exists(by_y, by_x))
            def _():
                pl.semaphore_signal(
                    barrier, 1, device_id=(ty + by_y, tx + by_x), device_id_type=MESH
                )

        greet_far(barrier)
        edge_y = jnp.where((ty == 0) | (ty == count_y - 1), 1, 0)
        edge_x = jnp.where((tx == 0) | (tx == count_x - 1), 1, 0)
        greeters = (3 - edge_y) * (3 - edge_x) - 1 + len(far_greets)
    else:
        for step in range(1, count):
            other = lax.rem(me + step, count)
            other = (other // count_x, lax.rem(other, count_x))
            pl.semaphore_signal(barrier, 1, device_id=other, device_id_type=MESH)
        greeters = count - 1

    tissue_load = pltpu.make_async_copy(tissue_hbm, tissue_ref, load_sem.at[2])
    tissue_load.start()
    loads = []
    for image, ref in enumerate((fixed_hbm, moving_hbm)):
        loads.append(
            pltpu.make_async_copy(ref, mid.at[image, RIM : RIM + height], load_sem.at[image])
        )
        loads[image].start()

    low, high = slice(0, RIM), slice(RIM + height, 2 * RIM + height)

    @pl.when(ty == 0)
    def _():
        for ref in (mid, left_side, right_side):
            ref[:, low] = jnp.zeros((2, RIM, ref.shape[2]), F32)

    @pl.when(ty == count_y - 1)
    def _():
        for ref in (mid, left_side, right_side):
            ref[:, high] = jnp.zeros((2, RIM, ref.shape[2]), F32)

    @pl.when(tx == 0)
    def _():
        left_side[...] = jnp.zeros(left_side.shape, F32)

    @pl.when(tx == count_x - 1)
    def _():
        right_side[...] = jnp.zeros(right_side.shape, F32)

    def rows_of(travel):
        if travel == 0:
            return slice(0, height), slice(RIM, RIM + height)
        if travel > 0:
            return slice(height - RIM, height), low
        return slice(0, RIM), high

    def landing(travel_y, travel_x):
        ref = mid if travel_x == 0 else (left_side if travel_x > 0 else right_side)
        return ref.at[:, rows_of(travel_y)[1]]

    for load in loads:
        load.wait()
    pl.semaphore_wait(barrier, greeters)

    for index, (travel_y, travel_x) in sorted(enumerate(travels), key=lambda item: -abs(item[1][1])):

        @pl.when(exists(travel_y, travel_x))
        def _():
            source_rows = rows_of(travel_y)[0]
            if travel_x == 0:
                lanes = slice(0, breadth)
            elif travel_x > 0:
                lanes = slice(breadth - 128, breadth)
            else:
                lanes = slice(0, 128)
            source_rows = slice(source_rows.start + RIM, source_rows.stop + RIM)
            pltpu.make_async_remote_copy(
                src_ref=mid.at[:, source_rows, lanes],
                dst_ref=landing(travel_y, travel_x),
                send_sem=rim_send.at[index],
                recv_sem=rim_recv.at[index],
                device_id=(ty + travel_y, tx + travel_x),
                device_id_type=MESH,
            ).start()

    if few:
        greet_far(ready)
    table_loads = [
        pltpu.make_async_copy(source, target, table_sem.at[index])
        for index, (source, target) in enumerate(zip(tables_hbm, tables))
    ]
    early, late = (9, 3, 4, 5), (8, 0, 1, 2, 6, 7, 10)
    for index in early + late:
        table_loads[index].start()

    boxes[:, :, :, used:] = jnp.zeros((2, 2, half, BLOCK - used, 128), F32)
    lane = lax.broadcasted_iota(jnp.int32, (8, 128), 1)
    tissue_load.wait()
    for i in range(cells_y):
        for at in range(PARTS):
            fine_at = PARTS * lane + at - 8
            coarse_at = jnp.where(lane < 64, -1, 2 * (PARTS * (lane - 64) + at - 6))
            fine_line = jnp.zeros((8, 128), F32)
            coarse_line = jnp.zeros((8, 128), F32)
            for j in range(cells_x):
                value = tissue_ref[i, j].astype(F32)
                low_x, high_x = j * SPACE, (j + 1) * SPACE
                inside = (fine_at >= low_x) & (fine_at < high_x)
                fine_line = jnp.where(inside, value, fine_line)
                inside = (coarse_at >= low_x) & (coarse_at < high_x)
                coarse_line = jnp.where(inside, value, coarse_line)
            lanes = slice(at * 128, (at + 1) * 128)
            for part in range(SPACE // 8):
                start = i * SPACE + part * 8
                fine_weight[start : start + 8, lanes] = fine_line
            for part in range(SPACE // 16):
                start = i * (SPACE // 2) + part * 8
                coarse_weight[start : start + 8, lanes] = coarse_line

    knot = lax.broadcasted_iota(jnp.int32, (128, breadth), 0)
    at_x = lax.broadcasted_iota(jnp.int32, (128, breadth), 1).astype(F32) / SPACE
    last = bspline(at_x - (knot - tx * cells_x).astype(F32))
    last_high, last_low = split(jnp.where(knot < knots_x, last, 0.0))
    last_cols[:, :breadth] = last_high
    last_cols[:, breadth:] = last_low
    knot = lax.broadcasted_iota(jnp.int32, (height, 128), 1)
    at_y = lax.broadcasted_iota(jnp.int32, (height, 128), 0).astype(F32) / SPACE
    third = knot // knots_y
    last_high, last_low = split(
        bspline(at_y - (lax.rem(knot, knots_y) - ty * cells_y).astype(F32))
    )
    kept = jnp.where(third < 2, last_high.astype(F32), last_low.astype(F32))
    last_rows[...] = jnp.where(third < 3, kept, 0.0).astype(B16)

    for index, (travel_y, travel_x) in enumerate(travels):

        @pl.when(exists(-travel_y, -travel_x))
        def _():
            spot = landing(travel_y, travel_x)
            pltpu.make_async_copy(spot, spot, rim_recv.at[index]).wait()

    tiles = breadth // 128
    side_lane = lax.broadcasted_iota(jnp.int32, (height + 2 * RIM, 128), 1)
    for image in range(2):
        for tile in range(tiles):
            full[image * (tiles + 1) + tile] = mid[image, :, tile * 128 : (tile + 1) * 128]
        full[image * (tiles + 1) + tiles] = jnp.where(
            side_lane < 64, right_side[image], left_side[image]
        )

    def fine_image(image):
        base = image * (tiles + 1)
        return jnp.concatenate(
            [full[base + tile, 8 : height + 24] for tile in range(tiles + 1)], axis=1
        )

    def coarse_image(image):
        base = image * (tiles + 1)
        span = height // 2 + RIM
        return jnp.concatenate(
            [
                full[base + tile, pl.ds(0, span, stride=2), :]
                + full[base + tile, pl.ds(1, span, stride=2), :]
                for tile in range(tiles + 1)
            ],
            axis=1,
        )

    def parts_of(values):
        return [values[:, at * 128 : (at + 1) * 128] for at in range(PARTS)]

    def coarse_terms_into():
        pieces = split_three(jnp.concatenate([coarse_image(0), coarse_image(1)], axis=1))
        out = dot(jnp.concatenate(pieces, axis=0), coarse_stride[...])
        rows = pieces[0].shape[0]
        pair = out[:rows] + out[rows : 2 * rows] + out[2 * rows :]
        minds_tiled(boxes_into(parts_of(pair), boxes_ref), boxes_ref, minds_ref)

        def fixed_of(index, base, own):
            return [pltpu.roll(part, 64, 1) for part in own]

        sums_into(minds_ref, fixed_of, 2, coarse_terms)

    def fine_terms_into():
        rows = height + 16
        turned = []
        for image in range(2):
            pieces = split_three(fine_image(image))
            out = dot(jnp.concatenate(pieces, axis=0), fine_stride[...])
            turned.append(parts_of(out[:rows] + out[rows : 2 * rows] + out[2 * rows :]))
        scale = boxes_into(turned[0], fixed_boxes)
        for at in range(PARTS):
            fixed_minds[:, at * 128 : (at + 1) * 128] = scale[at][8 : 8 + height]
        minds_tiled(boxes_into(turned[1], boxes_ref), boxes_ref, minds_ref)

        def fixed_of(index, base, own):
            return [
                jnp.exp2(
                    fixed_boxes[index, at, base : base + 8]
                    * fixed_minds[base - 8 : base, at * 128 : (at + 1) * 128]
                )
                for at in range(PARTS)
            ]

        sums_into(minds_ref, fixed_of, 1, fine_terms)

    def block_of(terms_ref, weight_ref, level):
        row_pairs, row_lines, col_table = level
        weight = weight_ref[...]
        upper, lower = split(
            jnp.concatenate([weight * terms_ref[index] for index in (2, 3, 4)], axis=1)
        )
        pairs = dot(row_pairs[...], jnp.concatenate([upper, lower, upper], axis=0))
        stack = []
        for member in range(2):
            upper, lower = split(weight * terms_ref[member])
            stack += [upper, lower, upper]
        lines = dot(row_lines[...], jnp.concatenate(stack, axis=0))
        upper, lower = split(jnp.concatenate([pairs, lines], axis=1))
        out = dot(jnp.concatenate([upper, lower], axis=0), col_table[...])
        return out[:BLOCK, :128] + out[BLOCK:, :128] + out[:BLOCK, 128:]

    def send_block(level, block):
        boxes[level, parity, place, 0:used] = block[:used]
        for step_y in [*range(1, count_y), 0]:
            for step_x in reversed(range(count_x // 2)):
                if step_y + step_x == 0:
                    continue
                to_y = lax.rem(ty + step_y, count_y)
                to_x = 2 * lax.rem(tx // 2 + step_x, count_x // 2) + parity
                pltpu.make_async_remote_copy(
                    src_ref=boxes.at[level, parity, place, 0:used],
                    dst_ref=boxes.at[level, parity, place, 0:used],
                    send_sem=block_send.at[level],
                    recv_sem=block_recv.at[level],
                    device_id=(to_y, to_x),
                    device_id_type=MESH,
                ).start()

    def relay_of(level):
        return pltpu.make_async_remote_copy(
            src_ref=boxes.at[level, parity, :, 0:used],
            dst_ref=boxes.at[level, parity, :, 0:used],
            send_sem=relay_send.at[level],
            recv_sem=relay_recv.at[level],
            device_id=sibling,
            device_id_type=MESH,
        )

    def columns_of(level, side):
        across = count_x // 2
        columns = [
            jnp.concatenate(
                [boxes[level, side, to_y * across + to_x] for to_y in range(count_y)], axis=0
            )
            for to_x in range(across)
        ]
        upper, lower = split(jnp.concatenate(columns, axis=1))
        lines = pl.ds(pl.multiple_of(side * (across * 128), 128), across * 128)
        placed = dot(gather_rows[...], jnp.concatenate([upper, lower], axis=0))
        out = dot(jnp.concatenate(split(placed), axis=0), gather_cols[lines])
        return out[: placed.shape[0]] + out[placed.shape[0] :]

    def relay(level):
        part = boxes.at[level, 0, 0 : half - 1, 0:used]
        pltpu.make_async_copy(part, part, block_recv.at[level]).wait()
        relay_of(level).start()

    def assemble(level, own):
        spot = boxes.at[level, 1 - parity, :, 0:used]
        pltpu.make_async_copy(spot, spot, relay_recv.at[level]).wait()
        stencils[level] = own + columns_of(level, 1 - parity)

    group = lax.broadcasted_iota(jnp.int32, (knots_y, 128), 1) // knots_x

    def spread(values):
        halves = []
        for start in (-3, 1):
            out = None
            for index in range(4):
                gap = start + index
                rolled = pltpu.roll(values, (-gap) % 128, 1) if gap else values
                out = rolled if out is None else jnp.where(group >= index, rolled, out)
            halves.append(out)
        return halves

    def start_of(level):
        return [
            stencils[level, (7 + member) * knots_y : (8 + member) * knots_y, 3 * width :]
            for member in range(2)
        ]

    def pull(level, spreads):
        sums = [None, None]
        for gap in range(-3, 4):
            at = (gap + 3) * knots_y
            for source in range(2):
                for part in range(2):
                    shifted = spreads[source][part]
                    if gap:
                        shifted = pltpu.roll(shifted, (-gap) % knots_y, 0)
                    for member in range(2):
                        lanes = (member + source) * width + part * 128
                        term = stencils[level, at : at + knots_y, lanes : lanes + 128] * shifted
                        old = sums[member]
                        sums[member] = term if old is None else old + term
        out = []
        for total in sums:
            total = total + pltpu.roll(total, 64, 1)
            out.append(total + pltpu.roll(total, 32, 1))
        return out

    def inner(first, second):
        return jnp.sum(first[0] * second[0] + first[1] * second[1], keepdims=True)

    def descend(level, control, gradient):
        image = pull(level, [spread(values) for values in gradient])
        step = inner(gradient, gradient) / inner(gradient, image)
        control = [c - step * g for c, g in zip(control, gradient)]
        return control, [g - step * i for g, i in zip(gradient, image)]

    for index in early:
        table_loads[index].wait()
    coarse_terms_into()
    coarse_block = block_of(coarse_terms, coarse_weight, coarse_tables)
    if few:
        pl.semaphore_wait(ready, len(far_greets))
    send_block(0, coarse_block)
    for index in late:
        table_loads[index].wait()
    fine_terms_into()
    send_block(1, block_of(fine_terms, fine_weight, fine_tables))

    for term in range(6):
        pieces = split_three(fine_terms[term])
        out = dot(jnp.concatenate(pieces, axis=0), stride_back[...])
        natural[term] = out[:height] + out[height : 2 * height] + out[2 * height :]

    relay(0)
    assemble(0, columns_of(0, parity))
    control = [jnp.zeros((knots_y, 128), F32)] * 2
    control, gradient = descend(0, control, start_of(0))
    relay(1)
    fine_own = columns_of(1, parity)
    control, _ = descend(0, control, gradient)
    spreads = [spread(values) for values in control]
    assemble(1, fine_own)
    gradient = [b + i for b, i in zip(start_of(1), pull(1, spreads))]
    control, gradient = descend(1, control, gradient)
    control, _ = descend(1, control, gradient)

    upper, lower = split(jnp.concatenate(control, axis=0))
    rows = 2 * knots_y
    out = dot(jnp.concatenate([upper, lower], axis=0), last_cols[...])
    lines = out[:rows, :breadth] + out[rows:, :breadth] + out[:rows, breadth:]
    upper, lower = split(jnp.concatenate([lines[:knots_y], lines[knots_y:]], axis=1))
    blank = jnp.zeros((128 - 3 * knots_y, 2 * breadth), B16)
    field = dot(last_rows[...], jnp.concatenate([upper, lower, upper, blank], axis=0))
    field_y, field_x = field[:, :breadth], field[:, breadth:]
    pull_y = natural[2] * field_y + natural[3] * field_x
    pull_x = natural[3] * field_y + natural[4] * field_x
    mismatch_ref[...] = (
        natural[5]
        + 2.0 * (natural[0] * field_y + natural[1] * field_x)
        + field_y * pull_y
        + field_x * pull_x
    )
    for member in range(2):
        own = pltpu.roll(control[member], lax.rem(128 - cells_x * tx, 128), 1)
        own = pltpu.roll(own, lax.rem(knots_y - cells_y * ty, knots_y), 0)
        coef_ref[member] = own[:cells_y, :cells_x]

    for index, (travel_y, travel_x) in enumerate(travels):

        @pl.when(exists(travel_y, travel_x))
        def _():
            spot = landing(travel_y, travel_x)
            pltpu.make_async_copy(spot, spot, rim_send.at[index]).wait()

    for level in range(2):
        part = boxes.at[level, 0, 0 : half - 1, 0:used]
        pltpu.make_async_copy(part, part, block_send.at[level]).wait()
        relay_of(level).wait_send()


def spread_call(count_y, count_x, tissue, fixed_image, moving_image):
    height, breadth = fixed_image.shape
    cells_y, cells_x = height // SPACE, breadth // SPACE
    count = count_y * count_x
    tall, full_lanes = height + 2 * RIM, breadth + 128
    vmem = pltpu.VMEM
    scratch = [
        vmem((2, tall, breadth), F32),
        vmem((2, tall, 128), F32),
        vmem((2, tall, 128), F32),
        vmem((2 * (breadth // 128 + 1), tall, 128), F32),
        vmem((12, height + 16, full_lanes), F32),
        vmem((12, height + 16, full_lanes), F32),
        vmem((6, height, breadth), F32),
        vmem((6, height // 2, breadth), F32),
        vmem((height, breadth), F32),
        vmem((height // 2, breadth), F32),
        vmem((REACH_Y, height, 128), F32),
        vmem((REACH_Y, height // 2, 128), F32),
        vmem((REACH_X, 8, breadth), F32),
        vmem((REACH_X, 8, breadth), F32),
        pltpu.SMEM((cells_y, cells_x), jnp.int32),
        vmem((4, 15, 8, 128), F32),
        vmem((2, count, 1, 128), F32),
        pltpu.SemaphoreType.DMA((3,)),
        pltpu.SemaphoreType.DMA((8,)),
        pltpu.SemaphoreType.DMA((8,)),
        pltpu.SemaphoreType.DMA((15,)),
        pltpu.SemaphoreType.DMA((4, 15)),
        pltpu.SemaphoreType.DMA((2,)),
        pltpu.SemaphoreType.DMA((2,)),
    ]
    return pl.pallas_call(
        functools.partial(spread_kernel, count_y, count_x),
        out_shape=(
            jax.ShapeDtypeStruct((2, cells_y, cells_x), F32),
            jax.ShapeDtypeStruct((height, breadth), F32),
        ),
        in_specs=[
            pl.BlockSpec(memory_space=pltpu.HBM),
            pl.BlockSpec(memory_space=pltpu.HBM),
            pl.BlockSpec(memory_space=pltpu.HBM),
        ],
        out_specs=(
            pl.BlockSpec(memory_space=pltpu.VMEM),
            pl.BlockSpec(memory_space=pltpu.VMEM),
        ),
        scratch_shapes=scratch,
        compiler_params=pltpu.CompilerParams(
            collective_id=0, has_side_effects=True, vmem_limit_bytes=16 * 1024 * 1024
        ),
    )(tissue, fixed_image, moving_image)


def closing(coef_in, mismatch_in, coef_out, mismatch_out, sem):
    loads = [
        pltpu.make_async_copy(mismatch_in, mismatch_out, sem.at[0]),
        pltpu.make_async_copy(coef_in, coef_out, sem.at[1]),
    ]
    for load in loads:
        load.start()
    for load in loads:
        load.wait()


def gathered_call(count_y, count_x, tissue, fixed_image, moving_image):
    height, breadth = fixed_image.shape
    cells_y, cells_x = height // SPACE, breadth // SPACE
    count = count_y * count_x
    tall, wide = height + 2 * RIM, PARTS * 128
    vmem, dma = pltpu.VMEM, pltpu.SemaphoreType.DMA
    tables = (
        level_tables(height, breadth, 1)
        + level_tables(height, breadth, 2)
        + assembly_tables(count_y, count_x, cells_y, cells_x)
        + stride_tables(breadth)
    )
    scratch = [vmem(table.shape, B16) for table in tables] + [
        vmem((2, tall, breadth), F32),
        vmem((2, tall, 128), F32),
        vmem((2, tall, 128), F32),
        vmem((2 * (breadth // 128 + 1), tall, 128), F32),
        vmem((12, PARTS, height + 16, 128), F32),
        vmem((12, PARTS, height + 16, 128), F32),
        vmem((12, PARTS, height + 16, 128), F32),
        vmem((height, wide), F32),
        vmem((6, height, wide), F32),
        vmem((6, height // 2, wide), F32),
        vmem((height, wide), F32),
        vmem((height // 2, wide), F32),
        pltpu.SMEM((cells_y, cells_x), jnp.int32),
        vmem((2, 2, count // 2, BLOCK, 128), F32),
        vmem((2, tables[7].shape[0], tables[6].shape[1]), F32),
        vmem((height, 128), B16),
        vmem((128, 2 * breadth), B16),
        vmem((6, height, breadth), F32),
        dma((3,)),
        dma((12,)),
        dma((8,)),
        dma((8,)),
        dma((2,)),
        dma((2,)),
        dma((2,)),
        dma((2,)),
        pltpu.SemaphoreType.REGULAR,
    ]
    held = [
        pltpu.with_memory_space_constraint(jnp.asarray(table), pltpu.HBM) for table in tables
    ]
    return pl.pallas_call(
        functools.partial(gathered_kernel, count_y, count_x),
        out_shape=(
            jax.ShapeDtypeStruct((2, cells_y, cells_x), F32),
            jax.ShapeDtypeStruct((height, breadth), F32),
        ),
        in_specs=[pl.BlockSpec(memory_space=pltpu.HBM)] * 14,
        out_specs=(
            pl.BlockSpec(memory_space=pltpu.VMEM),
            pl.BlockSpec(memory_space=pltpu.VMEM),
        ),
        scratch_shapes=scratch,
        compiler_params=pltpu.CompilerParams(
            collective_id=1, has_side_effects=True, vmem_limit_bytes=32 * 1024 * 1024
        ),
    )(tissue, fixed_image, moving_image, *held)


def shards(count_y, count_x, fixed_image, moving_image, tissue):
    held = [pltpu.with_memory_space_constraint(x, pltpu.HBM) for x in (tissue, fixed_image, moving_image)]
    height, breadth = fixed_image.shape
    fits = height == 2 * SPACE and breadth == 8 * SPACE and count_x % 2 == 0
    fits = fits and count_x * (breadth // SPACE) == 32 and count_y * count_x <= LARGEST
    call = gathered_call if fits else spread_call
    coef, mismatch = call(count_y, count_x, *held)
    return pl.pallas_call(
        closing,
        out_shape=(
            jax.ShapeDtypeStruct(coef.shape, F32),
            jax.ShapeDtypeStruct(mismatch.shape, F32),
        ),
        in_specs=[pl.BlockSpec(memory_space=pl.ANY)] * 2,
        out_specs=(pl.BlockSpec(memory_space=pltpu.HBM),) * 2,
        scratch_shapes=[pltpu.SemaphoreType.DMA((2,))],
        compiler_params=pltpu.CompilerParams(vmem_limit_bytes=4 * 1024 * 1024),
    )(coef, mismatch)


def solution(mesh):
    placed = (P("ty", "tx"), P("ty", "tx"), P("ty", "tx"))
    return jax.shard_map(
        functools.partial(shards, mesh.shape["ty"], mesh.shape["tx"]),
        mesh=mesh,
        in_specs=placed,
        out_specs=(P(None, "ty", "tx"), P("ty", "tx")),
        check_vma=False,
    )
```
